32 devices in a mesh: dp: 8 (over z, y), tensor: 4 (over x, core).
Axes of the slice: x: 2, y: 2, z: 4, core: 2. Of those that a mesh axis runs over, the one named last changes fastest.
Arguments:
- tokens: bfloat16 [16384, 1536], P(('dp', 'tensor')), may hold values from -6 to 6
- first_gain: bfloat16 [1536], P('dp'), may hold values from 0.099609375 to 1.8984375
- query_weight: bfloat16 [1536, 1536], P('dp', 'tensor'), may hold values from -0.15625 to 0.15625
- key_weight: bfloat16 [1536, 768], P('dp', 'tensor'), may hold values from -0.15625 to 0.15625
- value_weight: bfloat16 [1536, 768], P('dp', 'tensor'), may hold values from -0.15625 to 0.15625
- output_weight: bfloat16 [1536, 1536], P('tensor', 'dp'), may hold values from -1.25 to 1.25
- second_gain: bfloat16 [1536], P('dp'), may hold values from 0.099609375 to 1.8984375
- gate_weight: bfloat16 [1536, 4096], P('dp', 'tensor'), may hold values from -0.15625 to 0.15625
- up_weight: bfloat16 [1536, 4096], P('dp', 'tensor'), may hold values from -0.15625 to 0.15625
- down_weight: bfloat16 [4096, 1536], P('tensor', 'dp'), may hold values from -0.09375 to 0.09375
- cotangent: bfloat16 [16384, 1536], P(('dp', 'tensor')), may hold values from -6 to 6
Outputs:
- layer_out: bfloat16 [16384, 1536], P(('dp', 'tensor'))
- tokens_grad: bfloat16 [16384, 1536], P(('dp', 'tensor'))
- first_gain_grad: float32 [1536], P('dp')
- query_weight_grad: float32 [1536, 1536], P('dp', 'tensor')
- key_weight_grad: float32 [1536, 768], P('dp', 'tensor')
- value_weight_grad: float32 [1536, 768], P('dp', 'tensor')
- output_weight_grad: float32 [1536, 1536], P('tensor', 'dp')
- second_gain_grad: float32 [1536], P('dp')
- gate_weight_grad: float32 [1536, 4096], P('dp', 'tensor')
- up_weight_grad: float32 [1536, 4096], P('dp', 'tensor')
- down_weight_grad: float32 [4096, 1536], P('tensor', 'dp')
The draws below stay inside these ranges and needn't reach their ends.
All inputs are finite; a program needn't handle non-finite values.
Results may differ from the reference program's by a relative error of at most 0.023.
Values may be sent and summed in bfloat16 or wider, within the bound.
A program may use at most 192 MiB of HBM per device.

```python
import jax
import jax.numpy as jnp
from jax import lax

D = 1536
HEADS = 16
KV = 8
HEAD = 96
FF = 4096
LENGTH = 1024
TOKENS = 16384


def block_levels(own_key, extent, cuts, least, top_value):
    level = 1.0
    for position, blocks in cuts:
        steps = jax.random.uniform(jax.random.fold_in(jax.random.fold_in(own_key, 6), position), (blocks,), jnp.float32, least / len(cuts), top_value / len(cuts))
        level = level * jnp.repeat(jnp.exp(steps), extent[position] // blocks).reshape((-1,) + (1,) * (len(extent) - 1 - position))
    return level


def normal_values(rng, dims, spread, bound, pieces=(), kind=jnp.bfloat16):
    entries = jax.random.normal(rng, dims, jnp.float32) * spread
    if len(pieces) > 0:
        entries = block_levels(rng, dims, pieces, -0.22, 0.18) * entries
    return jnp.clip(entries, min=-bound, max=bound).astype(kind)


def setup_inputs(seed: int = 0) -> dict:
    streams_of = jax.random.split(jax.random.key(seed), 12)
    return {
        "tokens": normal_values(streams_of[0], (TOKENS, D), 1.0, 6.0, ((0, 32),)),
        "first_gain": jnp.clip(1.0 + 0.18 * jax.random.normal(streams_of[1], (D,), jnp.float32), 0.099609375, 1.8984375).astype(jnp.bfloat16),
        "query_weight": normal_values(streams_of[2], (D, HEADS * HEAD), D ** -0.5, 0.15625, ((0, 8), (1, 4))),
        "key_weight": normal_values(streams_of[3], (D, KV * HEAD), D ** -0.5, 0.15625, ((0, 8), (1, 4))),
        "value_weight": normal_values(streams_of[4], (D, KV * HEAD), D ** -0.5, 0.15625, ((0, 8), (1, 4))),
        "output_weight": normal_values(streams_of[5], (HEADS * HEAD, D), (HEADS * HEAD // 64) ** -0.5, 1.25, ((0, 4), (1, 8))),
        "second_gain": jnp.clip(1.0 + 0.18 * jax.random.normal(streams_of[6], (D,), jnp.float32), 0.099609375, 1.8984375).astype(jnp.bfloat16),
        "gate_weight": normal_values(streams_of[7], (D, FF), D ** -0.5, 0.15625, ((0, 8), (1, 4))),
        "up_weight": normal_values(streams_of[8], (D, FF), D ** -0.5, 0.15625, ((0, 8), (1, 4))),
        "down_weight": normal_values(streams_of[9], (FF, D), FF ** -0.5, 0.09375, ((0, 4), (1, 8))),
        "cotangent": normal_values(streams_of[10], (TOKENS, D), 1.0, 6.0, ((0, 32),)),
    }


@jax.custom_vjp
def low(v):
    return lax.optimization_barrier(v.astype(jnp.bfloat16)).astype(jnp.float32)

@jax.custom_vjp
def low_back(v):
    return v

def low_keep(v):
    return (low(v), None)

def low_pass(kept, grad):
    return (grad,)

def back_keep(v):
    return (v, None)

def back_low(kept, grad):
    return (low(grad),)
low.defvjp(low_keep, low_pass)
low_back.defvjp(back_keep, back_low)
norm_eps = 1e-05
rope_base = 100000.0
highest = lax.Precision.HIGHEST

def matmul(left_matrix, right_matrix):
    return jnp.dot(left_matrix, right_matrix, precision=highest)

def rms_norm(activations, gain_row):
    inverse_rms = lax.rsqrt(lax.optimization_barrier(jnp.mean(activations * activations, axis=-1, keepdims=True)) + norm_eps)
    return activations * inverse_rms * gain_row

def angles(row_count):
    half_head = HEAD // 2
    frequency = rope_base ** (jnp.arange(half_head, dtype=jnp.float32) * (-2.0 / HEAD))
    places = (jnp.arange(row_count, dtype=jnp.int32) % LENGTH).astype(jnp.float32)
    turned = places[:, None] * frequency[None, :]
    return (jnp.cos(turned), jnp.sin(turned))

def rotate(rows, cosine_table, sine_table):
    half_head = HEAD // 2
    first_half = rows[..., :half_head]
    second_half = rows[..., half_head:]
    cosine_rows = cosine_table[:, None, :]
    sine_rows = sine_table[:, None, :]
    return jnp.concatenate([first_half * cosine_rows - second_half * sine_rows, second_half * cosine_rows + first_half * sine_rows], axis=-1)

def attend_one(operands):
    queries, keys, values = operands
    length = queries.shape[0]
    group_size = HEADS // KV
    query_heads = queries.reshape(length, KV, group_size, HEAD)
    key_heads = keys.reshape(length, KV, HEAD)
    value_heads = values.reshape(length, KV, HEAD)
    scores = jnp.einsum('qgrd,kgd->grqk', query_heads, key_heads, precision=highest) * HEAD ** (-0.5)
    scores = low_back(scores)
    causal = jnp.arange(length, dtype=jnp.int32)[None, :] <= jnp.arange(length, dtype=jnp.int32)[:, None]
    scores = jnp.where(causal, scores, -1e+30)
    softmax_rows = jax.nn.softmax(scores, axis=-1)
    attended = jnp.einsum('grqk,kgd->qgrd', low(softmax_rows), value_heads, precision=highest)
    return attended.reshape(length, HEADS * HEAD)

def forward(activations, first_gain, query_weight, key_weight, value_weight, output_weight, second_gain, gate_weight, up_weight, down_weight):
    row_count = activations.shape[0]
    cosine_table, sine_table = angles(row_count)
    normed = low(rms_norm(activations, first_gain))
    query_rows = low_back(matmul(normed, query_weight))
    key_rows = low_back(matmul(normed, key_weight))
    value_rows = low(low_back(matmul(normed, value_weight)))
    queries = low(rotate(query_rows.reshape(row_count, HEADS, HEAD), cosine_table, sine_table))
    keys = low(rotate(key_rows.reshape(row_count, KV, HEAD), cosine_table, sine_table))
    seq_count = row_count // LENGTH
    attended = lax.map(jax.checkpoint(attend_one), (queries.reshape(seq_count, LENGTH, HEADS * HEAD), keys.reshape(seq_count, LENGTH, KV * HEAD), value_rows.reshape(seq_count, LENGTH, KV * HEAD)))
    attended = low(low_back(attended.reshape(row_count, HEADS * HEAD)))
    hidden_state = activations + low_back(matmul(attended, output_weight))
    normed_two = low(rms_norm(hidden_state, second_gain))
    gate_rows = low_back(matmul(normed_two, gate_weight))
    up_rows = low_back(matmul(normed_two, up_weight))
    inner_rows = low(jax.nn.silu(gate_rows) * up_rows)
    return hidden_state + low_back(matmul(inner_rows, down_weight))

def reference(tokens, first_gain, query_weight, key_weight, value_weight, output_weight, second_gain, gate_weight, up_weight, down_weight, cotangent):
    result, pullback = jax.vjp(forward, tokens.astype(jnp.float32), first_gain.astype(jnp.float32), query_weight.astype(jnp.float32), key_weight.astype(jnp.float32), value_weight.astype(jnp.float32), output_weight.astype(jnp.float32), second_gain.astype(jnp.float32), gate_weight.astype(jnp.float32), up_weight.astype(jnp.float32), down_weight.astype(jnp.float32))
    gradients = pullback(cotangent.astype(jnp.float32))
    return (result.astype(jnp.bfloat16), gradients[0].astype(jnp.bfloat16), gradients[1], gradients[2], gradients[3], gradients[4], gradients[5], gradients[6], gradients[7], gradients[8], gradients[9])
```

```python
import functools

import jax
import jax.numpy as jnp
import numpy as np
from jax import lax
from jax.experimental import pallas as pl
from jax.experimental.pallas import tpu as pltpu
from jax.sharding import PartitionSpec as P

HEAD = 96
LENGTH = 1024
LANES = 128
QB = 256
norm_eps = 1e-05
rope_base = 100000.0


def rope_tables():
    half = HEAD // 2
    freq = rope_base ** (np.arange(half, dtype=np.float64) * (-2.0 / HEAD))
    turned = np.arange(LENGTH, dtype=np.float64)[:, None] * freq[None, :]
    cos = np.zeros((LENGTH, LANES), np.float32); sin = np.zeros((LENGTH, LANES), np.float32)
    cos[:, :half] = np.cos(turned); cos[:, 64:64+half] = np.cos(turned)
    sin[:, :half] = -np.sin(turned); sin[:, 64:64+half] = np.sin(turned)
    return cos, sin

def spread(heads, rotary):
    e = np.zeros((heads * HEAD, heads * LANES), np.float32)
    for h in range(heads):
        for i in range(HEAD):
            lane = i if (not rotary[h] or i < 48) else i + 16
            e[h * HEAD + i, h * LANES + lane] = 1
    return e

def dot(a, b, dims=((1,), (0,))):
    return lax.dot_general(a, b, (dims, ((), ())), preferred_element_type=jnp.float32)

C2 = float(HEAD ** -0.5 * np.log2(np.e))

def fwd_kernel(normed, weight, spread_ref, cos_ref, sin_ref, qkv_ref, att_ref, lse_ref):
    w = dot(weight[...], spread_ref[...]).astype(jnp.bfloat16)
    rows = dot(normed[...], w)
    cos = cos_ref[...]; sin = sin_ref[...]
    def rot(u):
        return (u * cos + pltpu.roll(u, 64, 1) * sin).astype(jnp.bfloat16)
    qkv_ref[:, 0:128] = rot(rows[:, 0:128])
    qkv_ref[:, 128:256] = rot(rows[:, 128:256])
    qkv_ref[:, 256:384] = rot(rows[:, 256:384])
    qkv_ref[:, 384:512] = rows[:, 384:512].astype(jnp.bfloat16)
    vt = qkv_ref[:, 384:512].T
    for r in range(2):
        for i in range(LENGTH // QB):
            kk = (i + 1) * QB
            q = qkv_ref[i * QB:kk, r * 128:r * 128 + 128]
            s = dot(qkv_ref[:kk, 256:384], q, ((1,), (1,)))
            key_place = lax.broadcasted_iota(jnp.int32, (QB, QB), 0)
            query_place = lax.broadcasted_iota(jnp.int32, (QB, QB), 1)
            last = jnp.where(key_place <= query_place, s[kk - QB:], -1e30)
            s = jnp.concatenate([s[:kk - QB], last], axis=0) if i else last
            top = jnp.max(s, axis=0, keepdims=True)
            e = jnp.exp2((s - top) * C2)
            total = jnp.sum(e, axis=0, keepdims=True)
            o = dot(vt[:, :kk], e.astype(jnp.bfloat16))
            o = o / total
            att_ref[i * QB:kk, r * 128:r * 128 + 128] = o.T.astype(jnp.bfloat16)
            lse_ref[0, r, pl.ds(i * QB, QB)] = (top * C2 + jnp.log2(total))[0]

def attend_fwd(normed, weight):
    groups = weight.shape[1] // 384
    cos, sin = rope_tables()
    e = jnp.asarray(spread(4, (1, 1, 1, 0)), jnp.bfloat16)
    whole = lambda g: (0, 0)
    return pl.pallas_call(
        fwd_kernel, grid=(groups,),
        in_specs=[pl.BlockSpec((LENGTH, weight.shape[0]), whole), pl.BlockSpec((weight.shape[0], 384), lambda g: (0, g)),
                  pl.BlockSpec((384, 512), whole), pl.BlockSpec((LENGTH, LANES), whole), pl.BlockSpec((LENGTH, LANES), whole)],
        out_specs=[pl.BlockSpec((LENGTH, 512), lambda g: (0, g)), pl.BlockSpec((LENGTH, 256), lambda g: (0, g)),
                   pl.BlockSpec((1, 2, LENGTH), lambda g: (g, 0, 0))],
        out_shape=[jax.ShapeDtypeStruct((LENGTH, 512 * groups), jnp.bfloat16), jax.ShapeDtypeStruct((LENGTH, 256 * groups), jnp.bfloat16),
                   jax.ShapeDtypeStruct((groups, 2, LENGTH), jnp.float32)],
        compiler_params=pltpu.CompilerParams(vmem_limit_bytes=40 * 2**20),
        cost_estimate=pl.CostEstimate(flops=groups * 2 * 10**9 * 3, bytes_accessed=10 * 2**20, transcendentals=groups * 2**21),
        name="attend_forward",
    )(normed, weight, e, jnp.asarray(cos), jnp.asarray(sin))

def bwd_kernel(qkv_ref, att_ref, grad_ref, lse_ref, spread_ref, cos_ref, sin_ref, out_ref, dk_ref, dv_ref, dq_ref):
    kt = qkv_ref[:, 256:384].T
    cos = cos_ref[...]; sin = sin_ref[...]
    scale = HEAD ** -0.5
    def unrot(u):
        return (u * cos - pltpu.roll(u, 64, 1) * sin).astype(jnp.bfloat16)
    for r in range(2):
        prod = grad_ref[:, r * 128:r * 128 + 128].astype(jnp.float32) * att_ref[:, r * 128:r * 128 + 128].astype(jnp.float32)
        delta = jnp.sum(prod.T, axis=0, keepdims=True)
        for i in reversed(range(LENGTH // QB)):
            kk = (i + 1) * QB
            q = qkv_ref[i * QB:kk, r * 128:r * 128 + 128]
            g = grad_ref[i * QB:kk, r * 128:r * 128 + 128]
            s = dot(qkv_ref[:kk, 256:384], q, ((1,), (1,)))
            p = jnp.exp2(s * C2 - lse_ref[0, r:r + 1, i * QB:kk])
            key_place = lax.broadcasted_iota(jnp.int32, (QB, QB), 0)
            query_place = lax.broadcasted_iota(jnp.int32, (QB, QB), 1)
            last = jnp.where(key_place <= query_place, p[kk - QB:], 0.0)
            p = jnp.concatenate([p[:kk - QB], last], axis=0) if i else last
            dp = dot(qkv_ref[:kk, 384:512], g, ((1,), (1,)))
            ds = (p * (dp - delta[:, i * QB:kk])).astype(jnp.bfloat16)
            dk = dot(ds, q)
            dv = dot(p.astype(jnp.bfloat16), g)
            if r == 0 and i == LENGTH // QB - 1:
                dk_ref[...] = dk
                dv_ref[...] = dv
            else:
                dk_ref[:kk] += dk
                dv_ref[:kk] += dv
            dq = dot(kt[:, :kk], ds)
            dq_ref[i * QB:kk, r * 128:r * 128 + 128] = dq.T
    rows = jnp.concatenate([unrot(dq_ref[:, :128] * scale), unrot(dq_ref[:, 128:] * scale), unrot(dk_ref[...] * scale), dv_ref[...].astype(jnp.bfloat16)], axis=1)
    out_ref[...] = dot(rows, spread_ref[...], ((1,), (1,))).astype(jnp.bfloat16)

def attend_bwd(qkv, att, grad, lse):
    groups = qkv.shape[1] // 512
    cos, sin = rope_tables()
    e = jnp.asarray(spread(4, (1, 1, 1, 0)), jnp.bfloat16)
    whole = lambda g: (0, 0)
    return pl.pallas_call(
        bwd_kernel, grid=(groups,),
        in_specs=[pl.BlockSpec((LENGTH, 512), lambda g: (0, g)), pl.BlockSpec((LENGTH, 256), lambda g: (0, g)), pl.BlockSpec((LENGTH, 256), lambda g: (0, g)),
                  pl.BlockSpec((1, 2, LENGTH), lambda g: (g, 0, 0)),
                  pl.BlockSpec((384, 512), whole), pl.BlockSpec((LENGTH, LANES), whole), pl.BlockSpec((LENGTH, LANES), whole)],
        out_specs=pl.BlockSpec((LENGTH, 384), lambda g: (0, g)),
        out_shape=jax.ShapeDtypeStruct((LENGTH, 384 * groups), jnp.bfloat16),
        scratch_shapes=[pltpu.VMEM((LENGTH, LANES), jnp.float32), pltpu.VMEM((LENGTH, LANES), jnp.float32), pltpu.VMEM((LENGTH, 256), jnp.float32)],
        compiler_params=pltpu.CompilerParams(vmem_limit_bytes=40 * 2**20),
        cost_estimate=pl.CostEstimate(flops=groups * 4 * 10**9 * 3, bytes_accessed=10 * 2**20, transcendentals=groups * 2**21),
        name="attend_backward",
    )(qkv, att, grad, lse, e, jnp.asarray(cos), jnp.asarray(sin))


def swap_core(v):
    return lax.ppermute(v, "tensor", [(t, t ^ 1) for t in range(4)])


def swap_chip(v):
    return lax.ppermute(v, "tensor", [(t, t ^ 2) for t in range(4)])


class Ring:
    def __init__(self, size):
        self.size = size
        self.half = size // 2
        order = list(range(0, size, 2)) + list(range(size - 1, 0, -2))
        self.forward = [(order[i], order[(i + 1) % size]) for i in range(size)]
        self.backward = [(b, a) for a, b in self.forward]
        own = lax.axis_index("dp")
        self.place = jnp.where(own % 2 == 0, own // 2, size - 1 - own // 2)

    def index(self, step):
        place = (self.place + step + self.size) % self.size
        return jnp.where(place < self.half, 2 * place, 2 * (self.size - 1 - place) + 1)

    def up(self, v):
        return lax.ppermute(v, "dp", self.forward)

    def down(self, v):
        return lax.ppermute(v, "dp", self.backward)

    def gather(self, shard, passed=False):
        rows, columns = shard.shape
        parts = [(0, shard)]
        others = []
        if passed:
            others.append((0, swap_chip(shard)))
        up = down = shard
        for step in range(1, self.half):
            up, down = self.up(up), self.down(down)
            parts += [(-step, up), (step, down)]
            if passed:
                both = swap_chip(jnp.concatenate([up, down], axis=0))
                others += [(-step, both[:rows]), (step, both[rows:])]
        cut = rows // 2
        last = jnp.concatenate([self.up(up[:cut]), self.down(down[cut:])], axis=0)
        parts.append((self.half, last))
        if passed:
            others.append((self.half, swap_chip(last)))

        def lay(pieces):
            whole = jnp.zeros((self.size * rows, columns), shard.dtype)
            for step, piece in pieces:
                whole = lax.dynamic_update_slice(whole, piece, (self.index(step) * rows, 0))
            return whole

        return (lay(parts), lay(others)) if passed else lay(parts)

    def scatter(self, take):
        far = take(self.index(self.half))
        cut = far.shape[0] // 2
        up, down = self.up(far[:cut]), self.down(far[cut:])
        for step in range(self.half - 1, 0, -1):
            ahead = take(self.index(step)).astype(jnp.float32)
            behind = take(self.index(-step)).astype(jnp.float32)
            if step == self.half - 1:
                ahead = jnp.concatenate([ahead[:cut] + up.astype(jnp.float32), ahead[cut:]], axis=0)
                behind = jnp.concatenate([behind[:cut], behind[cut:] + down.astype(jnp.float32)], axis=0)
            else:
                ahead = ahead + up.astype(jnp.float32)
                behind = behind + down.astype(jnp.float32)
            up, down = self.up(ahead.astype(jnp.bfloat16)), self.down(behind.astype(jnp.bfloat16))
        own = take(self.index(0)).astype(jnp.float32)
        return own + up.astype(jnp.float32) + down.astype(jnp.float32)


def gather_gains(gains, size):
    own = lax.axis_index("dp")
    whole = jnp.zeros((size,) + gains.shape, gains.dtype)
    whole = lax.dynamic_update_slice(whole, gains[None], (own, 0, 0))
    for step in range(1, size):
        piece = lax.ppermute(gains, "dp", [(i, (i + step) % size) for i in range(size)])
        whole = lax.dynamic_update_slice(whole, piece[None], ((own - step + size) % size, 0, 0))
    return whole


def times(left, right):
    return dot(left, right)


def times_transpose(left, right):
    return dot(left, right, ((1,), (1,)))


def contract_rows(left, right):
    return dot(left, right, ((0,), (0,)))


def local(
    dp_size,
    tokens,
    first_gain,
    query_weight,
    key_weight,
    value_weight,
    output_weight,
    second_gain,
    gate_weight,
    up_weight,
    down_weight,
    cotangent,
):
    ring = Ring(dp_size)
    half_rows = tokens.shape[0]
    core = lax.axis_index("tensor") % 2
    bf16, f32 = jnp.bfloat16, jnp.float32

    def pair(own, other):
        return jnp.where(
            core == 0,
            jnp.concatenate([own, other], axis=0),
            jnp.concatenate([other, own], axis=0),
        )

    def mine(rows):
        return lax.dynamic_slice_in_dim(rows, core * half_rows, half_rows, 0)

    def theirs(rows):
        return lax.dynamic_slice_in_dim(rows, (1 - core) * half_rows, half_rows, 0)

    groups = key_weight.shape[1] // HEAD
    packs = []
    for group in range(groups):
        packs.append(query_weight[:, group * 2 * HEAD : (group + 1) * 2 * HEAD])
        packs.append(key_weight[:, group * HEAD : (group + 1) * HEAD])
        packs.append(value_weight[:, group * HEAD : (group + 1) * HEAD])
    attend_shard = jnp.concatenate(packs, axis=1)
    output_shard = output_weight.T
    feed_shard = jnp.concatenate([gate_weight, up_weight, down_weight.T], axis=1)
    hidden_units = gate_weight.shape[1]

    gains = gather_gains(jnp.stack([first_gain, second_gain]), dp_size)
    gain_one = gains[:, 0].reshape(1, -1).astype(f32)
    gain_two = gains[:, 1].reshape(1, -1).astype(f32)

    activations = tokens.astype(f32)
    inverse_one = lax.rsqrt(jnp.mean(activations * activations, axis=-1, keepdims=True) + norm_eps)
    normed_own = (activations * inverse_one * gain_one).astype(bf16)
    normed = pair(normed_own, swap_core(normed_own))

    attend_own, attend_other = ring.gather(attend_shard, passed=True)
    output_shard, attend_own_late = lax.optimization_barrier((output_shard, attend_own))
    output_both = ring.gather(jnp.concatenate([output_shard, swap_chip(output_shard)], axis=1))
    output_both_late, feed_shard = lax.optimization_barrier((output_both, feed_shard))
    feed = ring.gather(feed_shard)
    gate_up = feed[:, : 2 * hidden_units]
    down_turned = feed[:, 2 * hidden_units :]

    qkv_own, attended_own, log_own = attend_fwd(normed, attend_own)
    qkv_other, attended_other, log_other = attend_fwd(normed, attend_other)
    heads = output_both.shape[1] // HEAD
    spread_heads = jnp.asarray(spread(heads, (0,) * heads), bf16)
    output_spread = times(output_both, spread_heads).astype(bf16)
    attended = jnp.concatenate([attended_own, attended_other], axis=1)
    attention_terms = times_transpose(attended, output_spread).astype(bf16)
    hidden_state = (
        activations
        + mine(attention_terms).astype(f32)
        + swap_core(theirs(attention_terms)).astype(f32)
    )
    inverse_two = lax.rsqrt(
        jnp.mean(hidden_state * hidden_state, axis=-1, keepdims=True) + norm_eps
    )
    normed_two_own = (hidden_state * inverse_two * gain_two).astype(bf16)

    def spread_rows(own):
        across = swap_chip(own)
        return pair(own, swap_core(own)), pair(across, swap_core(across))

    def gather_rows(near, far):
        near_sum = mine(near).astype(f32) + swap_core(theirs(near)).astype(f32)
        far_sum = mine(far).astype(f32) + swap_core(theirs(far)).astype(f32)
        return near_sum + swap_chip(far_sum.astype(bf16)).astype(f32)

    cot_near, cot_far = spread_rows(cotangent)
    two_near, two_far = spread_rows(normed_two_own)

    def feed_forward(two, cot):
        both = times(two, gate_up)
        gate, up = both[:, :hidden_units], both[:, hidden_units:]
        inner_grad = times(cot, down_turned)
        sigmoid = jax.nn.sigmoid(gate)
        inner = (gate * sigmoid * up).astype(bf16)
        up_grad = (inner_grad * gate * sigmoid).astype(bf16)
        gate_grad = (inner_grad * up * sigmoid * (1.0 + gate * (1.0 - sigmoid))).astype(bf16)
        return inner, jnp.concatenate([gate_grad, up_grad], axis=1)

    inner_near, grad_near = feed_forward(two_near, cot_near)
    inner_far, grad_far = feed_forward(two_far, cot_far)
    two_terms_far = times_transpose(grad_far, gate_up).astype(bf16)
    two_terms_near = times_transpose(grad_near, gate_up).astype(bf16)
    out_far = times_transpose(inner_far, down_turned).astype(bf16)
    out_near = times_transpose(inner_near, down_turned).astype(bf16)
    normed_two_grad = gather_rows(two_terms_near, two_terms_far)
    layer_out = (hidden_state + gather_rows(out_near, out_far)).astype(bf16)

    down_grad = contract_rows(
        jnp.concatenate([cot_near, cot_far], axis=0),
        jnp.concatenate([inner_near, inner_far], axis=0),
    ).astype(bf16)
    gate_up_grad = contract_rows(
        jnp.concatenate([two_near, two_far], axis=0),
        jnp.concatenate([grad_near, grad_far], axis=0),
    ).astype(bf16)
    shard_rows = first_gain.shape[0]

    def part(whole):
        return lambda index: lax.dynamic_slice_in_dim(whole, index * shard_rows, shard_rows, 0)

    down_sum = ring.scatter(part(down_grad))
    gate_up_sum = ring.scatter(part(gate_up_grad))

    scaled_two = normed_two_grad * gain_two
    hidden_grad = (
        cotangent.astype(f32)
        + inverse_two * scaled_two
        - hidden_state
        * inverse_two**3
        * jnp.mean(scaled_two * hidden_state, axis=-1, keepdims=True)
    )
    branch_own = hidden_grad.astype(bf16)
    branch = pair(branch_own, swap_core(branch_own))
    attended_grad = times(branch, output_spread).astype(bf16)
    width = attended_own.shape[1]
    other_back = attend_bwd(qkv_other, attended_other, attended_grad[:, width:], log_other)
    own_back = attend_bwd(qkv_own, attended_own, attended_grad[:, :width], log_own)

    attended_close = times_transpose(attended, spread_heads).astype(bf16)
    output_grad = contract_rows(branch, attended_close).astype(bf16)
    columns = output_shard.shape[1]
    output_grad = output_grad[:, :columns].astype(f32) + swap_chip(output_grad[:, columns:]).astype(
        f32
    )
    output_sum = ring.scatter(part(output_grad.astype(bf16)))

    other_grad = swap_chip(contract_rows(normed, other_back).astype(bf16))
    own_grad = contract_rows(normed, own_back)
    attend_grad = (own_grad + other_grad.astype(f32)).astype(bf16)
    attend_sum = ring.scatter(part(attend_grad))

    normed_terms = (
        times_transpose(own_back, attend_own) + times_transpose(other_back, attend_other)
    ).astype(bf16)
    normed_grad = mine(normed_terms).astype(f32) + swap_core(theirs(normed_terms)).astype(f32)
    scaled_one = normed_grad * gain_one
    tokens_grad = (
        hidden_grad
        + inverse_one * scaled_one
        - activations * inverse_one**3 * jnp.mean(scaled_one * activations, axis=-1, keepdims=True)
    ).astype(bf16)

    gain_sums = jnp.stack(
        [
            jnp.sum(attend_sum * attend_shard.astype(f32), axis=1) / first_gain.astype(f32),
            jnp.sum(gate_up_sum * feed_shard[:, : 2 * hidden_units].astype(f32), axis=1)
            / second_gain.astype(f32),
        ]
    )
    gain_sums = gain_sums + swap_core(gain_sums)
    gain_sums = gain_sums + swap_chip(gain_sums)

    block = 4 * HEAD
    query_grad = jnp.concatenate(
        [attend_sum[:, g * block : g * block + 2 * HEAD] for g in range(groups)], axis=1
    )
    key_grad = jnp.concatenate(
        [attend_sum[:, g * block + 2 * HEAD : g * block + 3 * HEAD] for g in range(groups)], axis=1
    )
    value_grad = jnp.concatenate(
        [attend_sum[:, g * block + 3 * HEAD : (g + 1) * block] for g in range(groups)], axis=1
    )
    return (
        layer_out,
        tokens_grad,
        gain_sums[0],
        query_grad,
        key_grad,
        value_grad,
        output_sum.T,
        gain_sums[1],
        gate_up_sum[:, :hidden_units],
        gate_up_sum[:, hidden_units:],
        down_sum.T,
    )


def solution(mesh):
    in_specs = (
        P(("dp", "tensor"), None),
        P("dp"),
        P("dp", "tensor"),
        P("dp", "tensor"),
        P("dp", "tensor"),
        P("tensor", "dp"),
        P("dp"),
        P("dp", "tensor"),
        P("dp", "tensor"),
        P("tensor", "dp"),
        P(("dp", "tensor"), None),
    )
    out_specs = (
        P(("dp", "tensor"), None),
        P(("dp", "tensor"), None),
        P("dp"),
        P("dp", "tensor"),
        P("dp", "tensor"),
        P("dp", "tensor"),
        P("tensor", "dp"),
        P("dp"),
        P("dp", "tensor"),
        P("dp", "tensor"),
        P("tensor", "dp"),
    )
    body = functools.partial(local, mesh.shape["dp"])
    return jax.shard_map(body, mesh=mesh, in_specs=in_specs, out_specs=out_specs, check_vma=False)
```

```python
import functools

import jax
import jax.numpy as jnp
import numpy as np
from jax import lax
from jax.experimental import pallas as pl
from jax.experimental.pallas import tpu as pltpu
from jax.sharding import PartitionSpec as P

HEAD = 96
LENGTH = 1024
LANES = 128
QB = 256
norm_eps = 1e-05
rope_base = 100000.0


def rope_tables():
    half = HEAD // 2
    freq = rope_base ** (np.arange(half, dtype=np.float64) * (-2.0 / HEAD))
    turned = np.arange(LENGTH, dtype=np.float64)[:, None] * freq[None, :]
    cos = np.zeros((LENGTH, LANES), np.float32); sin = np.zeros((LENGTH, LANES), np.float32)
    cos[:, :half] = np.cos(turned); cos[:, 64:64+half] = np.cos(turned)
    sin[:, :half] = -np.sin(turned); sin[:, 64:64+half] = np.sin(turned)
    return cos, sin

def spread(heads, rotary):
    e = np.zeros((heads * HEAD, heads * LANES), np.float32)
    for h in range(heads):
        for i in range(HEAD):
            lane = i if (not rotary[h] or i < 48) else i + 16
            e[h * HEAD + i, h * LANES + lane] = 1
    return e

def dot(a, b, dims=((1,), (0,))):
    return lax.dot_general(a, b, (dims, ((), ())), preferred_element_type=jnp.float32)

C2 = float(HEAD ** -0.5 * np.log2(np.e))

def fwd_kernel(normed, weight, spread_ref, cos_ref, sin_ref, qkv_ref, att_ref, lse_ref):
    w = dot(weight[...], spread_ref[...]).astype(jnp.bfloat16)
    rows = dot(normed[...], w)
    cos = cos_ref[...]; sin = sin_ref[...]
    def rot(u):
        return (u * cos + pltpu.roll(u, 64, 1) * sin).astype(jnp.bfloat16)
    qkv_ref[:, 0:128] = rot(rows[:, 0:128])
    qkv_ref[:, 128:256] = rot(rows[:, 128:256])
    qkv_ref[:, 256:384] = rot(rows[:, 256:384])
    qkv_ref[:, 384:512] = rows[:, 384:512].astype(jnp.bfloat16)
    vt = qkv_ref[:, 384:512].T
    for r in range(2):
        for i in range(LENGTH // QB):
            kk = (i + 1) * QB
            q = qkv_ref[i * QB:kk, r * 128:r * 128 + 128]
            s = dot(qkv_ref[:kk, 256:384], q, ((1,), (1,)))
            key_place = lax.broadcasted_iota(jnp.int32, (QB, QB), 0)
            query_place = lax.broadcasted_iota(jnp.int32, (QB, QB), 1)
            last = jnp.where(key_place <= query_place, s[kk - QB:], -1e30)
            s = jnp.concatenate([s[:kk - QB], last], axis=0) if i else last
            top = jnp.max(s, axis=0, keepdims=True)
            e = jnp.exp2((s - top) * C2)
            total = jnp.sum(e, axis=0, keepdims=True)
            o = dot(vt[:, :kk], e.astype(jnp.bfloat16))
            o = o / total
            att_ref[i * QB:kk, r * 128:r * 128 + 128] = o.T.astype(jnp.bfloat16)
            lse_ref[0, r, pl.ds(i * QB, QB)] = (top * C2 + jnp.log2(total))[0]

def attend_fwd(normed, weight):
    groups = weight.shape[1] // 384
    cos, sin = rope_tables()
    e = jnp.asarray(spread(4, (1, 1, 1, 0)), jnp.bfloat16)
    whole = lambda g: (0, 0)
    return pl.pallas_call(
        fwd_kernel, grid=(groups,),
        in_specs=[pl.BlockSpec((LENGTH, weight.shape[0]), whole), pl.BlockSpec((weight.shape[0], 384), lambda g: (0, g)),
                  pl.BlockSpec((384, 512), whole), pl.BlockSpec((LENGTH, LANES), whole), pl.BlockSpec((LENGTH, LANES), whole)],
        out_specs=[pl.BlockSpec((LENGTH, 512), lambda g: (0, g)), pl.BlockSpec((LENGTH, 256), lambda g: (0, g)),
                   pl.BlockSpec((1, 2, LENGTH), lambda g: (g, 0, 0))],
        out_shape=[jax.ShapeDtypeStruct((LENGTH, 512 * groups), jnp.bfloat16), jax.ShapeDtypeStruct((LENGTH, 256 * groups), jnp.bfloat16),
                   jax.ShapeDtypeStruct((groups, 2, LENGTH), jnp.float32)],
        compiler_params=pltpu.CompilerParams(vmem_limit_bytes=40 * 2**20),
        cost_estimate=pl.CostEstimate(flops=groups * 2 * 10**9 * 3, bytes_accessed=10 * 2**20, transcendentals=groups * 2**21),
        name="attend_forward",
    )(normed, weight, e, jnp.asarray(cos), jnp.asarray(sin))

def bwd_kernel(qkv_ref, att_ref, grad_ref, lse_ref, spread_ref, cos_ref, sin_ref, out_ref, dk_ref, dv_ref, dq_ref):
    kt = qkv_ref[:, 256:384].T
    cos = cos_ref[...]; sin = sin_ref[...]
    scale = HEAD ** -0.5
    def unrot(u):
        return (u * cos - pltpu.roll(u, 64, 1) * sin).astype(jnp.bfloat16)
    for r in range(2):
        prod = grad_ref[:, r * 128:r * 128 + 128].astype(jnp.float32) * att_ref[:, r * 128:r * 128 + 128].astype(jnp.float32)
        delta = jnp.sum(prod.T, axis=0, keepdims=True)
        for i in reversed(range(LENGTH // QB)):
            kk = (i + 1) * QB
            q = qkv_ref[i * QB:kk, r * 128:r * 128 + 128]
            g = grad_ref[i * QB:kk, r * 128:r * 128 + 128]
            s = dot(qkv_ref[:kk, 256:384], q, ((1,), (1,)))
            p = jnp.exp2(s * C2 - lse_ref[0, r:r + 1, i * QB:kk])
            key_place = lax.broadcasted_iota(jnp.int32, (QB, QB), 0)
            query_place = lax.broadcasted_iota(jnp.int32, (QB, QB), 1)
            last = jnp.where(key_place <= query_place, p[kk - QB:], 0.0)
            p = jnp.concatenate([p[:kk - QB], last], axis=0) if i else last
            dp = dot(qkv_ref[:kk, 384:512], g, ((1,), (1,)))
            ds = (p * (dp - delta[:, i * QB:kk])).astype(jnp.bfloat16)
            dk = dot(ds, q)
            dv = dot(p.astype(jnp.bfloat16), g)
            if r == 0 and i == LENGTH // QB - 1:
                dk_ref[...] = dk
                dv_ref[...] = dv
            else:
                dk_ref[:kk] += dk
                dv_ref[:kk] += dv
            dq = dot(kt[:, :kk], ds)
            dq_ref[i * QB:kk, r * 128:r * 128 + 128] = dq.T
    rows = jnp.concatenate([unrot(dq_ref[:, :128] * scale), unrot(dq_ref[:, 128:] * scale), unrot(dk_ref[...] * scale), dv_ref[...].astype(jnp.bfloat16)], axis=1)
    out_ref[...] = dot(rows, spread_ref[...], ((1,), (1,))).astype(jnp.bfloat16)

def attend_bwd(qkv, att, grad, lse):
    groups = qkv.shape[1] // 512
    cos, sin = rope_tables()
    e = jnp.asarray(spread(4, (1, 1, 1, 0)), jnp.bfloat16)
    whole = lambda g: (0, 0)
    return pl.pallas_call(
        bwd_kernel, grid=(groups,),
        in_specs=[pl.BlockSpec((LENGTH, 512), lambda g: (0, g)), pl.BlockSpec((LENGTH, 256), lambda g: (0, g)), pl.BlockSpec((LENGTH, 256), lambda g: (0, g)),
                  pl.BlockSpec((1, 2, LENGTH), lambda g: (g, 0, 0)),
                  pl.BlockSpec((384, 512), whole), pl.BlockSpec((LENGTH, LANES), whole), pl.BlockSpec((LENGTH, LANES), whole)],
        out_specs=pl.BlockSpec((LENGTH, 384), lambda g: (0, g)),
        out_shape=jax.ShapeDtypeStruct((LENGTH, 384 * groups), jnp.bfloat16),
        scratch_shapes=[pltpu.VMEM((LENGTH, LANES), jnp.float32), pltpu.VMEM((LENGTH, LANES), jnp.float32), pltpu.VMEM((LENGTH, 256), jnp.float32)],
        compiler_params=pltpu.CompilerParams(vmem_limit_bytes=40 * 2**20),
        cost_estimate=pl.CostEstimate(flops=groups * 4 * 10**9 * 3, bytes_accessed=10 * 2**20, transcendentals=groups * 2**21),
        name="attend_backward",
    )(qkv, att, grad, lse, e, jnp.asarray(cos), jnp.asarray(sin))


MESH = pl.DeviceIdType.MESH


class Places:
    def __init__(self, size):
        self.size = size
        self.half = size // 2
        self.own = lax.axis_index("dp")
        self.tensor = lax.axis_index("tensor")
        odd = self.own % 2
        self.place = (1 - odd) * (self.own // 2) + odd * (size - 1 - self.own // 2)

    def index(self, step):
        place = (self.place + step + self.size) % self.size
        late = place // self.half
        return (1 - late) * 2 * place + late * (2 * (self.size - 1 - place) + 1)

    def on_ring(self, step):
        return (self.index(step), self.tensor)

    def peer(self, step):
        return ((self.own + step + self.size) % self.size, self.tensor)

    def chip(self):
        return (self.own, (self.tensor + 2) % 4)

    def core(self):
        return (self.own, self.tensor + 1 - 2 * (self.tensor % 2))


def remote(source, target, send, receive, device):
    return pltpu.make_async_remote_copy(
        src_ref=source,
        dst_ref=target,
        send_sem=send,
        recv_sem=receive,
        device_id=device,
        device_id_type=MESH,
    )


def greet(devices):
    barrier = pltpu.get_barrier_semaphore()
    for device in devices:
        pl.semaphore_signal(barrier, inc=1, device_id=device, device_id_type=MESH)
    pl.semaphore_wait(barrier, len(devices))


class RingGather:
    def __init__(self, places, slots, send, receive):
        self.places, self.slots, self.send, self.receive = places, slots, send, receive
        self.cut = slots.shape[1] // 32 * 16
        self.sent = []

    def start(self, hop, source=None):
        places, half = self.places, self.places.half
        for way, (step, device) in enumerate(
            ((1 - hop, places.on_ring(1)), (hop - 1, places.on_ring(-1)))
        ):
            slot = places.index(step)
            rows = slice(None)
            if hop == half:
                rows = pl.ds(0, self.cut) if way == 0 else pl.ds(self.cut, self.slots.shape[1] - self.cut)
            view = self.slots.at[slot, rows]
            copy = remote(
                view if source is None else source.at[rows],
                view,
                self.send.at[way, hop - 1],
                self.receive.at[way, hop - 1],
                device,
            )
            copy.start()
            self.sent.append(copy)

    def wait(self, hop):
        self.sent[2 * hop - 2].wait_recv()
        self.sent[2 * hop - 1].wait_recv()

    def finish(self):
        for copy in self.sent:
            copy.wait_send()


def head_kernel(
    size, tokens, gains, attend_shard, output_shard, normed, attend_own, attend_other, output_both, gain_rows,
    gain_slots, normed_half, gain_send, gain_receive, ring_send, ring_receive, pass_send, pass_receive,
    out_send, out_receive, across, local_sem,
):
    places = Places(size)
    half, own = places.half, places.own
    half_rows = tokens.shape[0]
    columns = output_shard.shape[1]
    greet([places.peer(step) for step in range(1, size)] + [places.chip(), places.core()])

    ring = RingGather(places, attend_own, ring_send, ring_receive)
    ring.start(1, attend_shard)
    passed = []

    def hand_on(step, number, source=None):
        slot = places.index(step)
        copy = remote(
            attend_own.at[slot] if source is None else source, attend_other.at[slot],
            pass_send.at[number], pass_receive.at[number], places.chip(),
        )
        copy.start()
        passed.append(copy)

    hand_on(0, 0, attend_shard)
    output_pass = remote(
        output_shard, output_both.at[own, :, pl.ds(columns, columns)], across.at[0], across.at[1], places.chip()
    )
    output_pass.start()
    gain_copies = []
    for step in range(1, size):
        copy = remote(gains, gain_slots.at[own], gain_send.at[step - 1], gain_receive.at[step - 1], places.peer(step))
        copy.start()
        gain_copies.append(copy)
    keep = pltpu.make_async_copy(attend_shard, attend_own.at[own], local_sem.at[0])
    keep.start()
    keep_output = pltpu.make_async_copy(output_shard, output_both.at[own, :, pl.ds(0, columns)], local_sem.at[1])
    keep_output.start()
    gain_slots[own] = gains[...]
    for copy in gain_copies:
        copy.wait_recv()
    width = tokens.shape[1] // size
    for index in range(size):
        gain_rows[:, index * width : (index + 1) * width] = gain_slots[index][:, :width]
    gain = gain_rows[0:1, :]
    tile = 64

    def norm_tile(number, carry):
        rows = pl.ds(pl.multiple_of(number * tile, tile), tile)
        values = tokens[rows, :].astype(jnp.float32)
        inverse = lax.rsqrt(jnp.mean(values * values, axis=1, keepdims=True) + norm_eps)
        normed_half[rows, :] = (values * inverse * gain).astype(jnp.bfloat16)
        return carry

    lax.fori_loop(0, half_rows // tile, norm_tile, 0)
    core = places.tensor % 2
    mine = pl.ds(pl.multiple_of(core * half_rows, half_rows), half_rows)
    swap = remote(normed_half, normed.at[mine], across.at[2], across.at[3], places.core())
    swap.start()
    keep_normed = pltpu.make_async_copy(normed_half, normed.at[mine], local_sem.at[2])
    keep_normed.start()

    outputs = RingGather(places, output_both, out_send, out_receive)
    for hop in range(1, half + 1):
        ring.wait(hop)
        if hop < half:
            ring.start(hop + 1)
            hand_on(-hop, 2 * hop - 1)
            hand_on(hop, 2 * hop)
        else:
            hand_on(half, size - 1)
        if hop == 1:
            output_pass.wait()
            keep_output.wait()
            outputs.start(1)
        else:
            outputs.wait(hop - 1)
            outputs.start(hop)
    outputs.wait(half)
    for copy in passed:
        copy.wait()
    for copy in gain_copies:
        copy.wait_send()
    ring.finish()
    outputs.finish()
    swap.wait()
    keep.wait()
    keep_normed.wait()


def head(size, tokens, gains, attend_shard, output_shard):
    half_rows, features = tokens.shape
    rows, width = attend_shard.shape
    columns = output_shard.shape[1]
    vmem = pl.BlockSpec(memory_space=pltpu.VMEM)
    anywhere = pl.BlockSpec(memory_space=pl.ANY)
    dma = pltpu.SemaphoreType.DMA
    half = size // 2
    bf16 = jnp.bfloat16
    return pl.pallas_call(
        functools.partial(head_kernel, size),
        in_specs=[vmem, vmem, vmem, vmem],
        out_specs=[anywhere, anywhere, anywhere, anywhere, vmem],
        out_shape=[
            jax.ShapeDtypeStruct((2 * half_rows, features), bf16),
            jax.ShapeDtypeStruct((size, rows, width), bf16),
            jax.ShapeDtypeStruct((size, rows, width), bf16),
            jax.ShapeDtypeStruct((size, rows, 2 * columns), bf16),
            jax.ShapeDtypeStruct((8, features), jnp.float32),
        ],
        scratch_shapes=[
            pltpu.VMEM((size,) + gains.shape, jnp.float32),
            pltpu.VMEM((half_rows, features), bf16),
            dma((size - 1,)), dma((size - 1,)),
            dma((2, half)), dma((2, half)),
            dma((size,)), dma((size,)),
            dma((2, half)), dma((2, half)),
            dma((4,)), dma((3,)),
        ],
        compiler_params=pltpu.CompilerParams(collective_id=1, has_side_effects=True, vmem_limit_bytes=24 * 2**20),
        cost_estimate=pl.CostEstimate(flops=10**9, bytes_accessed=200 * 2**20, transcendentals=0),
        name="head",
    )(tokens, gains, attend_shard, output_shard)


def swap_core(v):
    return lax.ppermute(v, "tensor", [(t, t ^ 1) for t in range(4)])


def swap_chip(v):
    return lax.ppermute(v, "tensor", [(t, t ^ 2) for t in range(4)])


class Ring:
    def __init__(self, size):
        self.size = size
        self.half = size // 2
        order = list(range(0, size, 2)) + list(range(size - 1, 0, -2))
        self.forward = [(order[i], order[(i + 1) % size]) for i in range(size)]
        self.backward = [(b, a) for a, b in self.forward]
        own = lax.axis_index("dp")
        self.place = jnp.where(own % 2 == 0, own // 2, size - 1 - own // 2)

    def index(self, step):
        place = (self.place + step + self.size) % self.size
        return jnp.where(place < self.half, 2 * place, 2 * (self.size - 1 - place) + 1)

    def up(self, v):
        return lax.ppermute(v, "dp", self.forward)

    def down(self, v):
        return lax.ppermute(v, "dp", self.backward)

    def gather(self, shard, passed=False):
        rows, columns = shard.shape
        parts = [(0, shard)]
        others = []
        if passed:
            others.append((0, swap_chip(shard)))
        up = down = shard
        for step in range(1, self.half):
            up, down = self.up(up), self.down(down)
            parts += [(-step, up), (step, down)]
            if passed:
                both = swap_chip(jnp.concatenate([up, down], axis=0))
                others += [(-step, both[:rows]), (step, both[rows:])]
        cut = rows // 2
        last = jnp.concatenate([self.up(up[:cut]), self.down(down[cut:])], axis=0)
        parts.append((self.half, last))
        if passed:
            others.append((self.half, swap_chip(last)))

        def lay(pieces):
            whole = jnp.zeros((self.size * rows, columns), shard.dtype)
            for step, piece in pieces:
                whole = lax.dynamic_update_slice(whole, piece, (self.index(step) * rows, 0))
            return whole

        return (lay(parts), lay(others)) if passed else lay(parts)

    def scatter(self, take):
        far = take(self.index(self.half))
        cut = far.shape[0] // 2
        up, down = self.up(far[:cut]), self.down(far[cut:])
        for step in range(self.half - 1, 0, -1):
            ahead = take(self.index(step)).astype(jnp.float32)
            behind = take(self.index(-step)).astype(jnp.float32)
            if step == self.half - 1:
                ahead = jnp.concatenate([ahead[:cut] + up.astype(jnp.float32), ahead[cut:]], axis=0)
                behind = jnp.concatenate([behind[:cut], behind[cut:] + down.astype(jnp.float32)], axis=0)
            else:
                ahead = ahead + up.astype(jnp.float32)
                behind = behind + down.astype(jnp.float32)
            up, down = self.up(ahead.astype(jnp.bfloat16)), self.down(behind.astype(jnp.bfloat16))
        own = take(self.index(0)).astype(jnp.float32)
        return own + up.astype(jnp.float32) + down.astype(jnp.float32)


def times(left, right):
    return dot(left, right)


def times_transpose(left, right):
    return dot(left, right, ((1,), (1,)))


def contract_rows(left, right):
    return dot(left, right, ((0,), (0,)))


def local(
    dp_size,
    tokens,
    first_gain,
    query_weight,
    key_weight,
    value_weight,
    output_weight,
    second_gain,
    gate_weight,
    up_weight,
    down_weight,
    cotangent,
):
    ring = Ring(dp_size)
    half_rows = tokens.shape[0]
    core = lax.axis_index("tensor") % 2
    bf16, f32 = jnp.bfloat16, jnp.float32

    def pair(own, other):
        return jnp.where(
            core == 0,
            jnp.concatenate([own, other], axis=0),
            jnp.concatenate([other, own], axis=0),
        )

    def mine(rows):
        return lax.dynamic_slice_in_dim(rows, core * half_rows, half_rows, 0)

    def theirs(rows):
        return lax.dynamic_slice_in_dim(rows, (1 - core) * half_rows, half_rows, 0)

    groups = key_weight.shape[1] // HEAD
    packs = []
    for group in range(groups):
        packs.append(query_weight[:, group * 2 * HEAD : (group + 1) * 2 * HEAD])
        packs.append(key_weight[:, group * HEAD : (group + 1) * HEAD])
        packs.append(value_weight[:, group * HEAD : (group + 1) * HEAD])
    attend_shard = jnp.concatenate(packs, axis=1)
    output_shard = output_weight.T
    feed_shard = jnp.concatenate([gate_weight, up_weight, down_weight.T], axis=1)
    hidden_units = gate_weight.shape[1]

    lanes = LANES * pl.cdiv(first_gain.shape[0], LANES)
    both_gains = jnp.stack([first_gain, second_gain]).astype(f32)
    both_gains = jnp.pad(both_gains, ((0, 6), (0, lanes - first_gain.shape[0])))
    normed, attend_own, attend_other, output_both, gain_rows = head(
        dp_size, tokens, both_gains, attend_shard, output_shard
    )
    features = tokens.shape[1]
    attend_own = attend_own.reshape(features, -1)
    attend_other = attend_other.reshape(features, -1)
    output_both = output_both.reshape(features, -1)
    gain_one = gain_rows[0:1]
    gain_two = gain_rows[1:2]
    activations = tokens.astype(f32)
    inverse_one = lax.rsqrt(jnp.mean(activations * activations, axis=-1, keepdims=True) + norm_eps)

    normed, feed_shard, attend_own = lax.optimization_barrier((normed, feed_shard, attend_own))
    feed = ring.gather(feed_shard)
    gate_up = feed[:, : 2 * hidden_units]
    down_turned = feed[:, 2 * hidden_units :]

    qkv_own, attended_own, log_own = attend_fwd(normed, attend_own)
    qkv_other, attended_other, log_other = attend_fwd(normed, attend_other)
    heads = output_both.shape[1] // HEAD
    spread_heads = jnp.asarray(spread(heads, (0,) * heads), bf16)
    output_spread = times(output_both, spread_heads).astype(bf16)
    attended = jnp.concatenate([attended_own, attended_other], axis=1)
    attention_terms = times_transpose(attended, output_spread).astype(bf16)
    hidden_state = (
        activations
        + mine(attention_terms).astype(f32)
        + swap_core(theirs(attention_terms)).astype(f32)
    )
    inverse_two = lax.rsqrt(
        jnp.mean(hidden_state * hidden_state, axis=-1, keepdims=True) + norm_eps
    )
    normed_two_own = (hidden_state * inverse_two * gain_two).astype(bf16)

    def spread_rows(own):
        across = swap_chip(own)
        return pair(own, swap_core(own)), pair(across, swap_core(across))

    def gather_rows(near, far):
        near_sum = mine(near).astype(f32) + swap_core(theirs(near)).astype(f32)
        far_sum = mine(far).astype(f32) + swap_core(theirs(far)).astype(f32)
        return near_sum + swap_chip(far_sum.astype(bf16)).astype(f32)

    cot_near, cot_far = spread_rows(cotangent)
    two_near, two_far = spread_rows(normed_two_own)

    def feed_forward(two, cot):
        both = times(two, gate_up)
        gate, up = both[:, :hidden_units], both[:, hidden_units:]
        inner_grad = times(cot, down_turned)
        sigmoid = jax.nn.sigmoid(gate)
        inner = (gate * sigmoid * up).astype(bf16)
        up_grad = (inner_grad * gate * sigmoid).astype(bf16)
        gate_grad = (inner_grad * up * sigmoid * (1.0 + gate * (1.0 - sigmoid))).astype(bf16)
        return inner, jnp.concatenate([gate_grad, up_grad], axis=1)

    inner_near, grad_near = feed_forward(two_near, cot_near)
    inner_far, grad_far = feed_forward(two_far, cot_far)
    two_terms_far = times_transpose(grad_far, gate_up).astype(bf16)
    two_terms_near = times_transpose(grad_near, gate_up).astype(bf16)
    out_far = times_transpose(inner_far, down_turned).astype(bf16)
    out_near = times_transpose(inner_near, down_turned).astype(bf16)
    normed_two_grad = gather_rows(two_terms_near, two_terms_far)
    layer_out = (hidden_state + gather_rows(out_near, out_far)).astype(bf16)

    down_grad = contract_rows(
        jnp.concatenate([cot_near, cot_far], axis=0),
        jnp.concatenate([inner_near, inner_far], axis=0),
    ).astype(bf16)
    gate_up_grad = contract_rows(
        jnp.concatenate([two_near, two_far], axis=0),
        jnp.concatenate([grad_near, grad_far], axis=0),
    ).astype(bf16)
    shard_rows = first_gain.shape[0]

    def part(whole):
        return lambda index: lax.dynamic_slice_in_dim(whole, index * shard_rows, shard_rows, 0)

    down_sum = ring.scatter(part(down_grad))
    gate_up_sum = ring.scatter(part(gate_up_grad))

    scaled_two = normed_two_grad * gain_two
    hidden_grad = (
        cotangent.astype(f32)
        + inverse_two * scaled_two
        - hidden_state
        * inverse_two**3
        * jnp.mean(scaled_two * hidden_state, axis=-1, keepdims=True)
    )
    branch_own = hidden_grad.astype(bf16)
    branch = pair(branch_own, swap_core(branch_own))
    attended_grad = times(branch, output_spread).astype(bf16)
    width = attended_own.shape[1]
    other_back = attend_bwd(qkv_other, attended_other, attended_grad[:, width:], log_other)
    own_back = attend_bwd(qkv_own, attended_own, attended_grad[:, :width], log_own)

    attended_close = times_transpose(attended, spread_heads).astype(bf16)
    output_grad = contract_rows(branch, attended_close).astype(bf16)
    columns = output_shard.shape[1]
    output_grad = output_grad[:, :columns].astype(f32) + swap_chip(output_grad[:, columns:]).astype(
        f32
    )
    output_sum = ring.scatter(part(output_grad.astype(bf16)))

    other_grad = swap_chip(contract_rows(normed, other_back).astype(bf16))
    own_grad = contract_rows(normed, own_back)
    attend_grad = (own_grad + other_grad.astype(f32)).astype(bf16)
    attend_sum = ring.scatter(part(attend_grad))

    normed_terms = (
        times_transpose(own_back, attend_own) + times_transpose(other_back, attend_other)
    ).astype(bf16)
    normed_grad = mine(normed_terms).astype(f32) + swap_core(theirs(normed_terms)).astype(f32)
    scaled_one = normed_grad * gain_one
    tokens_grad = (
        hidden_grad
        + inverse_one * scaled_one
        - activations * inverse_one**3 * jnp.mean(scaled_one * activations, axis=-1, keepdims=True)
    ).astype(bf16)

    gain_sums = jnp.stack(
        [
            jnp.sum(attend_sum * attend_shard.astype(f32), axis=1) / first_gain.astype(f32),
            jnp.sum(gate_up_sum * feed_shard[:, : 2 * hidden_units].astype(f32), axis=1)
            / second_gain.astype(f32),
        ]
    )
    gain_sums = gain_sums + swap_core(gain_sums)
    gain_sums = gain_sums + swap_chip(gain_sums)

    block = 4 * HEAD
    query_grad = jnp.concatenate(
        [attend_sum[:, g * block : g * block + 2 * HEAD] for g in range(groups)], axis=1
    )
    key_grad = jnp.concatenate(
        [attend_sum[:, g * block + 2 * HEAD : g * block + 3 * HEAD] for g in range(groups)], axis=1
    )
    value_grad = jnp.concatenate(
        [attend_sum[:, g * block + 3 * HEAD : (g + 1) * block] for g in range(groups)], axis=1
    )
    return (
        layer_out,
        tokens_grad,
        gain_sums[0],
        query_grad,
        key_grad,
        value_grad,
        output_sum.T,
        gain_sums[1],
        gate_up_sum[:, :hidden_units],
        gate_up_sum[:, hidden_units:],
        down_sum.T,
    )


def solution(mesh):
    in_specs = (
        P(("dp", "tensor"), None),
        P("dp"),
        P("dp", "tensor"),
        P("dp", "tensor"),
        P("dp", "tensor"),
        P("tensor", "dp"),
        P("dp"),
        P("dp", "tensor"),
        P("dp", "tensor"),
        P("tensor", "dp"),
        P(("dp", "tensor"), None),
    )
    out_specs = (
        P(("dp", "tensor"), None),
        P(("dp", "tensor"), None),
        P("dp"),
        P("dp", "tensor"),
        P("dp", "tensor"),
        P("dp", "tensor"),
        P("tensor", "dp"),
        P("dp"),
        P("dp", "tensor"),
        P("dp", "tensor"),
        P("tensor", "dp"),
    )
    body = functools.partial(local, mesh.shape["dp"])
    return jax.shard_map(body, mesh=mesh, in_specs=in_specs, out_specs=out_specs, check_vma=False)
```

```python
import functools

import jax
import jax.numpy as jnp
import numpy as np
from jax import lax
from jax.experimental import pallas as pl
from jax.experimental.pallas import tpu as pltpu
from jax.sharding import PartitionSpec as P

HEAD = 96
LENGTH = 1024
LANES = 128
QB = 256
norm_eps = 1e-05
rope_base = 100000.0


def rope_tables():
    half = HEAD // 2
    freq = rope_base ** (np.arange(half, dtype=np.float64) * (-2.0 / HEAD))
    turned = np.arange(LENGTH, dtype=np.float64)[:, None] * freq[None, :]
    cos = np.zeros((LENGTH, LANES), np.float32); sin = np.zeros((LENGTH, LANES), np.float32)
    cos[:, :half] = np.cos(turned); cos[:, 64:64+half] = np.cos(turned)
    sin[:, :half] = -np.sin(turned); sin[:, 64:64+half] = np.sin(turned)
    return cos, sin

def spread(heads, rotary):
    e = np.zeros((heads * HEAD, heads * LANES), np.float32)
    for h in range(heads):
        for i in range(HEAD):
            lane = i if (not rotary[h] or i < 48) else i + 16
            e[h * HEAD + i, h * LANES + lane] = 1
    return e

def dot(a, b, dims=((1,), (0,))):
    return lax.dot_general(a, b, (dims, ((), ())), preferred_element_type=jnp.float32)

C2 = float(HEAD ** -0.5 * np.log2(np.e))


MESH = pl.DeviceIdType.MESH


class Places:
    def __init__(self, size):
        self.size = size
        self.half = size // 2
        self.own = lax.axis_index("dp")
        self.tensor = lax.axis_index("tensor")
        self.side = self.tensor % 2
        odd = self.own % 2
        self.place = (1 - odd) * (self.own // 2) + odd * (size - 1 - self.own // 2)

    def index(self, step):
        place = (self.place + step + self.size) % self.size
        late = place // self.half
        return (1 - late) * 2 * place + late * (2 * (self.size - 1 - place) + 1)

    def on_ring(self, step):
        return (self.index(step), self.tensor)

    def peer(self, step):
        return ((self.own + step + self.size) % self.size, self.tensor)

    def chip(self):
        return (self.own, (self.tensor + 2) % 4)

    def core(self):
        return (self.own, self.tensor + 1 - 2 * self.side)


def remote(source, target, send, receive, device):
    return pltpu.make_async_remote_copy(
        src_ref=source,
        dst_ref=target,
        send_sem=send,
        recv_sem=receive,
        device_id=device,
        device_id_type=MESH,
    )


def greet(devices):
    barrier = pltpu.get_barrier_semaphore()
    for device in devices:
        pl.semaphore_signal(barrier, inc=1, device_id=device, device_id_type=MESH)
    pl.semaphore_wait(barrier, len(devices))


class RingGather:
    def __init__(self, places, slots, send, receive):
        self.places, self.slots, self.send, self.receive = places, slots, send, receive
        self.cut = slots.shape[1] // 32 * 16
        self.sent = []

    def start(self, hop, source=None):
        places, half = self.places, self.places.half
        for way, (step, device) in enumerate(
            ((1 - hop, places.on_ring(1)), (hop - 1, places.on_ring(-1)))
        ):
            slot = places.index(step)
            rows = pl.ds(0, self.slots.shape[1])
            if hop == half:
                rows = (pl.ds(0, self.cut), pl.ds(self.cut, self.slots.shape[1] - self.cut))[way]
            view = self.slots.at[slot, rows]
            copy = remote(
                view if source is None else source.at[rows],
                view,
                self.send.at[way, hop - 1],
                self.receive.at[way, hop - 1],
                device,
            )
            copy.start()
            self.sent.append(copy)

    def wait(self, hop):
        self.sent[2 * hop - 2].wait_recv()
        self.sent[2 * hop - 1].wait_recv()

    def finish(self):
        for copy in self.sent:
            copy.wait_send()


class Spread:
    def __init__(self, places, own, slots, send, receive):
        self.places, self.slots, self.send, self.receive = places, slots, send, receive
        near, far = slots.at[places.side], slots.at[2 + places.side]
        self.chip = remote(own, far, send.at[0], receive.at[0], places.chip())
        self.core = remote(own, near, send.at[1], receive.at[1], places.core())
        self.far = far

    def start(self):
        self.chip.start()
        self.core.start()

    def pass_on(self):
        self.chip.wait_recv()
        self.last = remote(self.far, self.far, self.send.at[2], self.receive.at[2], self.places.core())
        self.last.start()

    def finish(self):
        self.chip.wait_send()
        self.core.wait()
        self.last.wait()


def begin_kernel(
    size, tokens, cotangent, gains, attend_shard, output_shard, feed_shard, cos_ref, sin_ref, rotary_spread,
    plain_spread,
    normed, weights, output_spread, qkv_ref, att_ref, log_ref, hidden, two_slots, cot_slots, feed, gain_rows,
    gain_slots, output_both, terms, received, two_own, gain_send, gain_receive, ring_send, ring_receive,
    pass_send, pass_receive, out_send, out_receive, feed_send, feed_receive, across, two_send, two_receive,
    cot_send, cot_receive, local_sem,
):
    bf16, f32 = jnp.bfloat16, jnp.float32
    places = Places(size)
    half, own = places.half, places.own
    half_rows = tokens.shape[0]
    columns = output_shard.shape[1]
    width = attend_shard.shape[1]
    greet([places.peer(step) for step in range(1, size)] + [places.chip(), places.core()])

    def own_side(slot):
        return weights.at[slot, :, pl.ds(0, width)]

    def other_side(slot):
        return weights.at[slot, :, pl.ds(width, width)]

    ring = RingGather(places, weights.at[:, :, pl.ds(0, width)], ring_send, ring_receive)
    ring.start(1, attend_shard)
    passed = []

    def hand_on(step, number, source=None):
        slot = places.index(step)
        copy = remote(
            own_side(slot) if source is None else source, other_side(slot),
            pass_send.at[number], pass_receive.at[number], places.chip(),
        )
        copy.start()
        passed.append(copy)

    hand_on(0, 0, attend_shard)
    output_pass = remote(
        output_shard, output_both.at[own, :, pl.ds(columns, columns)], across.at[0], across.at[1], places.chip()
    )
    output_pass.start()
    gain_copies = []
    for step in range(1, size):
        copy = remote(gains, gain_slots.at[own], gain_send.at[step - 1], gain_receive.at[step - 1], places.peer(step))
        copy.start()
        gain_copies.append(copy)
    near = cot_slots.at[places.side]
    keep = [
        pltpu.make_async_copy(attend_shard, own_side(own), local_sem.at[0]),
        pltpu.make_async_copy(output_shard, output_both.at[own, :, pl.ds(0, columns)], local_sem.at[1]),
        pltpu.make_async_copy(feed_shard, feed.at[own], local_sem.at[2]),
        pltpu.make_async_copy(cotangent, near, local_sem.at[3]),
    ]
    for copy in keep:
        copy.start()
    gain_slots[own] = gains[...]
    for copy in gain_copies:
        copy.wait_recv()
    part = tokens.shape[1] // size
    for index in range(size):
        gain_rows[:, index * part : (index + 1) * part] = gain_slots[index][:, :part]
    tile = 64
    mine_start = places.side * half_rows

    def norm_tile(number, carry):
        rows = pl.ds(pl.multiple_of(number * tile, tile), tile)
        values = tokens[rows, :].astype(f32)
        inverse = lax.rsqrt(jnp.mean(values * values, axis=1, keepdims=True) + norm_eps)
        target = pl.ds(pl.multiple_of(mine_start + number * tile, tile), tile)
        normed[target, :] = (values * inverse * gain_rows[0:1, :]).astype(bf16)
        return carry

    lax.fori_loop(0, half_rows // tile, norm_tile, 0)
    mine = pl.ds(pl.multiple_of(mine_start, half_rows), half_rows)
    swap = remote(normed.at[mine], normed.at[mine], across.at[2], across.at[3], places.core())
    swap.start()

    for hop in range(1, half + 1):
        ring.wait(hop)
        if hop < half:
            ring.start(hop + 1)
            hand_on(-hop, 2 * hop - 1)
            hand_on(hop, 2 * hop)
        else:
            hand_on(half, size - 1)
    outputs = RingGather(places, output_both, out_send, out_receive)
    output_pass.wait()
    for copy in keep:
        copy.wait()
    outputs.start(1)
    swap.wait()

    def attend(group):
        lanes = pl.ds(group * 4 * HEAD, 4 * HEAD)
        weight = weights[:, :, lanes].reshape(tokens.shape[1], 4 * HEAD)
        weight = dot(weight, rotary_spread[...]).astype(bf16)
        rows = dot(normed[...], weight)
        cos, sin = cos_ref[...], sin_ref[...]
        base = group * 4 * LANES

        def rot(u):
            return (u * cos + pltpu.roll(u, 64, 1) * sin).astype(bf16)

        for head in range(3):
            lane = head * LANES
            qkv_ref[:, base + lane : base + lane + LANES] = rot(rows[:, lane : lane + LANES])
        qkv_ref[:, base + 3 * LANES : base + 4 * LANES] = rows[:, 3 * LANES :].astype(bf16)
        turned = qkv_ref[:, base + 3 * LANES : base + 4 * LANES].T
        key_place = lax.broadcasted_iota(jnp.int32, (QB, QB), 0)
        query_place = lax.broadcasted_iota(jnp.int32, (QB, QB), 1)
        for head in range(2):
            for block in range(LENGTH // QB):
                first, last = block * QB, (block + 1) * QB
                query = qkv_ref[first:last, base + head * LANES : base + (head + 1) * LANES]
                key = qkv_ref[:last, base + 2 * LANES : base + 3 * LANES]
                score = dot(key, query, ((1,), (1,)))
                edge = jnp.where(key_place <= query_place, score[first:], -1e30)
                score = jnp.concatenate([score[:first], edge], axis=0) if block else edge
                top = jnp.max(score, axis=0, keepdims=True)
                weight = jnp.exp2((score - top) * C2)
                total = jnp.sum(weight, axis=0, keepdims=True)
                result = dot(turned[:, :last], weight.astype(bf16)) / total
                lane = group * 2 * LANES + head * LANES
                att_ref[first:last, lane : lane + LANES] = result.T.astype(bf16)
                log_ref[group, head, pl.ds(first, QB)] = (top * C2 + jnp.log2(total))[0]

    attend(0)
    outputs.wait(1)
    outputs.start(2)
    attend(1)
    for hop in range(2, half + 1):
        outputs.wait(hop)
        if hop < half:
            outputs.start(hop + 1)
    ring_feed = RingGather(places, feed, feed_send, feed_receive)
    ring_feed.start(1, feed_shard)
    for copy in passed:
        copy.wait()
    cot = Spread(places, cotangent, cot_slots, cot_send, cot_receive)
    cot.start()
    attend(2)
    attend(3)
    ring_feed.wait(1)
    ring_feed.start(2)

    heads_width = columns // HEAD * LANES
    out_rows = output_shard.shape[0]

    def spread_slot(number, carry):
        rows = pl.ds(pl.multiple_of(number * out_rows, out_rows), out_rows)
        for side in range(2):
            value = dot(output_both[number, :, side * columns : (side + 1) * columns], plain_spread[...])
            output_spread[rows, side * heads_width : (side + 1) * heads_width] = value.astype(bf16)
        return carry

    lax.fori_loop(0, size, spread_slot, 0)
    big = 256

    def theirs_tile(number, carry):
        start = (1 - places.side) * half_rows + number * big
        rows = pl.ds(pl.multiple_of(start, big), big)
        value = dot(att_ref[rows, :], output_spread[...], ((1,), (1,)))
        terms[pl.ds(pl.multiple_of(number * big, big), big), :] = value.astype(bf16)
        return carry

    lax.fori_loop(0, half_rows // big, theirs_tile, 0)
    sum_swap = remote(terms, received, across.at[4], across.at[5], places.core())
    sum_swap.start()

    def mine_tile(number, carry):
        rows = pl.ds(pl.multiple_of(mine_start + number * big, big), big)
        value = dot(att_ref[rows, :], output_spread[...], ((1,), (1,)))
        here = pl.ds(pl.multiple_of(number * big, big), big)
        hidden[here, :] = value + tokens[here, :].astype(f32)
        return carry

    lax.fori_loop(0, half_rows // big, mine_tile, 0)
    sum_swap.wait()

    def second_tile(number, carry):
        rows = pl.ds(pl.multiple_of(number * tile, tile), tile)
        values = hidden[rows, :] + received[rows, :].astype(f32)
        hidden[rows, :] = values
        inverse = lax.rsqrt(jnp.mean(values * values, axis=1, keepdims=True) + norm_eps)
        two_own[rows, :] = (values * inverse * gain_rows[1:2, :]).astype(bf16)
        return carry

    lax.fori_loop(0, half_rows // tile, second_tile, 0)
    two = Spread(places, two_own, two_slots, two_send, two_receive)
    two.start()
    keep_two = pltpu.make_async_copy(two_own, two_slots.at[places.side], local_sem.at[4])
    keep_two.start()
    ring_feed.wait(2)
    ring_feed.start(3)
    cot.pass_on()
    for hop in range(3, half + 1):
        ring_feed.wait(hop)
        if hop < half:
            ring_feed.start(hop + 1)
    two.pass_on()
    cot.finish()
    two.finish()
    keep_two.wait()
    for copy in gain_copies:
        copy.wait_send()
    ring.finish()
    outputs.finish()
    ring_feed.finish()


def begin(size, tokens, cotangent, gains, attend_shard, output_shard, feed_shard):
    half_rows, features = tokens.shape
    rows, width = attend_shard.shape
    columns = output_shard.shape[1]
    heads_width = columns // HEAD * LANES
    groups = 2 * width // (4 * HEAD)
    vmem = pl.BlockSpec(memory_space=pltpu.VMEM)
    anywhere = pl.BlockSpec(memory_space=pl.ANY)
    dma = pltpu.SemaphoreType.DMA
    half = size // 2
    bf16, f32 = jnp.bfloat16, jnp.float32
    cos, sin = rope_tables()
    shape = jax.ShapeDtypeStruct
    return pl.pallas_call(
        functools.partial(begin_kernel, size),
        in_specs=[vmem] * 10,
        out_specs=[vmem, vmem, vmem, vmem, vmem, vmem, vmem, anywhere, anywhere, anywhere, vmem],
        out_shape=[
            shape((2 * half_rows, features), bf16),
            shape((size, rows, 2 * width), bf16),
            shape((features, 2 * heads_width), bf16),
            shape((LENGTH, groups * 4 * LANES), bf16),
            shape((LENGTH, groups * 2 * LANES), bf16),
            shape((groups, 2, LENGTH), f32),
            shape((half_rows, features), f32),
            shape((4, half_rows, features), bf16),
            shape((4, half_rows, features), bf16),
            shape((size,) + feed_shard.shape, bf16),
            shape((8, features), f32),
        ],
        scratch_shapes=[
            pltpu.VMEM((size,) + gains.shape, f32),
            pltpu.VMEM((size, rows, 2 * columns), bf16),
            pltpu.VMEM((half_rows, features), bf16),
            pltpu.VMEM((half_rows, features), bf16),
            pltpu.VMEM((half_rows, features), bf16),
            dma((size - 1,)), dma((size - 1,)),
            dma((2, half)), dma((2, half)),
            dma((size,)), dma((size,)),
            dma((2, half)), dma((2, half)),
            dma((2, half)), dma((2, half)),
            dma((6,)),
            dma((3,)), dma((3,)),
            dma((3,)), dma((3,)),
            dma((5,)),
        ],
        compiler_params=pltpu.CompilerParams(collective_id=1, has_side_effects=True, vmem_limit_bytes=56 * 2**20),
        cost_estimate=pl.CostEstimate(flops=10**10, bytes_accessed=400 * 2**20, transcendentals=0),
        name="begin",
    )(
        tokens, cotangent, gains, attend_shard, output_shard, feed_shard, jnp.asarray(cos), jnp.asarray(sin),
        jnp.asarray(spread(4, (1, 1, 1, 0)), bf16), jnp.asarray(spread(columns // HEAD, (0,) * 4), bf16),
    )


class RingScatter:
    def __init__(self, places, partial, received, send, receive):
        self.places, self.partial, self.received = places, partial, received
        self.send, self.receive = send, receive
        self.rows = received.shape[2]
        self.cut = self.rows // 32 * 16
        self.sent = []

    def start(self, hop):
        places = self.places
        for way in range(2):
            rows = pl.ds(0, self.rows)
            if hop == 1:
                rows = (pl.ds(0, self.cut), pl.ds(self.cut, self.rows - self.cut))[way]
                source = self.partial(places.index(places.half)).at[rows]
            else:
                source = self.received.at[way, hop - 2]
            copy = remote(
                source,
                self.received.at[way, hop - 1, rows],
                self.send.at[way, hop - 1],
                self.receive.at[way, hop - 1],
                places.on_ring(1 - 2 * way),
            )
            copy.start()
            self.sent.append(copy)

    def wait(self, hop):
        self.sent[2 * hop - 2].wait_recv()
        self.sent[2 * hop - 1].wait_recv()

    def add(self, hop):
        distance = self.places.half - hop
        for way in range(2):
            own = self.partial(self.places.index(distance * (1 - 2 * way)))
            here = self.received.at[way, hop - 1]
            first, last = 0, self.rows // 16
            if hop == 1:
                first, last = ((0, self.cut // 16), (self.cut // 16, last))[way]
                start, count = ((self.cut, self.rows - self.cut), (0, self.cut))[way]
                here[start : start + count, :] = own[start : start + count, :]

            def tile(number, carry, own=own, here=here):
                rows = pl.ds(pl.multiple_of(number * 16, 16), 16)
                here[rows, :] = (here[rows, :].astype(jnp.float32) + own[rows, :].astype(jnp.float32)).astype(jnp.bfloat16)
                return carry

            lax.fori_loop(first, last, tile, 0)

    def total(self, rows):
        half = self.places.half
        own = self.partial(self.places.index(0))
        return (
            own[rows, :].astype(jnp.float32)
            + self.received[0, half - 1, rows, :].astype(jnp.float32)
            + self.received[1, half - 1, rows, :].astype(jnp.float32)
        )

    def finish(self):
        for copy in self.sent:
            copy.wait_send()


def finish_kernel(
    size, tokens_hbm, hidden_hbm, branch_own, normed_hbm, weights_hbm, output_hbm, qkv_hbm, att_hbm, feed_grad,
    second_part, log_ref, gain_rows, attend_shard, cos_ref, sin_ref, rotary_spread, plain_spread,
    tokens_grad, attend_sum, output_sum, feed_sum, gain_sum,
    branch, grad_ref, back, dq_ref, dk_ref, dv_ref, own_grad, other_grad, crossed, ring_got, output_grad, output_got,
    feed_got, feed_own, terms, got_terms, output_across, gain_parts,
    normed, weights, output_spread, qkv_two, att_ref, tokens, hidden_grad, load_sem,
    ring_send, ring_receive, out_send, out_receive, feed_send, feed_receive, cross_send, cross_receive, across,
    feed_sem, gain_send, gain_receive,
):
    bf16, f32 = jnp.bfloat16, jnp.float32
    places = Places(size)
    half, own = places.half, places.own
    half_rows, features = tokens_hbm.shape
    rows = attend_shard.shape[0]
    width = attend_shard.shape[1]
    span = 4 * HEAD
    diagonal = (own, 3 - places.tensor)
    greet([places.on_ring(1), places.on_ring(-1), places.chip(), places.core(), diagonal])

    def feed_slot(number):
        return feed_grad.at[pl.ds(pl.multiple_of(number * rows, rows), rows)]

    big = 256
    group_order = (2, 3, 0, 1)

    def qkv_load(number):
        lanes = pl.ds(group_order[number] * 4 * LANES, 4 * LANES)
        return pltpu.make_async_copy(qkv_hbm.at[:, lanes], qkv_two.at[number % 2], load_sem.at[number])

    def row_loads(number):
        here = pl.ds(number * big, big)
        return (
            pltpu.make_async_copy(tokens_hbm.at[here], tokens, load_sem.at[4]),
            pltpu.make_async_copy(hidden_hbm.at[here], hidden_grad, load_sem.at[5]),
        )

    mine = pl.ds(pl.multiple_of(places.side * half_rows, half_rows), half_rows)
    fetch = {
        "branch": pltpu.make_async_copy(branch_own, branch.at[mine], load_sem.at[6]),
        "output": pltpu.make_async_copy(output_hbm, output_spread, load_sem.at[7]),
        "att": pltpu.make_async_copy(att_hbm, att_ref, load_sem.at[8]),
        "normed": pltpu.make_async_copy(normed_hbm, normed, load_sem.at[9]),
        "weights": pltpu.make_async_copy(weights_hbm, weights, load_sem.at[10]),
    }
    loads = []

    def load(step, way):
        copy = pltpu.make_async_copy(feed_slot(places.index(step)), feed_own.at[way], feed_sem.at[len(loads)])
        copy.start()
        loads.append(copy)

    load(half, 0)
    swap = remote(branch_own, branch.at[mine], across.at[0], across.at[1], places.core())
    swap.start()
    fetch["branch"].start()
    fetch["output"].start()
    qkv_loads = [qkv_load(number) for number in range(4)]
    qkv_loads[0].start()
    for name in ("att", "normed", "weights"):
        fetch[name].start()

    current = {}

    def feed_partial(number):
        return current["slot"]

    feed = RingScatter(places, feed_partial, feed_got, feed_send, feed_receive)

    def feed_step(hop):
        feed.wait(hop)
        loads[-2].wait()
        loads[-1].wait()
        distance = half - hop
        for way in range(2):
            part = feed_own.at[way]
            here = feed_got.at[way, hop - 1]
            first, last = 0, rows // 16
            if hop == 1:
                first, last = ((0, feed.cut // 16), (feed.cut // 16, last))[way]
                start, count = ((feed.cut, rows - feed.cut), (0, feed.cut))[way]
                here[start : start + count, :] = part[start : start + count, :]

            def tile(number, carry, part=part, here=here):
                place = pl.ds(pl.multiple_of(number * 16, 16), 16)
                here[place, :] = (here[place, :].astype(f32) + part[place, :].astype(f32)).astype(bf16)
                return carry

            lax.fori_loop(first, last, tile, 0)
        feed.start(hop + 1)
        if distance > 1:
            load(distance - 1, 0)
            load(1 - distance, 1)
        else:
            load(0, 0)

    loads[0].wait()
    current["slot"] = feed_own.at[0]
    feed.start(1)
    swap.wait()
    fetch["branch"].wait()
    fetch["output"].wait()
    fetch["att"].wait()
    token_rows = row_loads(0)
    for copy in token_rows:
        copy.start()

    def back_group(number, target, lane):
        group = group_order[number]
        qkv_loads[number].wait()
        if number < 3:
            qkv_loads[number + 1].start()
        qkv_ref = qkv_two.at[number % 2]
        base = 0
        for part in range(2):
            block = pl.ds(part * half_rows, half_rows)
            value = dot(branch[block, :], output_spread[:, group * 2 * LANES : (group + 1) * 2 * LANES])
            grad_ref[block, :] = value.astype(bf16)
        turned = qkv_ref[:, base + 2 * LANES : base + 3 * LANES].T
        cos, sin = cos_ref[...], sin_ref[...]
        scale = HEAD**-0.5

        def unrot(u):
            return (u * cos - pltpu.roll(u, 64, 1) * sin).astype(bf16)

        key_place = lax.broadcasted_iota(jnp.int32, (QB, QB), 0)
        query_place = lax.broadcasted_iota(jnp.int32, (QB, QB), 1)
        for head in range(2):
            lanes = slice(head * LANES, (head + 1) * LANES)
            att_lane = (2 * group + head) * LANES
            prod = grad_ref[:, lanes].astype(f32) * att_ref[:, att_lane : att_lane + LANES].astype(f32)
            delta = jnp.sum(prod.T, axis=0, keepdims=True)
            for block in reversed(range(LENGTH // QB)):
                first, last = block * QB, (block + 1) * QB
                query = qkv_ref[first:last, base + head * LANES : base + (head + 1) * LANES]
                out_grad = grad_ref[first:last, lanes]
                score = dot(qkv_ref[:last, base + 2 * LANES : base + 3 * LANES], query, ((1,), (1,)))
                prob = jnp.exp2(score * C2 - log_ref[group, head : head + 1, first:last])
                edge = jnp.where(key_place <= query_place, prob[first:], 0.0)
                prob = jnp.concatenate([prob[:first], edge], axis=0) if block else edge
                prob_grad = dot(qkv_ref[:last, base + 3 * LANES : base + 4 * LANES], out_grad, ((1,), (1,)))
                score_grad = (prob * (prob_grad - delta[:, first:last])).astype(bf16)
                key_part = dot(score_grad, query)
                value_part = dot(prob.astype(bf16), out_grad)
                if head == 0 and block == LENGTH // QB - 1:
                    dk_ref[...] = key_part
                    dv_ref[...] = value_part
                else:
                    dk_ref[:last] += key_part
                    dv_ref[:last] += value_part
                dq_ref[first:last, lanes] = dot(turned[:, :last], score_grad).T
        wide = jnp.concatenate(
            [
                unrot(dq_ref[:, :LANES] * scale),
                unrot(dq_ref[:, LANES:] * scale),
                unrot(dk_ref[...] * scale),
                dv_ref[...].astype(bf16),
            ],
            axis=1,
        )
        close_back = dot(wide, rotary_spread[...], ((1,), (1,))).astype(bf16)
        back[:, group * span : (group + 1) * span] = close_back
        if number == 0:
            fetch["normed"].wait()
        for part in range(2):
            block = slice(part * features // 2, (part + 1) * features // 2)
            value = dot(normed[:, block], close_back, ((0,), (0,))).astype(bf16)
            target[part * size // 2 : (part + 1) * size // 2, :, lane : lane + span] = value.reshape(
                size // 2, rows, span
            )

    order = [half]
    for step in range(half - 1, 0, -1):
        order += [step, -step]
    order.append(0)
    crossing = {}

    def cross(group):
        for number, step in enumerate(order):
            slot = places.index(step)
            lanes = pl.ds(group * span, span)
            copy = remote(
                other_grad.at[slot, :, lanes], crossed.at[slot, :, lanes],
                cross_send.at[group, number], cross_receive.at[group, number], places.chip(),
            )
            copy.start()
            crossing[(group, step)] = copy

    back_group(0, other_grad, 0)
    cross(0)
    for copy in feed.sent:
        copy.wait_send()
    load(half - 1, 0)
    load(1 - half, 1)
    back_group(1, other_grad, span)
    cross(1)
    feed_step(1)

    def prepare(step):
        for group in range(2):
            crossing[(group, step)].wait_recv()
        slot = places.index(step)

        def tile(number, carry):
            place = pl.ds(pl.multiple_of(number * 16, 16), 16)
            crossed[slot, place, :] = (crossed[slot, place, :].astype(f32) + own_grad[slot, place, :].astype(f32)).astype(bf16)
            return carry

        lax.fori_loop(0, rows // 16, tile, 0)

    back_group(2, own_grad, 0)
    back_group(3, own_grad, span)

    columns = output_spread.shape[1] // 2 // LANES * HEAD
    heads_width = output_spread.shape[1] // 2
    for side in range(2):
        close = dot(att_ref[:, side * heads_width : (side + 1) * heads_width], plain_spread[...], ((1,), (1,))).astype(bf16)
        for part in range(2):
            block = slice(part * features // 2, (part + 1) * features // 2)
            value = dot(branch[:, block], close, ((0,), (0,))).astype(bf16)
            output_grad[part * size // 2 : (part + 1) * size // 2, :, side * columns : (side + 1) * columns] = value.reshape(
                size // 2, rows, columns
            )
    outputs = RingScatter(places, lambda slot: output_grad.at[slot], output_got, out_send, out_receive)
    outputs.start(1)
    feed_step(2)

    whole = weights.shape[2]
    fetch["weights"].wait()

    def terms_of(block):
        return dot(back[block, :], weights[...].reshape(features, whole), ((1,), (1,)))

    def theirs_tile(number, carry):
        place = (1 - places.side) * half_rows + number * big
        value = terms_of(pl.ds(pl.multiple_of(place, big), big))
        terms[pl.ds(pl.multiple_of(number * big, big), big), :] = value.astype(bf16)
        return carry

    lax.fori_loop(0, half_rows // big, theirs_tile, 0)
    terms_swap = remote(terms, got_terms, across.at[2], across.at[3], places.core())
    terms_swap.start()
    prepare(half)
    attend = RingScatter(places, lambda slot: crossed.at[slot], ring_got, ring_send, ring_receive)
    attend.start(1)
    outputs.wait(1)
    outputs.add(1)
    outputs.start(2)
    terms_swap.wait()

    for number in range(half_rows // big):
        for copy in token_rows:
            copy.wait()
        here = slice(number * big, (number + 1) * big)
        place = places.side * half_rows + number * big
        value = terms_of(pl.ds(pl.multiple_of(place, big), big)) + got_terms[here, :].astype(f32)
        values = tokens[...].astype(f32)
        inverse = lax.rsqrt(jnp.mean(values * values, axis=1, keepdims=True) + norm_eps)
        scaled = value * gain_rows[0:1, :]
        inner = jnp.mean(scaled * values, axis=1, keepdims=True)
        result = hidden_grad[...] + inverse * scaled - values * (inverse * inverse * inverse) * inner
        tokens_grad[here, :] = result.astype(bf16)
        if number < half_rows // big - 1:
            token_rows = row_loads(number + 1)
            for copy in token_rows:
                copy.start()
    prepare(half - 1)
    prepare(1 - half)
    attend.wait(1)
    attend.add(1)
    attend.start(2)
    for hop in range(2, half + 1):
        outputs.wait(hop)
        if hop < half:
            outputs.add(hop)
            outputs.start(hop + 1)
        if hop > 2 and hop < half:
            feed_step(hop)
        if hop < half:
            prepare(half - hop)
            prepare(hop - half)
            attend.wait(hop)
            attend.add(hop)
            attend.start(hop + 1)
    prepare(0)

    def output_total(place):
        return outputs.total(place)

    def output_tile(number, carry):
        place = pl.ds(pl.multiple_of(number * 16, 16), 16)
        value = output_total(place)
        output_sum[place, :] = value[:, :columns]
        output_across[0, place, :] = value[:, columns:]
        return carry

    lax.fori_loop(0, rows // 16, output_tile, 0)
    output_swap = remote(output_across.at[0], output_across.at[1], across.at[4], across.at[5], places.chip())
    output_swap.start()
    attend.wait(half)

    def attend_tile(number, carry):
        place = pl.ds(pl.multiple_of(number * 16, 16), 16)
        value = attend.total(place)
        attend_sum[place, :] = value
        gain = jnp.sum(value * attend_shard[place, :].astype(f32), axis=1, keepdims=True)
        lane = lax.broadcasted_iota(jnp.int32, (16, LANES), 1)
        gain_parts[0, place, :] = jnp.where(lane == 0, gain, 0.0)
        return carry

    lax.fori_loop(0, rows // 16, attend_tile, 0)
    feed.wait(half)
    loads[-1].wait()
    second = pltpu.make_async_copy(second_part, feed_own.at[1], load_sem.at[11])
    second.start()
    second.wait()

    def feed_tile(number, carry):
        place = pl.ds(pl.multiple_of(number * 16, 16), 16)
        value = (
            feed_own[0, place, :].astype(f32)
            + feed_got[0, half - 1, place, :].astype(f32)
            + feed_got[1, half - 1, place, :].astype(f32)
        )
        feed_sum[place, :] = value
        gain = jnp.sum(value * feed_own[1, place, :].astype(f32), axis=1, keepdims=True)
        lane = lax.broadcasted_iota(jnp.int32, (16, LANES), 1)
        gain_parts[0, place, :] += jnp.where(lane == 1, gain, 0.0)
        return carry

    lax.fori_loop(0, rows // 16, feed_tile, 0)
    gain_copies = []
    for number, device in enumerate((places.core(), places.chip(), diagonal)):
        copy = remote(gain_parts.at[0], gain_parts.at[1 + number], gain_send.at[number], gain_receive.at[number], device)
        copy.start()
        gain_copies.append(copy)
    output_swap.wait()
    output_sum[...] += output_across[1]
    for copy in gain_copies:
        copy.wait()
    gain_sum[...] = (gain_parts[0] + gain_parts[1]) + (gain_parts[2] + gain_parts[3])
    for copy in crossing.values():
        copy.wait_send()
    outputs.finish()
    attend.finish()
    for copy in feed.sent[2:]:
        copy.wait_send()


def finish(
    size, tokens, hidden_grad, branch_own, normed, weights, output_spread, qkv, att, logs, gain_rows, feed_grad,
    attend_shard, second_part,
):
    half_rows, features = tokens.shape
    rows, width = attend_shard.shape
    columns = output_spread.shape[1] // 2 // LANES * HEAD
    feed_width = feed_grad.shape[1]
    vmem = pl.BlockSpec(memory_space=pltpu.VMEM)
    anywhere = pl.BlockSpec(memory_space=pl.ANY)
    dma = pltpu.SemaphoreType.DMA
    half = size // 2
    bf16, f32 = jnp.bfloat16, jnp.float32
    cos, sin = rope_tables()
    shape = jax.ShapeDtypeStruct
    buffer = pltpu.VMEM
    return pl.pallas_call(
        functools.partial(finish_kernel, size),
        in_specs=[anywhere] * 10 + [vmem] * 7,
        out_specs=[vmem] * 5,
        out_shape=[
            shape((half_rows, features), bf16),
            shape((rows, width), f32),
            shape((rows, columns), f32),
            shape((rows, feed_width), f32),
            shape((rows, LANES), f32),
        ],
        scratch_shapes=[
            buffer((LENGTH, features), bf16),
            buffer((LENGTH, 2 * LANES), bf16),
            buffer((LENGTH, 2 * width), bf16),
            buffer((LENGTH, 2 * LANES), f32),
            buffer((LENGTH, LANES), f32),
            buffer((LENGTH, LANES), f32),
            buffer((size, rows, width), bf16),
            buffer((size, rows, width), bf16),
            buffer((size, rows, width), bf16),
            buffer((2, half, rows, width), bf16),
            buffer((size, rows, 2 * columns), bf16),
            buffer((2, half, rows, 2 * columns), bf16),
            buffer((2, half, rows, feed_width), bf16),
            buffer((2, rows, feed_width), bf16),
            buffer((half_rows, features), bf16),
            buffer((half_rows, features), bf16),
            buffer((2, rows, columns), f32),
            buffer((4, rows, LANES), f32),
            buffer((LENGTH, features), bf16),
            buffer(weights.shape, bf16),
            buffer(output_spread.shape, bf16),
            buffer((2, LENGTH, 4 * LANES), bf16),
            buffer(att.shape, bf16),
            buffer((256, features), bf16),
            buffer((256, features), f32),
            dma((12,)),
            dma((2, half)), dma((2, half)),
            dma((2, half)), dma((2, half)),
            dma((2, half)), dma((2, half)),
            dma((2, size)), dma((2, size)),
            dma((6,)),
            dma((2 * half,)),
            dma((3,)), dma((3,)),
        ],
        compiler_params=pltpu.CompilerParams(collective_id=2, has_side_effects=True, vmem_limit_bytes=62 * 2**20),
        cost_estimate=pl.CostEstimate(flops=3 * 10**10, bytes_accessed=300 * 2**20, transcendentals=0),
        name="finish",
    )(
        tokens, hidden_grad, branch_own, normed, weights, output_spread, qkv, att, feed_grad, second_part, logs,
        gain_rows, attend_shard, jnp.asarray(cos), jnp.asarray(sin),
        jnp.asarray(spread(4, (1, 1, 1, 0)), bf16), jnp.asarray(spread(4, (0,) * 4), bf16),
    )


def swap_core(v):
    return lax.ppermute(v, "tensor", [(t, t ^ 1) for t in range(4)])


def swap_chip(v):
    return lax.ppermute(v, "tensor", [(t, t ^ 2) for t in range(4)])


class Ring:
    def __init__(self, size):
        self.size = size
        self.half = size // 2
        order = list(range(0, size, 2)) + list(range(size - 1, 0, -2))
        self.forward = [(order[i], order[(i + 1) % size]) for i in range(size)]
        self.backward = [(b, a) for a, b in self.forward]
        own = lax.axis_index("dp")
        self.place = jnp.where(own % 2 == 0, own // 2, size - 1 - own // 2)

    def index(self, step):
        place = (self.place + step + self.size) % self.size
        return jnp.where(place < self.half, 2 * place, 2 * (self.size - 1 - place) + 1)

    def up(self, v):
        return lax.ppermute(v, "dp", self.forward)

    def down(self, v):
        return lax.ppermute(v, "dp", self.backward)

    def scatter(self, take):
        far = take(self.index(self.half))
        cut = far.shape[0] // 2
        up, down = self.up(far[:cut]), self.down(far[cut:])
        for step in range(self.half - 1, 0, -1):
            ahead = take(self.index(step)).astype(jnp.float32)
            behind = take(self.index(-step)).astype(jnp.float32)
            if step == self.half - 1:
                ahead = jnp.concatenate([ahead[:cut] + up.astype(jnp.float32), ahead[cut:]], axis=0)
                behind = jnp.concatenate([behind[:cut], behind[cut:] + down.astype(jnp.float32)], axis=0)
            else:
                ahead = ahead + up.astype(jnp.float32)
                behind = behind + down.astype(jnp.float32)
            up, down = self.up(ahead.astype(jnp.bfloat16)), self.down(behind.astype(jnp.bfloat16))
        own = take(self.index(0)).astype(jnp.float32)
        return own + up.astype(jnp.float32) + down.astype(jnp.float32)


def times(left, right):
    return dot(left, right)


def times_transpose(left, right):
    return dot(left, right, ((1,), (1,)))


def contract_rows(left, right):
    return dot(left, right, ((0,), (0,)))


def local(
    dp_size,
    tokens,
    first_gain,
    query_weight,
    key_weight,
    value_weight,
    output_weight,
    second_gain,
    gate_weight,
    up_weight,
    down_weight,
    cotangent,
):
    ring = Ring(dp_size)
    half_rows = tokens.shape[0]
    core = lax.axis_index("tensor") % 2
    bf16, f32 = jnp.bfloat16, jnp.float32

    def pair(own, other):
        return jnp.where(
            core == 0,
            jnp.concatenate([own, other], axis=0),
            jnp.concatenate([other, own], axis=0),
        )

    def mine(rows):
        return lax.dynamic_slice_in_dim(rows, core * half_rows, half_rows, 0)

    def theirs(rows):
        return lax.dynamic_slice_in_dim(rows, (1 - core) * half_rows, half_rows, 0)

    groups = key_weight.shape[1] // HEAD
    packs = []
    for group in range(groups):
        packs.append(query_weight[:, group * 2 * HEAD : (group + 1) * 2 * HEAD])
        packs.append(key_weight[:, group * HEAD : (group + 1) * HEAD])
        packs.append(value_weight[:, group * HEAD : (group + 1) * HEAD])
    attend_shard = jnp.concatenate(packs, axis=1)
    output_shard = output_weight.T
    feed_shard = jnp.concatenate([gate_weight, up_weight, down_weight.T], axis=1)
    hidden_units = gate_weight.shape[1]

    lanes = LANES * pl.cdiv(first_gain.shape[0], LANES)
    both_gains = jnp.stack([first_gain, second_gain]).astype(f32)
    both_gains = jnp.pad(both_gains, ((0, 6), (0, lanes - first_gain.shape[0])))
    gate_up_shard, down_shard = feed_shard[:, : 2 * hidden_units], feed_shard[:, 2 * hidden_units :]
    (normed, weights, output_spread, qkv, attended, logs, hidden_state, two_slots, cot_slots, feed, gain_rows) = begin(
        dp_size, tokens, cotangent, both_gains, attend_shard, output_shard, feed_shard
    )
    features = tokens.shape[1]
    feed = feed.reshape(features, -1)
    gate_up = feed[:, : 2 * hidden_units]
    down_turned = feed[:, 2 * hidden_units :]
    gain_two = gain_rows[1:2]
    inverse_two = lax.rsqrt(
        jnp.mean(hidden_state * hidden_state, axis=-1, keepdims=True) + norm_eps
    )
    two_all = two_slots.reshape(-1, features)
    cot_all = cot_slots.reshape(-1, features)
    both_rows = 2 * half_rows
    two_near, two_far = two_all[:both_rows], two_all[both_rows:]
    cot_near, cot_far = cot_all[:both_rows], cot_all[both_rows:]

    def gather_rows(near, far):
        near_sum = mine(near).astype(f32) + swap_core(theirs(near)).astype(f32)
        far_sum = mine(far).astype(f32) + swap_core(theirs(far)).astype(f32)
        return near_sum + swap_chip(far_sum.astype(bf16)).astype(f32)

    def feed_forward(two, cot):
        both = times(two, gate_up)
        gate, up = both[:, :hidden_units], both[:, hidden_units:]
        inner_grad = times(cot, down_turned)
        sigmoid = jax.nn.sigmoid(gate)
        inner = (gate * sigmoid * up).astype(bf16)
        up_grad = (inner_grad * gate * sigmoid).astype(bf16)
        gate_grad = (inner_grad * up * sigmoid * (1.0 + gate * (1.0 - sigmoid))).astype(bf16)
        return inner, jnp.concatenate([gate_grad, up_grad], axis=1)

    inner_near, grad_near = feed_forward(two_near, cot_near)
    inner_far, grad_far = feed_forward(two_far, cot_far)
    two_terms_far = times_transpose(grad_far, gate_up).astype(bf16)
    two_terms_near = times_transpose(grad_near, gate_up).astype(bf16)
    out_far = times_transpose(inner_far, down_turned).astype(bf16)
    out_near = times_transpose(inner_near, down_turned).astype(bf16)
    normed_two_grad = gather_rows(two_terms_near, two_terms_far)
    layer_out = (hidden_state + gather_rows(out_near, out_far)).astype(bf16)

    down_grad = contract_rows(
        cot_all,
        jnp.concatenate([inner_near, inner_far], axis=0),
    ).astype(bf16)
    gate_up_grad = contract_rows(
        two_all,
        jnp.concatenate([grad_near, grad_far], axis=0),
    ).astype(bf16)
    shard_rows = first_gain.shape[0]

    def part(whole):
        return lambda index: lax.dynamic_slice_in_dim(whole, index * shard_rows, shard_rows, 0)

    down_sum = ring.scatter(part(down_grad))

    scaled_two = normed_two_grad * gain_two
    hidden_grad = (
        cotangent.astype(f32)
        + inverse_two * scaled_two
        - hidden_state
        * inverse_two**3
        * jnp.mean(scaled_two * hidden_state, axis=-1, keepdims=True)
    )
    branch_own = hidden_grad.astype(bf16)
    tokens_grad, attend_sum, output_sum, gate_up_sum, gain_sums = finish(
        dp_size, tokens, hidden_grad, branch_own, normed, weights, output_spread, qkv, attended, logs, gain_rows,
        gate_up_grad, attend_shard, gate_up_shard,
    )
    block = 4 * HEAD
    query_grad = jnp.concatenate(
        [attend_sum[:, g * block : g * block + 2 * HEAD] for g in range(groups)], axis=1
    )
    key_grad = jnp.concatenate(
        [attend_sum[:, g * block + 2 * HEAD : g * block + 3 * HEAD] for g in range(groups)], axis=1
    )
    value_grad = jnp.concatenate(
        [attend_sum[:, g * block + 3 * HEAD : (g + 1) * block] for g in range(groups)], axis=1
    )
    return (
        layer_out,
        tokens_grad,
        gain_sums[:, 0] / first_gain.astype(f32),
        query_grad,
        key_grad,
        value_grad,
        output_sum.T,
        gain_sums[:, 1] / second_gain.astype(f32),
        gate_up_sum[:, :hidden_units],
        gate_up_sum[:, hidden_units:],
        down_sum.T,
    )


def solution(mesh):
    in_specs = (
        P(("dp", "tensor"), None),
        P("dp"),
        P("dp", "tensor"),
        P("dp", "tensor"),
        P("dp", "tensor"),
        P("tensor", "dp"),
        P("dp"),
        P("dp", "tensor"),
        P("dp", "tensor"),
        P("tensor", "dp"),
        P(("dp", "tensor"), None),
    )
    out_specs = (
        P(("dp", "tensor"), None),
        P(("dp", "tensor"), None),
        P("dp"),
        P("dp", "tensor"),
        P("dp", "tensor"),
        P("dp", "tensor"),
        P("tensor", "dp"),
        P("dp"),
        P("dp", "tensor"),
        P("dp", "tensor"),
        P("tensor", "dp"),
    )
    body = functools.partial(local, mesh.shape["dp"])
    return jax.shard_map(body, mesh=mesh, in_specs=in_specs, out_specs=out_specs, check_vma=False)
```

```python
import functools

import jax
import jax.numpy as jnp
import numpy as np
from jax import lax
from jax.experimental import pallas as pl
from jax.experimental.pallas import tpu as pltpu
from jax.sharding import PartitionSpec as P

HEAD = 96
LENGTH = 1024
LANES = 128
QB = 256
norm_eps = 1e-05
rope_base = 100000.0


def rope_tables():
    half = HEAD // 2
    freq = rope_base ** (np.arange(half, dtype=np.float64) * (-2.0 / HEAD))
    turned = np.arange(LENGTH, dtype=np.float64)[:, None] * freq[None, :]
    cos = np.zeros((LENGTH, LANES), np.float32); sin = np.zeros((LENGTH, LANES), np.float32)
    cos[:, :half] = np.cos(turned); cos[:, 64:64+half] = np.cos(turned)
    sin[:, :half] = -np.sin(turned); sin[:, 64:64+half] = np.sin(turned)
    return cos, sin

def spread(heads, rotary):
    e = np.zeros((heads * HEAD, heads * LANES), np.float32)
    for h in range(heads):
        for i in range(HEAD):
            lane = i if (not rotary[h] or i < 48) else i + 16
            e[h * HEAD + i, h * LANES + lane] = 1
    return e

def dot(a, b, dims=((1,), (0,))):
    return lax.dot_general(a, b, (dims, ((), ())), preferred_element_type=jnp.float32)

C2 = float(HEAD ** -0.5 * np.log2(np.e))


MESH = pl.DeviceIdType.MESH


class Places:
    def __init__(self, size):
        self.size = size
        self.half = size // 2
        self.own = lax.axis_index("dp")
        self.tensor = lax.axis_index("tensor")
        self.side = self.tensor % 2
        odd = self.own % 2
        self.place = (1 - odd) * (self.own // 2) + odd * (size - 1 - self.own // 2)

    def index(self, step):
        place = (self.place + step + self.size) % self.size
        late = place // self.half
        return (1 - late) * 2 * place + late * (2 * (self.size - 1 - place) + 1)

    def on_ring(self, step):
        return (self.index(step), self.tensor)

    def peer(self, step):
        return ((self.own + step + self.size) % self.size, self.tensor)

    def chip(self):
        return (self.own, (self.tensor + 2) % 4)

    def core(self):
        return (self.own, self.tensor + 1 - 2 * self.side)


def remote(source, target, send, receive, device):
    return pltpu.make_async_remote_copy(
        src_ref=source,
        dst_ref=target,
        send_sem=send,
        recv_sem=receive,
        device_id=device,
        device_id_type=MESH,
    )


def greet(devices):
    barrier = pltpu.get_barrier_semaphore()
    for device in devices:
        pl.semaphore_signal(barrier, inc=1, device_id=device, device_id_type=MESH)
    pl.semaphore_wait(barrier, len(devices))


class RingGather:
    def __init__(self, places, slots, send, receive):
        self.places, self.slots, self.send, self.receive = places, slots, send, receive
        self.cut = slots.shape[1] // 32 * 16
        self.sent = []

    def start(self, hop, source=None):
        places, half = self.places, self.places.half
        for way, (step, device) in enumerate(
            ((1 - hop, places.on_ring(1)), (hop - 1, places.on_ring(-1)))
        ):
            slot = places.index(step)
            rows = pl.ds(0, self.slots.shape[1])
            if hop == half:
                rows = (pl.ds(0, self.cut), pl.ds(self.cut, self.slots.shape[1] - self.cut))[way]
            view = self.slots.at[slot, rows]
            copy = remote(
                view if source is None else source.at[rows],
                view,
                self.send.at[way, hop - 1],
                self.receive.at[way, hop - 1],
                device,
            )
            copy.start()
            self.sent.append(copy)

    def wait(self, hop):
        self.sent[2 * hop - 2].wait_recv()
        self.sent[2 * hop - 1].wait_recv()

    def finish(self):
        for copy in self.sent:
            copy.wait_send()


class Spread:
    def __init__(self, places, own, slots, send, receive):
        self.places, self.slots, self.send, self.receive = places, slots, send, receive
        near, far = slots.at[places.side], slots.at[2 + places.side]
        self.chip = remote(own, far, send.at[0], receive.at[0], places.chip())
        self.core = remote(own, near, send.at[1], receive.at[1], places.core())
        self.far = far

    def start(self):
        self.chip.start()
        self.core.start()

    def pass_on(self):
        self.chip.wait_recv()
        self.last = remote(self.far, self.far, self.send.at[2], self.receive.at[2], self.places.core())
        self.last.start()

    def finish(self):
        self.chip.wait_send()
        self.core.wait()
        self.last.wait()


def begin_kernel(
    size, tokens, cotangent, gains, attend_shard, output_shard, feed_shard, cos_ref, sin_ref, rotary_spread,
    plain_spread,
    normed, weights, output_spread, qkv_ref, att_ref, log_ref, hidden, two_slots, cot_slots, feed, gain_rows,
    gain_slots, output_both, terms, received, two_own, gain_send, gain_receive, ring_send, ring_receive,
    pass_send, pass_receive, out_send, out_receive, feed_send, feed_receive, across, two_send, two_receive,
    cot_send, cot_receive, local_sem,
):
    bf16, f32 = jnp.bfloat16, jnp.float32
    places = Places(size)
    half, own = places.half, places.own
    half_rows = tokens.shape[0]
    columns = output_shard.shape[1]
    width = attend_shard.shape[1]
    greet([places.peer(step) for step in range(1, size)] + [places.chip(), places.core()])

    def own_side(slot):
        return weights.at[slot, :, pl.ds(0, width)]

    def other_side(slot):
        return weights.at[slot, :, pl.ds(width, width)]

    ring = RingGather(places, weights.at[:, :, pl.ds(0, width)], ring_send, ring_receive)
    ring.start(1, attend_shard)
    passed = []

    def hand_on(step, number, source=None):
        slot = places.index(step)
        copy = remote(
            own_side(slot) if source is None else source, other_side(slot),
            pass_send.at[number], pass_receive.at[number], places.chip(),
        )
        copy.start()
        passed.append(copy)

    hand_on(0, 0, attend_shard)
    output_pass = remote(
        output_shard, output_both.at[own, :, pl.ds(columns, columns)], across.at[0], across.at[1], places.chip()
    )
    output_pass.start()
    gain_copies = []
    for step in range(1, size):
        copy = remote(gains, gain_slots.at[own], gain_send.at[step - 1], gain_receive.at[step - 1], places.peer(step))
        copy.start()
        gain_copies.append(copy)
    near = cot_slots.at[places.side]
    keep = [
        pltpu.make_async_copy(attend_shard, own_side(own), local_sem.at[0]),
        pltpu.make_async_copy(output_shard, output_both.at[own, :, pl.ds(0, columns)], local_sem.at[1]),
        pltpu.make_async_copy(feed_shard, feed.at[own], local_sem.at[2]),
        pltpu.make_async_copy(cotangent, near, local_sem.at[3]),
    ]
    for copy in keep:
        copy.start()
    gain_slots[own] = gains[...]
    for copy in gain_copies:
        copy.wait_recv()
    part = tokens.shape[1] // size
    for index in range(size):
        gain_rows[:, index * part : (index + 1) * part] = gain_slots[index][:, :part]
    tile = 64
    mine_start = places.side * half_rows

    def norm_tile(number, carry):
        rows = pl.ds(pl.multiple_of(number * tile, tile), tile)
        values = tokens[rows, :].astype(f32)
        inverse = lax.rsqrt(jnp.mean(values * values, axis=1, keepdims=True) + norm_eps)
        target = pl.ds(pl.multiple_of(mine_start + number * tile, tile), tile)
        normed[target, :] = (values * inverse * gain_rows[0:1, :]).astype(bf16)
        return carry

    lax.fori_loop(0, half_rows // tile, norm_tile, 0)
    mine = pl.ds(pl.multiple_of(mine_start, half_rows), half_rows)
    swap = remote(normed.at[mine], normed.at[mine], across.at[2], across.at[3], places.core())
    swap.start()

    for hop in range(1, half + 1):
        ring.wait(hop)
        if hop < half:
            ring.start(hop + 1)
            hand_on(-hop, 2 * hop - 1)
            hand_on(hop, 2 * hop)
        else:
            hand_on(half, size - 1)
    outputs = RingGather(places, output_both, out_send, out_receive)
    output_pass.wait()
    for copy in keep:
        copy.wait()
    outputs.start(1)
    swap.wait()

    def attend(group):
        lanes = pl.ds(group * 4 * HEAD, 4 * HEAD)
        weight = weights[:, :, lanes].reshape(tokens.shape[1], 4 * HEAD)
        weight = dot(weight, rotary_spread[...]).astype(bf16)
        rows = dot(normed[...], weight)
        cos, sin = cos_ref[...], sin_ref[...]
        base = group * 4 * LANES

        def rot(u):
            return (u * cos + pltpu.roll(u, 64, 1) * sin).astype(bf16)

        for head in range(3):
            lane = head * LANES
            qkv_ref[:, base + lane : base + lane + LANES] = rot(rows[:, lane : lane + LANES])
        qkv_ref[:, base + 3 * LANES : base + 4 * LANES] = rows[:, 3 * LANES :].astype(bf16)
        turned = qkv_ref[:, base + 3 * LANES : base + 4 * LANES].T
        key_place = lax.broadcasted_iota(jnp.int32, (QB, QB), 0)
        query_place = lax.broadcasted_iota(jnp.int32, (QB, QB), 1)
        for head in range(2):
            for block in range(LENGTH // QB):
                first, last = block * QB, (block + 1) * QB
                query = qkv_ref[first:last, base + head * LANES : base + (head + 1) * LANES]
                key = qkv_ref[:last, base + 2 * LANES : base + 3 * LANES]
                score = dot(key, query, ((1,), (1,)))
                edge = jnp.where(key_place <= query_place, score[first:], -1e30)
                score = jnp.concatenate([score[:first], edge], axis=0) if block else edge
                top = jnp.max(score, axis=0, keepdims=True)
                weight = jnp.exp2((score - top) * C2)
                total = jnp.sum(weight, axis=0, keepdims=True)
                result = dot(turned[:, :last], weight.astype(bf16)) / total
                lane = group * 2 * LANES + head * LANES
                att_ref[first:last, lane : lane + LANES] = result.T.astype(bf16)
                log_ref[group, head, pl.ds(first, QB)] = (top * C2 + jnp.log2(total))[0]

    attend(0)
    outputs.wait(1)
    outputs.start(2)
    attend(1)
    for hop in range(2, half + 1):
        outputs.wait(hop)
        if hop < half:
            outputs.start(hop + 1)
    ring_feed = RingGather(places, feed, feed_send, feed_receive)
    ring_feed.start(1, feed_shard)
    for copy in passed:
        copy.wait()
    cot = Spread(places, cotangent, cot_slots, cot_send, cot_receive)
    cot.start()
    attend(2)
    attend(3)
    ring_feed.wait(1)
    ring_feed.start(2)

    heads_width = columns // HEAD * LANES
    out_rows = output_shard.shape[0]

    def spread_slot(number, carry):
        rows = pl.ds(pl.multiple_of(number * out_rows, out_rows), out_rows)
        for side in range(2):
            value = dot(output_both[number, :, side * columns : (side + 1) * columns], plain_spread[...])
            output_spread[rows, side * heads_width : (side + 1) * heads_width] = value.astype(bf16)
        return carry

    lax.fori_loop(0, size, spread_slot, 0)
    big = 256

    def theirs_tile(number, carry):
        start = (1 - places.side) * half_rows + number * big
        rows = pl.ds(pl.multiple_of(start, big), big)
        value = dot(att_ref[rows, :], output_spread[...], ((1,), (1,)))
        terms[pl.ds(pl.multiple_of(number * big, big), big), :] = value.astype(bf16)
        return carry

    lax.fori_loop(0, half_rows // big, theirs_tile, 0)
    sum_swap = remote(terms, received, across.at[4], across.at[5], places.core())
    sum_swap.start()

    def mine_tile(number, carry):
        rows = pl.ds(pl.multiple_of(mine_start + number * big, big), big)
        value = dot(att_ref[rows, :], output_spread[...], ((1,), (1,)))
        here = pl.ds(pl.multiple_of(number * big, big), big)
        hidden[here, :] = value + tokens[here, :].astype(f32)
        return carry

    lax.fori_loop(0, half_rows // big, mine_tile, 0)
    sum_swap.wait()

    def second_tile(number, carry):
        rows = pl.ds(pl.multiple_of(number * tile, tile), tile)
        values = hidden[rows, :] + received[rows, :].astype(f32)
        hidden[rows, :] = values
        inverse = lax.rsqrt(jnp.mean(values * values, axis=1, keepdims=True) + norm_eps)
        two_own[rows, :] = (values * inverse * gain_rows[1:2, :]).astype(bf16)
        return carry

    lax.fori_loop(0, half_rows // tile, second_tile, 0)
    two = Spread(places, two_own, two_slots, two_send, two_receive)
    two.start()
    keep_two = pltpu.make_async_copy(two_own, two_slots.at[places.side], local_sem.at[4])
    keep_two.start()
    ring_feed.wait(2)
    ring_feed.start(3)
    cot.pass_on()
    for hop in range(3, half + 1):
        ring_feed.wait(hop)
        if hop < half:
            ring_feed.start(hop + 1)
    two.pass_on()
    cot.finish()
    two.finish()
    keep_two.wait()
    for copy in gain_copies:
        copy.wait_send()
    ring.finish()
    outputs.finish()
    ring_feed.finish()


def begin(size, tokens, cotangent, gains, attend_shard, output_shard, feed_shard):
    half_rows, features = tokens.shape
    rows, width = attend_shard.shape
    columns = output_shard.shape[1]
    heads_width = columns // HEAD * LANES
    groups = 2 * width // (4 * HEAD)
    vmem = pl.BlockSpec(memory_space=pltpu.VMEM)
    anywhere = pl.BlockSpec(memory_space=pl.ANY)
    dma = pltpu.SemaphoreType.DMA
    half = size // 2
    bf16, f32 = jnp.bfloat16, jnp.float32
    cos, sin = rope_tables()
    shape = jax.ShapeDtypeStruct
    return pl.pallas_call(
        functools.partial(begin_kernel, size),
        in_specs=[vmem] * 10,
        out_specs=[vmem, vmem, vmem, vmem, vmem, vmem, vmem, anywhere, anywhere, anywhere, vmem],
        out_shape=[
            shape((2 * half_rows, features), bf16),
            shape((size, rows, 2 * width), bf16),
            shape((features, 2 * heads_width), bf16),
            shape((LENGTH, groups * 4 * LANES), bf16),
            shape((LENGTH, groups * 2 * LANES), bf16),
            shape((groups, 2, LENGTH), f32),
            shape((half_rows, features), f32),
            shape((4, half_rows, features), bf16),
            shape((4, half_rows, features), bf16),
            shape((size,) + feed_shard.shape, bf16),
            shape((8, features), f32),
        ],
        scratch_shapes=[
            pltpu.VMEM((size,) + gains.shape, f32),
            pltpu.VMEM((size, rows, 2 * columns), bf16),
            pltpu.VMEM((half_rows, features), bf16),
            pltpu.VMEM((half_rows, features), bf16),
            pltpu.VMEM((half_rows, features), bf16),
            dma((size - 1,)), dma((size - 1,)),
            dma((2, half)), dma((2, half)),
            dma((size,)), dma((size,)),
            dma((2, half)), dma((2, half)),
            dma((2, half)), dma((2, half)),
            dma((6,)),
            dma((3,)), dma((3,)),
            dma((3,)), dma((3,)),
            dma((5,)),
        ],
        compiler_params=pltpu.CompilerParams(collective_id=1, has_side_effects=True, vmem_limit_bytes=56 * 2**20),
        cost_estimate=pl.CostEstimate(flops=10**10, bytes_accessed=400 * 2**20, transcendentals=0),
        name="begin",
    )(
        tokens, cotangent, gains, attend_shard, output_shard, feed_shard, jnp.asarray(cos), jnp.asarray(sin),
        jnp.asarray(spread(4, (1, 1, 1, 0)), bf16), jnp.asarray(spread(columns // HEAD, (0,) * 4), bf16),
    )


class RingScatter:
    def __init__(self, places, partial, received, send, receive):
        self.places, self.partial, self.received = places, partial, received
        self.send, self.receive = send, receive
        self.rows = received.shape[2]
        self.cut = self.rows // 32 * 16
        self.sent = []

    def start(self, hop):
        places = self.places
        for way in range(2):
            rows = pl.ds(0, self.rows)
            if hop == 1:
                rows = (pl.ds(0, self.cut), pl.ds(self.cut, self.rows - self.cut))[way]
                source = self.partial(places.index(places.half)).at[rows]
            else:
                source = self.received.at[way, hop - 2]
            copy = remote(
                source,
                self.received.at[way, hop - 1, rows],
                self.send.at[way, hop - 1],
                self.receive.at[way, hop - 1],
                places.on_ring(1 - 2 * way),
            )
            copy.start()
            self.sent.append(copy)

    def wait(self, hop):
        self.sent[2 * hop - 2].wait_recv()
        self.sent[2 * hop - 1].wait_recv()

    def add(self, hop):
        distance = self.places.half - hop
        for way in range(2):
            own = self.partial(self.places.index(distance * (1 - 2 * way)))
            here = self.received.at[way, hop - 1]
            first, last = 0, self.rows // 16
            if hop == 1:
                first, last = ((0, self.cut // 16), (self.cut // 16, last))[way]
                start, count = ((self.cut, self.rows - self.cut), (0, self.cut))[way]
                here[start : start + count, :] = own[start : start + count, :]

            def tile(number, carry, own=own, here=here):
                rows = pl.ds(pl.multiple_of(number * 16, 16), 16)
                here[rows, :] = (here[rows, :].astype(jnp.float32) + own[rows, :].astype(jnp.float32)).astype(jnp.bfloat16)
                return carry

            lax.fori_loop(first, last, tile, 0)

    def total(self, rows):
        half = self.places.half
        own = self.partial(self.places.index(0))
        return (
            own[rows, :].astype(jnp.float32)
            + self.received[0, half - 1, rows, :].astype(jnp.float32)
            + self.received[1, half - 1, rows, :].astype(jnp.float32)
        )

    def finish(self):
        for copy in self.sent:
            copy.wait_send()


def middle_kernel(
    size, two_slots, cot_slots, feed, hidden_hbm, cot_own, gain_rows,
    gate_up_grad, down_sum, hidden_grad, branch, far_out, near_out,
    two, cot, weights, inner, grads, down_grad, down_got, outgoing, far_part, core_far, core_near, chip_got,
    stage, hidden, half_result, load_sem, stage_sem, ring_send, ring_receive, send_sem, receive_sem, store_sem,
):
    bf16, f32 = jnp.bfloat16, jnp.float32
    places = Places(size)
    half = places.half
    half_rows, features = hidden_hbm.shape
    rows = feed.shape[1]
    units = inner.shape[1]
    greet([places.on_ring(1), places.on_ring(-1), places.chip(), places.core()])

    fetch = [pltpu.make_async_copy(feed, weights, load_sem.at[0])]
    for number, slot in enumerate((2, 3, 0, 1)):
        here = pl.ds(slot * half_rows, half_rows)
        fetch.append(pltpu.make_async_copy(two_slots.at[slot], two.at[here], load_sem.at[1 + 2 * number]))
        fetch.append(pltpu.make_async_copy(cot_slots.at[slot], cot.at[here], load_sem.at[2 + 2 * number]))
    for copy in fetch:
        copy.start()
    fetch[0].wait()
    block = 512

    def weight_lanes(start, count):
        return weights[:, :, pl.ds(start, count)].reshape(features, count)

    def feed_forward(slot):
        here = pl.ds(slot * half_rows, half_rows)

        def column(number, carry):
            lane = pl.multiple_of(number * block, block)
            gate = dot(two[here, :], weight_lanes(lane, block))
            up = dot(two[here, :], weight_lanes(pl.multiple_of(units + lane, block), block))
            inner_grad = dot(cot[here, :], weight_lanes(pl.multiple_of(2 * units + lane, block), block))
            sigmoid = 1.0 / (1.0 + jnp.exp(-gate))
            silu = gate * sigmoid
            inner[here, pl.ds(lane, block)] = (silu * up).astype(bf16)
            grads[here, pl.ds(lane, block)] = (inner_grad * up * (sigmoid + silu * (1.0 - sigmoid))).astype(bf16)
            grads[here, pl.ds(pl.multiple_of(units + lane, block), block)] = (inner_grad * silu).astype(bf16)
            return carry

        lax.fori_loop(0, units // block, column, 0)

    big = 256
    mine_start = places.side * half_rows
    theirs_start = (1 - places.side) * half_rows
    both_rows = 2 * half_rows

    def terms_to(target, start, left, first, count):
        def tile(number, carry):
            place = pl.ds(pl.multiple_of(start + number * big, big), big)
            value = dot(left[place, :], weight_lanes(first, count), ((1,), (1,)))
            target[pl.ds(pl.multiple_of(number * big, big), big), :] = value.astype(bf16)
            return carry

        lax.fori_loop(0, half_rows // big, tile, 0)

    def add_to(target, other):
        def tile(number, carry):
            place = pl.ds(pl.multiple_of(number * 32, 32), 32)
            target[place, :] = (target[place, :].astype(f32) + other[place, :].astype(f32)).astype(bf16)
            return carry

        lax.fori_loop(0, half_rows // 32, tile, 0)

    for number, slot in enumerate((2, 3)):
        fetch[1 + 2 * number].wait()
        fetch[2 + 2 * number].wait()
        feed_forward(slot)
    terms_to(outgoing, both_rows + theirs_start, grads, 0, 2 * units)
    far_swap = remote(outgoing, core_far, send_sem.at[0], receive_sem.at[0], places.core())
    far_swap.start()
    terms_to(far_part, both_rows + mine_start, grads, 0, 2 * units)
    far_swap.wait()
    add_to(far_part, core_far)
    chip_swap = remote(far_part, chip_got, send_sem.at[1], receive_sem.at[1], places.chip())
    chip_swap.start()
    for number, slot in enumerate((0, 1)):
        fetch[5 + 2 * number].wait()
        fetch[6 + 2 * number].wait()
        feed_forward(slot)

    span = 384
    per_span = span // rows

    def down_tile(number, carry):
        lanes = pl.ds(pl.multiple_of(number * span, span), span)
        value = dot(cot[:, lanes], inner[...], ((0,), (0,))).astype(bf16)
        down_grad[pl.ds(number * per_span, per_span)] = value.reshape(per_span, rows, units)
        return carry

    lax.fori_loop(0, features // span, down_tile, 0)
    ring = RingScatter(places, lambda slot: down_grad.at[slot], down_got, ring_send, ring_receive)
    ring.start(1)

    terms_to(outgoing, theirs_start, grads, 0, 2 * units)
    near_swap = remote(outgoing, core_near, send_sem.at[2], receive_sem.at[2], places.core())
    near_swap.start()

    def stage_copy(number, side):
        place = pl.ds(pl.multiple_of(number * span, span), span)
        return pltpu.make_async_copy(stage.at[side], gate_up_grad.at[place, pl.ds(side * units, units)], stage_sem.at[side])

    def gate_up_tile(number, carry):
        lanes = pl.ds(pl.multiple_of(number * span, span), span)
        for side in range(2):
            value = dot(two[:, lanes], grads[:, side * units : (side + 1) * units], ((0,), (0,))).astype(bf16)

            @pl.when(number > 0)
            def _(side=side):
                stage_copy(number - 1, side).wait()

            stage[side] = value
            stage_copy(number, side).start()
        return carry

    spans = features // span
    for part in range(2):
        lax.fori_loop(part * spans // 2, (part + 1) * spans // 2, gate_up_tile, 0)
        if part == 0:
            ring.wait(1)
            ring.add(1)
            ring.start(2)
    for side in range(2):
        stage_copy(spans - 1, side).wait()

    near_swap.wait()
    chip_swap.wait()
    for number in range(half_rows // big):
        here = pl.ds(number * big, big)
        if number > 0:
            store_grad.wait()
        load_hidden = pltpu.make_async_copy(hidden_hbm.at[here], hidden, load_sem.at[9])
        load_cot = pltpu.make_async_copy(cot_own.at[here], half_result.at[number], load_sem.at[10])
        load_hidden.start()
        load_cot.start()
        place = pl.ds(pl.multiple_of(mine_start + number * big, big), big)
        value = dot(grads[place, :], weight_lanes(0, 2 * units), ((1,), (1,)))
        value = value + core_near[here, :].astype(f32) + chip_got[here, :].astype(f32)
        load_hidden.wait()
        load_cot.wait()
        values = hidden[...]
        inverse = lax.rsqrt(jnp.mean(values * values, axis=1, keepdims=True) + norm_eps)
        scaled = value * gain_rows[1:2, :]
        mean = jnp.mean(scaled * values, axis=1, keepdims=True)
        total = half_result[number].astype(f32) + inverse * scaled - values * (inverse * inverse * inverse) * mean
        hidden[...] = total
        half_result[number] = total.astype(bf16)
        store_grad = pltpu.make_async_copy(hidden, hidden_grad.at[here], store_sem.at[0])
        store_grad.start()
        branch_place = branch.at[pl.ds(pl.multiple_of(mine_start + number * big, big), big)]
        keep = pltpu.make_async_copy(half_result.at[number], branch_place, store_sem.at[1 + number])
        send = remote(half_result.at[number], branch_place, send_sem.at[3 + number], receive_sem.at[3 + number], places.core())
        keep.start()
        send.start()
        if number == 0:
            first = (keep, send)
    store_grad.wait()
    ring.wait(2)
    if half > 2:
        ring.add(2)
        ring.start(3)

    down = 2 * units
    terms_to(outgoing, both_rows + theirs_start, inner, down, units)
    far_swap = remote(outgoing, core_far, send_sem.at[5], receive_sem.at[5], places.core())
    far_swap.start()
    terms_to(far_part, both_rows + mine_start, inner, down, units)
    far_swap.wait()
    add_to(far_part, core_far)
    store_far = pltpu.make_async_copy(far_part, far_out, store_sem.at[3])
    store_far.start()
    terms_to(outgoing, theirs_start, inner, down, units)
    near_swap = remote(outgoing, core_near, send_sem.at[6], receive_sem.at[6], places.core())
    near_swap.start()
    for number in range(half_rows // big):
        here = pl.ds(number * big, big)
        if number > 0:
            store_near.wait()
        load_hidden = pltpu.make_async_copy(hidden_hbm.at[here], hidden, load_sem.at[9])
        load_hidden.start()
        place = pl.ds(pl.multiple_of(mine_start + number * big, big), big)
        value = dot(inner[place, :], weight_lanes(down, units), ((1,), (1,)))
        load_hidden.wait()
        if number == 0:
            near_swap.wait()
        hidden[...] = value + hidden[...] + core_near[here, :].astype(f32)
        store_near = pltpu.make_async_copy(hidden, near_out.at[here], store_sem.at[4])
        store_near.start()
    store_near.wait()
    store_far.wait()
    for keep, send in (first, (keep, send)):
        keep.wait()
        send.wait()
    for hop in range(3, half):
        ring.wait(hop)
        ring.add(hop)
        ring.start(hop + 1)
    if half > 2:
        ring.wait(half)

    def down_total(number, carry):
        place = pl.ds(pl.multiple_of(number * 16, 16), 16)
        down_sum[place, :] = ring.total(place)
        return carry

    lax.fori_loop(0, rows // 16, down_total, 0)
    ring.finish()


def middle(size, two_slots, cot_slots, feed, hidden_state, cotangent, gain_rows):
    half_rows, features = hidden_state.shape
    rows, width = feed.shape[1:]
    units = width // 3
    vmem = pl.BlockSpec(memory_space=pltpu.VMEM)
    anywhere = pl.BlockSpec(memory_space=pl.ANY)
    dma = pltpu.SemaphoreType.DMA
    half = size // 2
    bf16, f32 = jnp.bfloat16, jnp.float32
    shape = jax.ShapeDtypeStruct
    buffer = pltpu.VMEM
    return pl.pallas_call(
        functools.partial(middle_kernel, size),
        in_specs=[anywhere] * 5 + [vmem],
        out_specs=[anywhere, vmem, anywhere, anywhere, anywhere, anywhere],
        out_shape=[
            shape((features, 2 * units), bf16),
            shape((rows, units), f32),
            shape((half_rows, features), f32),
            shape((2 * half_rows, features), bf16),
            shape((half_rows, features), bf16),
            shape((half_rows, features), f32),
        ],
        scratch_shapes=[
            buffer((4 * half_rows, features), bf16),
            buffer((4 * half_rows, features), bf16),
            buffer(feed.shape, bf16),
            buffer((4 * half_rows, units), bf16),
            buffer((4 * half_rows, 2 * units), bf16),
            buffer((size, rows, units), bf16),
            buffer((2, half, rows, units), bf16),
            buffer((half_rows, features), bf16),
            buffer((half_rows, features), bf16),
            buffer((half_rows, features), bf16),
            buffer((half_rows, features), bf16),
            buffer((half_rows, features), bf16),
            buffer((2, 384, units), bf16),
            buffer((256, features), f32),
            buffer((half_rows // 256, 256, features), bf16),
            dma((11,)),
            dma((2,)),
            dma((2, half)), dma((2, half)),
            dma((7,)), dma((7,)),
            dma((5,)),
        ],
        compiler_params=pltpu.CompilerParams(collective_id=3, has_side_effects=True, vmem_limit_bytes=62 * 2**20),
        cost_estimate=pl.CostEstimate(flops=6 * 10**10, bytes_accessed=300 * 2**20, transcendentals=0),
        name="middle",
    )(two_slots, cot_slots, feed, hidden_state, cotangent, gain_rows)


def finish_kernel(
    size, tokens_hbm, hidden_hbm, branch_hbm, normed_hbm, weights_hbm, output_hbm, qkv_hbm, att_hbm, feed_grad,
    second_part, far_out, log_ref, gain_rows, attend_shard, cos_ref, sin_ref, rotary_spread, plain_spread,
    tokens_grad, attend_sum, output_sum, feed_sum, gain_sum, out_got,
    branch, grad_ref, back, dq_ref, dk_ref, dv_ref, own_grad, other_grad, crossed, ring_got, output_grad, output_got,
    feed_got, feed_own, terms, got_terms, output_across, gain_parts,
    normed, weights, output_spread, qkv_two, att_ref, tokens, hidden_grad, load_sem,
    ring_send, ring_receive, out_send, out_receive, feed_send, feed_receive, cross_send, cross_receive, across,
    feed_sem, gain_send, gain_receive,
):
    bf16, f32 = jnp.bfloat16, jnp.float32
    places = Places(size)
    half, own = places.half, places.own
    half_rows, features = tokens_hbm.shape
    rows = attend_shard.shape[0]
    width = attend_shard.shape[1]
    span = 4 * HEAD
    diagonal = (own, 3 - places.tensor)
    greet([places.on_ring(1), places.on_ring(-1), places.chip(), places.core(), diagonal])

    def feed_slot(number):
        return feed_grad.at[pl.ds(pl.multiple_of(number * rows, rows), rows)]

    big = 256
    group_order = (2, 3, 0, 1)

    def qkv_load(number):
        lanes = pl.ds(group_order[number] * 4 * LANES, 4 * LANES)
        return pltpu.make_async_copy(qkv_hbm.at[:, lanes], qkv_two.at[number % 2], load_sem.at[number])

    def row_loads(number):
        here = pl.ds(number * big, big)
        return (
            pltpu.make_async_copy(tokens_hbm.at[here], tokens, load_sem.at[4]),
            pltpu.make_async_copy(hidden_hbm.at[here], hidden_grad, load_sem.at[5]),
        )

    fetch = {
        "branch": pltpu.make_async_copy(branch_hbm, branch, load_sem.at[6]),
        "output": pltpu.make_async_copy(output_hbm, output_spread, load_sem.at[7]),
        "att": pltpu.make_async_copy(att_hbm, att_ref, load_sem.at[8]),
        "normed": pltpu.make_async_copy(normed_hbm, normed, load_sem.at[9]),
        "weights": pltpu.make_async_copy(weights_hbm, weights, load_sem.at[10]),
    }
    loads = []

    def load(step, way):
        copy = pltpu.make_async_copy(feed_slot(places.index(step)), feed_own.at[way], feed_sem.at[len(loads)])
        copy.start()
        loads.append(copy)

    load(half, 0)
    out_swap = remote(far_out, out_got, across.at[0], across.at[1], places.chip())
    out_swap.start()
    fetch["branch"].start()
    fetch["output"].start()
    qkv_loads = [qkv_load(number) for number in range(4)]
    qkv_loads[0].start()
    for name in ("att", "normed", "weights"):
        fetch[name].start()

    current = {}

    def feed_partial(number):
        return current["slot"]

    feed = RingScatter(places, feed_partial, feed_got, feed_send, feed_receive)

    def feed_step(hop):
        feed.wait(hop)
        loads[-2].wait()
        loads[-1].wait()
        distance = half - hop
        for way in range(2):
            part = feed_own.at[way]
            here = feed_got.at[way, hop - 1]
            first, last = 0, rows // 16
            if hop == 1:
                first, last = ((0, feed.cut // 16), (feed.cut // 16, last))[way]
                start, count = ((feed.cut, rows - feed.cut), (0, feed.cut))[way]
                here[start : start + count, :] = part[start : start + count, :]

            def tile(number, carry, part=part, here=here):
                place = pl.ds(pl.multiple_of(number * 16, 16), 16)
                here[place, :] = (here[place, :].astype(f32) + part[place, :].astype(f32)).astype(bf16)
                return carry

            lax.fori_loop(first, last, tile, 0)
        feed.start(hop + 1)
        if distance > 1:
            load(distance - 1, 0)
            load(1 - distance, 1)
        else:
            load(0, 0)

    loads[0].wait()
    current["slot"] = feed_own.at[0]
    feed.start(1)
    fetch["branch"].wait()
    fetch["output"].wait()
    fetch["att"].wait()
    token_rows = row_loads(0)
    for copy in token_rows:
        copy.start()

    def back_group(number, target, lane):
        group = group_order[number]
        qkv_loads[number].wait()
        if number < 3:
            qkv_loads[number + 1].start()
        qkv_ref = qkv_two.at[number % 2]
        base = 0
        for part in range(2):
            block = pl.ds(part * half_rows, half_rows)
            value = dot(branch[block, :], output_spread[:, group * 2 * LANES : (group + 1) * 2 * LANES])
            grad_ref[block, :] = value.astype(bf16)
        turned = qkv_ref[:, base + 2 * LANES : base + 3 * LANES].T
        cos, sin = cos_ref[...], sin_ref[...]
        scale = HEAD**-0.5

        def unrot(u):
            return (u * cos - pltpu.roll(u, 64, 1) * sin).astype(bf16)

        key_place = lax.broadcasted_iota(jnp.int32, (QB, QB), 0)
        query_place = lax.broadcasted_iota(jnp.int32, (QB, QB), 1)
        for head in range(2):
            lanes = slice(head * LANES, (head + 1) * LANES)
            att_lane = (2 * group + head) * LANES
            prod = grad_ref[:, lanes].astype(f32) * att_ref[:, att_lane : att_lane + LANES].astype(f32)
            delta = jnp.sum(prod.T, axis=0, keepdims=True)
            for block in reversed(range(LENGTH // QB)):
                first, last = block * QB, (block + 1) * QB
                query = qkv_ref[first:last, base + head * LANES : base + (head + 1) * LANES]
                out_grad = grad_ref[first:last, lanes]
                score = dot(qkv_ref[:last, base + 2 * LANES : base + 3 * LANES], query, ((1,), (1,)))
                prob = jnp.exp2(score * C2 - log_ref[group, head : head + 1, first:last])
                edge = jnp.where(key_place <= query_place, prob[first:], 0.0)
                prob = jnp.concatenate([prob[:first], edge], axis=0) if block else edge
                prob_grad = dot(qkv_ref[:last, base + 3 * LANES : base + 4 * LANES], out_grad, ((1,), (1,)))
                score_grad = (prob * (prob_grad - delta[:, first:last])).astype(bf16)
                key_part = dot(score_grad, query)
                value_part = dot(prob.astype(bf16), out_grad)
                if head == 0 and block == LENGTH // QB - 1:
                    dk_ref[...] = key_part
                    dv_ref[...] = value_part
                else:
                    dk_ref[:last] += key_part
                    dv_ref[:last] += value_part
                dq_ref[first:last, lanes] = dot(turned[:, :last], score_grad).T
        wide = jnp.concatenate(
            [
                unrot(dq_ref[:, :LANES] * scale),
                unrot(dq_ref[:, LANES:] * scale),
                unrot(dk_ref[...] * scale),
                dv_ref[...].astype(bf16),
            ],
            axis=1,
        )
        close_back = dot(wide, rotary_spread[...], ((1,), (1,))).astype(bf16)
        back[:, group * span : (group + 1) * span] = close_back
        if number == 0:
            fetch["normed"].wait()
        for part in range(2):
            block = slice(part * features // 2, (part + 1) * features // 2)
            value = dot(normed[:, block], close_back, ((0,), (0,))).astype(bf16)
            target[part * size // 2 : (part + 1) * size // 2, :, lane : lane + span] = value.reshape(
                size // 2, rows, span
            )

    order = [half]
    for step in range(half - 1, 0, -1):
        order += [step, -step]
    order.append(0)
    crossing = {}

    def cross(group):
        for number, step in enumerate(order):
            slot = places.index(step)
            lanes = pl.ds(group * span, span)
            copy = remote(
                other_grad.at[slot, :, lanes], crossed.at[slot, :, lanes],
                cross_send.at[group, number], cross_receive.at[group, number], places.chip(),
            )
            copy.start()
            crossing[(group, step)] = copy

    back_group(0, other_grad, 0)
    cross(0)
    for copy in feed.sent:
        copy.wait_send()
    load(half - 1, 0)
    load(1 - half, 1)
    back_group(1, other_grad, span)
    cross(1)
    feed_step(1)

    def prepare(step):
        for group in range(2):
            crossing[(group, step)].wait_recv()
        slot = places.index(step)

        def tile(number, carry):
            place = pl.ds(pl.multiple_of(number * 16, 16), 16)
            crossed[slot, place, :] = (crossed[slot, place, :].astype(f32) + own_grad[slot, place, :].astype(f32)).astype(bf16)
            return carry

        lax.fori_loop(0, rows // 16, tile, 0)

    back_group(2, own_grad, 0)
    back_group(3, own_grad, span)

    columns = output_spread.shape[1] // 2 // LANES * HEAD
    heads_width = output_spread.shape[1] // 2
    for side in range(2):
        close = dot(att_ref[:, side * heads_width : (side + 1) * heads_width], plain_spread[...], ((1,), (1,))).astype(bf16)
        for part in range(2):
            block = slice(part * features // 2, (part + 1) * features // 2)
            value = dot(branch[:, block], close, ((0,), (0,))).astype(bf16)
            output_grad[part * size // 2 : (part + 1) * size // 2, :, side * columns : (side + 1) * columns] = value.reshape(
                size // 2, rows, columns
            )
    outputs = RingScatter(places, lambda slot: output_grad.at[slot], output_got, out_send, out_receive)
    outputs.start(1)
    feed_step(2)

    whole = weights.shape[2]
    fetch["weights"].wait()

    def terms_of(block):
        return dot(back[block, :], weights[...].reshape(features, whole), ((1,), (1,)))

    def theirs_tile(number, carry):
        place = (1 - places.side) * half_rows + number * big
        value = terms_of(pl.ds(pl.multiple_of(place, big), big))
        terms[pl.ds(pl.multiple_of(number * big, big), big), :] = value.astype(bf16)
        return carry

    lax.fori_loop(0, half_rows // big, theirs_tile, 0)
    terms_swap = remote(terms, got_terms, across.at[2], across.at[3], places.core())
    terms_swap.start()
    prepare(half)
    attend = RingScatter(places, lambda slot: crossed.at[slot], ring_got, ring_send, ring_receive)
    attend.start(1)
    outputs.wait(1)
    outputs.add(1)
    outputs.start(2)
    terms_swap.wait()

    for number in range(half_rows // big):
        for copy in token_rows:
            copy.wait()
        here = slice(number * big, (number + 1) * big)
        place = places.side * half_rows + number * big
        value = terms_of(pl.ds(pl.multiple_of(place, big), big)) + got_terms[here, :].astype(f32)
        values = tokens[...].astype(f32)
        inverse = lax.rsqrt(jnp.mean(values * values, axis=1, keepdims=True) + norm_eps)
        scaled = value * gain_rows[0:1, :]
        inner = jnp.mean(scaled * values, axis=1, keepdims=True)
        result = hidden_grad[...] + inverse * scaled - values * (inverse * inverse * inverse) * inner
        tokens_grad[here, :] = result.astype(bf16)
        if number < half_rows // big - 1:
            token_rows = row_loads(number + 1)
            for copy in token_rows:
                copy.start()
    prepare(half - 1)
    prepare(1 - half)
    attend.wait(1)
    attend.add(1)
    attend.start(2)
    for hop in range(2, half + 1):
        outputs.wait(hop)
        if hop < half:
            outputs.add(hop)
            outputs.start(hop + 1)
        if hop > 2 and hop < half:
            feed_step(hop)
        if hop < half:
            prepare(half - hop)
            prepare(hop - half)
            attend.wait(hop)
            attend.add(hop)
            attend.start(hop + 1)
    prepare(0)

    def output_total(place):
        return outputs.total(place)

    def output_tile(number, carry):
        place = pl.ds(pl.multiple_of(number * 16, 16), 16)
        value = output_total(place)
        output_sum[place, :] = value[:, :columns]
        output_across[0, place, :] = value[:, columns:]
        return carry

    lax.fori_loop(0, rows // 16, output_tile, 0)
    output_swap = remote(output_across.at[0], output_across.at[1], across.at[4], across.at[5], places.chip())
    output_swap.start()
    attend.wait(half)

    def attend_tile(number, carry):
        place = pl.ds(pl.multiple_of(number * 16, 16), 16)
        value = attend.total(place)
        attend_sum[place, :] = value
        gain = jnp.sum(value * attend_shard[place, :].astype(f32), axis=1, keepdims=True)
        lane = lax.broadcasted_iota(jnp.int32, (16, LANES), 1)
        gain_parts[0, place, :] = jnp.where(lane == 0, gain, 0.0)
        return carry

    lax.fori_loop(0, rows // 16, attend_tile, 0)
    feed.wait(half)
    loads[-1].wait()
    second = pltpu.make_async_copy(second_part, feed_own.at[1], load_sem.at[11])
    second.start()
    second.wait()

    def feed_tile(number, carry):
        place = pl.ds(pl.multiple_of(number * 16, 16), 16)
        value = (
            feed_own[0, place, :].astype(f32)
            + feed_got[0, half - 1, place, :].astype(f32)
            + feed_got[1, half - 1, place, :].astype(f32)
        )
        feed_sum[place, :] = value
        gain = jnp.sum(value * feed_own[1, place, :].astype(f32), axis=1, keepdims=True)
        lane = lax.broadcasted_iota(jnp.int32, (16, LANES), 1)
        gain_parts[0, place, :] += jnp.where(lane == 1, gain, 0.0)
        return carry

    lax.fori_loop(0, rows // 16, feed_tile, 0)
    gain_copies = []
    for number, device in enumerate((places.core(), places.chip(), diagonal)):
        copy = remote(gain_parts.at[0], gain_parts.at[1 + number], gain_send.at[number], gain_receive.at[number], device)
        copy.start()
        gain_copies.append(copy)
    output_swap.wait()
    output_sum[...] += output_across[1]
    for copy in gain_copies:
        copy.wait()
    gain_sum[...] = (gain_parts[0] + gain_parts[1]) + (gain_parts[2] + gain_parts[3])
    for copy in crossing.values():
        copy.wait_send()
    out_swap.wait()
    outputs.finish()
    attend.finish()
    for copy in feed.sent[2:]:
        copy.wait_send()


def finish(
    size, tokens, hidden_grad, branch, normed, weights, output_spread, qkv, att, logs, gain_rows, feed_grad,
    attend_shard, second_part, far_out,
):
    half_rows, features = tokens.shape
    rows, width = attend_shard.shape
    columns = output_spread.shape[1] // 2 // LANES * HEAD
    feed_width = feed_grad.shape[1]
    vmem = pl.BlockSpec(memory_space=pltpu.VMEM)
    anywhere = pl.BlockSpec(memory_space=pl.ANY)
    dma = pltpu.SemaphoreType.DMA
    half = size // 2
    bf16, f32 = jnp.bfloat16, jnp.float32
    cos, sin = rope_tables()
    shape = jax.ShapeDtypeStruct
    buffer = pltpu.VMEM
    return pl.pallas_call(
        functools.partial(finish_kernel, size),
        in_specs=[anywhere] * 11 + [vmem] * 7,
        out_specs=[vmem] * 5 + [anywhere],
        out_shape=[
            shape((half_rows, features), bf16),
            shape((rows, width), f32),
            shape((rows, columns), f32),
            shape((rows, feed_width), f32),
            shape((rows, LANES), f32),
            shape((half_rows, features), bf16),
        ],
        scratch_shapes=[
            buffer((LENGTH, features), bf16),
            buffer((LENGTH, 2 * LANES), bf16),
            buffer((LENGTH, 2 * width), bf16),
            buffer((LENGTH, 2 * LANES), f32),
            buffer((LENGTH, LANES), f32),
            buffer((LENGTH, LANES), f32),
            buffer((size, rows, width), bf16),
            buffer((size, rows, width), bf16),
            buffer((size, rows, width), bf16),
            buffer((2, half, rows, width), bf16),
            buffer((size, rows, 2 * columns), bf16),
            buffer((2, half, rows, 2 * columns), bf16),
            buffer((2, half, rows, feed_width), bf16),
            buffer((2, rows, feed_width), bf16),
            buffer((half_rows, features), bf16),
            buffer((half_rows, features), bf16),
            buffer((2, rows, columns), f32),
            buffer((4, rows, LANES), f32),
            buffer((LENGTH, features), bf16),
            buffer(weights.shape, bf16),
            buffer(output_spread.shape, bf16),
            buffer((2, LENGTH, 4 * LANES), bf16),
            buffer(att.shape, bf16),
            buffer((256, features), bf16),
            buffer((256, features), f32),
            dma((12,)),
            dma((2, half)), dma((2, half)),
            dma((2, half)), dma((2, half)),
            dma((2, half)), dma((2, half)),
            dma((2, size)), dma((2, size)),
            dma((6,)),
            dma((2 * half,)),
            dma((3,)), dma((3,)),
        ],
        compiler_params=pltpu.CompilerParams(collective_id=2, has_side_effects=True, vmem_limit_bytes=62 * 2**20),
        cost_estimate=pl.CostEstimate(flops=3 * 10**10, bytes_accessed=300 * 2**20, transcendentals=0),
        name="finish",
    )(
        tokens, hidden_grad, branch, normed, weights, output_spread, qkv, att, feed_grad, second_part, far_out, logs,
        gain_rows, attend_shard, jnp.asarray(cos), jnp.asarray(sin),
        jnp.asarray(spread(4, (1, 1, 1, 0)), bf16), jnp.asarray(spread(4, (0,) * 4), bf16),
    )


def local(
    dp_size,
    tokens,
    first_gain,
    query_weight,
    key_weight,
    value_weight,
    output_weight,
    second_gain,
    gate_weight,
    up_weight,
    down_weight,
    cotangent,
):
    bf16, f32 = jnp.bfloat16, jnp.float32

    groups = key_weight.shape[1] // HEAD
    packs = []
    for group in range(groups):
        packs.append(query_weight[:, group * 2 * HEAD : (group + 1) * 2 * HEAD])
        packs.append(key_weight[:, group * HEAD : (group + 1) * HEAD])
        packs.append(value_weight[:, group * HEAD : (group + 1) * HEAD])
    attend_shard = jnp.concatenate(packs, axis=1)
    output_shard = output_weight.T
    feed_shard = jnp.concatenate([gate_weight, up_weight, down_weight.T], axis=1)
    hidden_units = gate_weight.shape[1]

    lanes = LANES * pl.cdiv(first_gain.shape[0], LANES)
    both_gains = jnp.stack([first_gain, second_gain]).astype(f32)
    both_gains = jnp.pad(both_gains, ((0, 6), (0, lanes - first_gain.shape[0])))
    gate_up_shard = feed_shard[:, : 2 * hidden_units]
    (normed, weights, output_spread, qkv, attended, logs, hidden_state, two_slots, cot_slots, feed, gain_rows) = begin(
        dp_size, tokens, cotangent, both_gains, attend_shard, output_shard, feed_shard
    )
    gate_up_grad, down_sum, hidden_grad, branch, far_out, near_out = middle(
        dp_size, two_slots, cot_slots, feed, hidden_state, cotangent, gain_rows
    )
    tokens_grad, attend_sum, output_sum, gate_up_sum, gain_sums, out_got = finish(
        dp_size, tokens, hidden_grad, branch, normed, weights, output_spread, qkv, attended, logs, gain_rows,
        gate_up_grad, attend_shard, gate_up_shard, far_out,
    )
    layer_out = (near_out + out_got.astype(f32)).astype(bf16)

    block = 4 * HEAD
    query_grad = jnp.concatenate(
        [attend_sum[:, g * block : g * block + 2 * HEAD] for g in range(groups)], axis=1
    )
    key_grad = jnp.concatenate(
        [attend_sum[:, g * block + 2 * HEAD : g * block + 3 * HEAD] for g in range(groups)], axis=1
    )
    value_grad = jnp.concatenate(
        [attend_sum[:, g * block + 3 * HEAD : (g + 1) * block] for g in range(groups)], axis=1
    )
    return (
        layer_out,
        tokens_grad,
        gain_sums[:, 0] / first_gain.astype(f32),
        query_grad,
        key_grad,
        value_grad,
        output_sum.T,
        gain_sums[:, 1] / second_gain.astype(f32),
        gate_up_sum[:, :hidden_units],
        gate_up_sum[:, hidden_units:],
        down_sum.T,
    )


def solution(mesh):
    in_specs = (
        P(("dp", "tensor"), None),
        P("dp"),
        P("dp", "tensor"),
        P("dp", "tensor"),
        P("dp", "tensor"),
        P("tensor", "dp"),
        P("dp"),
        P("dp", "tensor"),
        P("dp", "tensor"),
        P("tensor", "dp"),
        P(("dp", "tensor"), None),
    )
    out_specs = (
        P(("dp", "tensor"), None),
        P(("dp", "tensor"), None),
        P("dp"),
        P("dp", "tensor"),
        P("dp", "tensor"),
        P("dp", "tensor"),
        P("tensor", "dp"),
        P("dp"),
        P("dp", "tensor"),
        P("dp", "tensor"),
        P("tensor", "dp"),
    )
    body = functools.partial(local, mesh.shape["dp"])
    return jax.shard_map(body, mesh=mesh, in_specs=in_specs, out_specs=out_specs, check_vma=False)
```

```python
import functools

import jax
import jax.numpy as jnp
import numpy as np
from jax import lax
from jax.experimental import pallas as pl
from jax.experimental.pallas import tpu as pltpu
from jax.sharding import PartitionSpec as P

HEAD = 96
LENGTH = 1024
LANES = 128
QB = 256
norm_eps = 1e-05
rope_base = 100000.0


def rope_tables():
    half = HEAD // 2
    freq = rope_base ** (np.arange(half, dtype=np.float64) * (-2.0 / HEAD))
    turned = np.arange(LENGTH, dtype=np.float64)[:, None] * freq[None, :]
    cos = np.zeros((LENGTH, LANES), np.float32); sin = np.zeros((LENGTH, LANES), np.float32)
    cos[:, :half] = np.cos(turned); cos[:, 64:64+half] = np.cos(turned)
    sin[:, :half] = -np.sin(turned); sin[:, 64:64+half] = np.sin(turned)
    return cos, sin

def spread(heads, rotary):
    e = np.zeros((heads * HEAD, heads * LANES), np.float32)
    for h in range(heads):
        for i in range(HEAD):
            lane = i if (not rotary[h] or i < 48) else i + 16
            e[h * HEAD + i, h * LANES + lane] = 1
    return e

def dot(a, b, dims=((1,), (0,))):
    return lax.dot_general(a, b, (dims, ((), ())), preferred_element_type=jnp.float32)

C2 = float(HEAD ** -0.5 * np.log2(np.e))


MESH = pl.DeviceIdType.MESH


class Places:
    def __init__(self, size):
        self.size = size
        self.half = size // 2
        self.own = lax.axis_index("dp")
        self.tensor = lax.axis_index("tensor")
        self.side = self.tensor % 2
        odd = self.own % 2
        self.place = (1 - odd) * (self.own // 2) + odd * (size - 1 - self.own // 2)

    def index(self, step):
        place = (self.place + step + self.size) % self.size
        late = place // self.half
        return (1 - late) * 2 * place + late * (2 * (self.size - 1 - place) + 1)

    def on_ring(self, step):
        return (self.index(step), self.tensor)

    def peer(self, step):
        return ((self.own + step + self.size) % self.size, self.tensor)

    def chip(self):
        return (self.own, (self.tensor + 2) % 4)

    def core(self):
        return (self.own, self.tensor + 1 - 2 * self.side)


def remote(source, target, send, receive, device):
    return pltpu.make_async_remote_copy(
        src_ref=source,
        dst_ref=target,
        send_sem=send,
        recv_sem=receive,
        device_id=device,
        device_id_type=MESH,
    )


def greet(devices):
    barrier = pltpu.get_barrier_semaphore()
    for device in devices:
        pl.semaphore_signal(barrier, inc=1, device_id=device, device_id_type=MESH)
    pl.semaphore_wait(barrier, len(devices))


class RingGather:
    def __init__(self, places, slots, send, receive):
        self.places, self.slots, self.send, self.receive = places, slots, send, receive
        self.cut = slots.shape[1] // 32 * 16
        self.sent = []

    def start(self, hop, source=None):
        places, half = self.places, self.places.half
        for way, (step, device) in enumerate(
            ((1 - hop, places.on_ring(1)), (hop - 1, places.on_ring(-1)))
        ):
            slot = places.index(step)
            rows = pl.ds(0, self.slots.shape[1])
            if hop == half:
                rows = (pl.ds(0, self.cut), pl.ds(self.cut, self.slots.shape[1] - self.cut))[way]
            view = self.slots.at[slot, rows]
            copy = remote(
                view if source is None else source.at[rows],
                view,
                self.send.at[way, hop - 1],
                self.receive.at[way, hop - 1],
                device,
            )
            copy.start()
            self.sent.append(copy)

    def wait(self, hop):
        self.sent[2 * hop - 2].wait_recv()
        self.sent[2 * hop - 1].wait_recv()

    def step(self, hop):
        self.wait(hop)
        if hop < self.places.half:
            self.start(hop + 1)

    def finish(self):
        for copy in self.sent:
            copy.wait_send()


class Parts:
    def __init__(self, rings):
        self.rings = rings

    def start(self, hop, sources=None):
        for number, ring in enumerate(self.rings):
            ring.start(hop) if sources is None else ring.start(hop, sources[number])

    def wait(self, hop):
        for ring in self.rings:
            ring.wait(hop)

    def step(self, hop):
        for ring in self.rings:
            ring.step(hop)

    def finish(self):
        for ring in self.rings:
            ring.finish()


class Spread:
    def __init__(self, places, own, slots, send, receive):
        self.places, self.slots, self.send, self.receive = places, slots, send, receive
        near, far = slots.at[places.side], slots.at[2 + places.side]
        self.chip = remote(own, far, send.at[0], receive.at[0], places.chip())
        self.core = remote(own, near, send.at[1], receive.at[1], places.core())
        self.far = far

    def start(self):
        self.chip.start()
        self.core.start()

    def pass_on(self):
        self.chip.wait_recv()
        self.last = remote(self.far, self.far, self.send.at[2], self.receive.at[2], self.places.core())
        self.last.start()

    def finish(self):
        self.chip.wait_send()
        self.core.wait()
        self.last.wait()


def begin_kernel(
    size, tokens, cotangent, gains, attend_shard, output_shard, gate_shard, up_shard, cos_ref, sin_ref, rotary_spread,
    plain_spread,
    normed, weights, output_spread, qkv_ref, att_ref, log_ref, hidden, two_slots, cot_slots, feed, gain_rows,
    gain_slots, output_both, terms, received, two_own, gain_send, gain_receive, ring_send, ring_receive,
    pass_send, pass_receive, out_send, out_receive, feed_send, feed_receive, across, two_send, two_receive,
    cot_send, cot_receive, local_sem,
):
    bf16, f32 = jnp.bfloat16, jnp.float32
    places = Places(size)
    half, own = places.half, places.own
    half_rows = tokens.shape[0]
    columns = output_shard.shape[1]
    width = attend_shard.shape[1]
    units = gate_shard.shape[1]
    greet([places.peer(step) for step in range(1, size)] + [places.chip(), places.core()])

    def own_side(slot):
        return weights.at[slot, :, pl.ds(0, width)]

    def other_side(slot):
        return weights.at[slot, :, pl.ds(width, width)]

    def lanes_of(number, count):
        return pl.ds(number * count, count)

    ring = Parts([
        RingGather(places, weights.at[:, :, lanes_of(number, width // 2)], ring_send.at[number], ring_receive.at[number])
        for number in range(2)
    ])
    ring.start(1, [attend_shard.at[:, lanes_of(number, width // 2)] for number in range(2)])
    passed = []

    def hand_on(step, number, source=None):
        slot = places.index(step)
        copy = remote(
            own_side(slot) if source is None else source, other_side(slot),
            pass_send.at[number], pass_receive.at[number], places.chip(),
        )
        copy.start()
        passed.append(copy)

    hand_on(0, 0, attend_shard)
    output_pass = remote(
        output_shard, output_both.at[own, :, pl.ds(columns, columns)], across.at[0], across.at[1], places.chip()
    )
    output_pass.start()
    gain_copies = []
    for step in range(1, size):
        copy = remote(gains, gain_slots.at[own], gain_send.at[step - 1], gain_receive.at[step - 1], places.peer(step))
        copy.start()
        gain_copies.append(copy)
    near = cot_slots.at[places.side]
    keep = [
        pltpu.make_async_copy(attend_shard, own_side(own), local_sem.at[0]),
        pltpu.make_async_copy(output_shard, output_both.at[own, :, pl.ds(0, columns)], local_sem.at[1]),
        pltpu.make_async_copy(gate_shard, feed.at[own, :, lanes_of(0, units)], local_sem.at[2]),
        pltpu.make_async_copy(up_shard, feed.at[own, :, lanes_of(1, units)], local_sem.at[5]),
        pltpu.make_async_copy(cotangent, near, local_sem.at[3]),
    ]
    for copy in keep:
        copy.start()
    gain_slots[own] = gains[...]

    def ring_step(hop):
        ring.step(hop)
        if hop < half:
            hand_on(-hop, 2 * hop - 1)
            hand_on(hop, 2 * hop)
        else:
            hand_on(half, size - 1)

    for copy in gain_copies:
        copy.wait_recv()
    part = tokens.shape[1] // size
    for index in range(size):
        gain_rows[:, index * part : (index + 1) * part] = gain_slots[index][:, :part]
    tile = 64
    mine_start = places.side * half_rows

    def norm_tile(number, carry):
        rows = pl.ds(pl.multiple_of(number * tile, tile), tile)
        values = tokens[rows, :].astype(f32)
        inverse = lax.rsqrt(jnp.mean(values * values, axis=1, keepdims=True) + norm_eps)
        target = pl.ds(pl.multiple_of(mine_start + number * tile, tile), tile)
        normed[target, :] = (values * inverse * gain_rows[0:1, :]).astype(bf16)
        return carry

    tiles = half_rows // tile
    ring_step(1)
    lax.fori_loop(0, tiles // 2, norm_tile, 0)
    ring_step(2)
    lax.fori_loop(tiles // 2, tiles, norm_tile, 0)
    mine = pl.ds(pl.multiple_of(mine_start, half_rows), half_rows)
    swap = remote(normed.at[mine], normed.at[mine], across.at[2], across.at[3], places.core())
    swap.start()
    for hop in range(3, half):
        ring_step(hop)
    outputs = Parts([
        RingGather(places, output_both.at[:, :, lanes_of(number, columns)], out_send.at[number], out_receive.at[number])
        for number in range(2)
    ])
    output_pass.wait()
    for copy in keep:
        copy.wait()
    outputs.start(1)
    ring_step(half)
    swap.wait()

    def attend(group):
        lanes = pl.ds(group * 4 * HEAD, 4 * HEAD)
        weight = weights[:, :, lanes].reshape(tokens.shape[1], 4 * HEAD)
        weight = dot(weight, rotary_spread[...]).astype(bf16)
        rows = dot(normed[...], weight)
        cos, sin = cos_ref[...], sin_ref[...]
        base = group * 4 * LANES

        def rot(u):
            return (u * cos + pltpu.roll(u, 64, 1) * sin).astype(bf16)

        for head in range(3):
            lane = head * LANES
            qkv_ref[:, base + lane : base + lane + LANES] = rot(rows[:, lane : lane + LANES])
        qkv_ref[:, base + 3 * LANES : base + 4 * LANES] = rows[:, 3 * LANES :].astype(bf16)
        turned = qkv_ref[:, base + 3 * LANES : base + 4 * LANES].T
        key_place = lax.broadcasted_iota(jnp.int32, (QB, QB), 0)
        query_place = lax.broadcasted_iota(jnp.int32, (QB, QB), 1)
        for head in range(2):
            for block in range(LENGTH // QB):
                first, last = block * QB, (block + 1) * QB
                query = qkv_ref[first:last, base + head * LANES : base + (head + 1) * LANES]
                key = qkv_ref[:last, base + 2 * LANES : base + 3 * LANES]
                score = dot(key, query, ((1,), (1,)))
                edge = jnp.where(key_place <= query_place, score[first:], -1e30)
                score = jnp.concatenate([score[:first], edge], axis=0) if block else edge
                top = jnp.max(score, axis=0, keepdims=True)
                weight = jnp.exp2((score - top) * C2)
                total = jnp.sum(weight, axis=0, keepdims=True)
                result = dot(turned[:, :last], weight.astype(bf16)) / total
                lane = group * 2 * LANES + head * LANES
                att_ref[first:last, lane : lane + LANES] = result.T.astype(bf16)
                log_ref[group, head, pl.ds(first, QB)] = (top * C2 + jnp.log2(total))[0]

    attend(0)
    outputs.step(1)
    attend(1)
    for hop in range(2, half):
        outputs.step(hop)
    ring_feed = Parts([
        RingGather(places, feed.at[:, :, lanes_of(number, units)], feed_send.at[number], feed_receive.at[number])
        for number in range(2)
    ])
    ring_feed.start(1, [gate_shard, up_shard])
    outputs.step(half)
    for copy in passed:
        copy.wait()
    cot = Spread(places, cotangent, cot_slots, cot_send, cot_receive)
    cot.start()
    attend(2)
    attend(3)
    ring_feed.step(1)

    heads_width = columns // HEAD * LANES
    out_rows = output_shard.shape[0]

    def spread_slot(number, carry):
        rows = pl.ds(pl.multiple_of(number * out_rows, out_rows), out_rows)
        for side in range(2):
            value = dot(output_both[number, :, side * columns : (side + 1) * columns], plain_spread[...])
            output_spread[rows, side * heads_width : (side + 1) * heads_width] = value.astype(bf16)
        return carry

    lax.fori_loop(0, size, spread_slot, 0)
    big = 256

    def theirs_tile(number, carry):
        start = (1 - places.side) * half_rows + number * big
        rows = pl.ds(pl.multiple_of(start, big), big)
        value = dot(att_ref[rows, :], output_spread[...], ((1,), (1,)))
        terms[pl.ds(pl.multiple_of(number * big, big), big), :] = value.astype(bf16)
        return carry

    lax.fori_loop(0, half_rows // big, theirs_tile, 0)
    sum_swap = remote(terms, received, across.at[4], across.at[5], places.core())
    sum_swap.start()

    def mine_tile(number, carry):
        rows = pl.ds(pl.multiple_of(mine_start + number * big, big), big)
        value = dot(att_ref[rows, :], output_spread[...], ((1,), (1,)))
        here = pl.ds(pl.multiple_of(number * big, big), big)
        hidden[here, :] = value + tokens[here, :].astype(f32)
        return carry

    lax.fori_loop(0, half_rows // big, mine_tile, 0)
    sum_swap.wait()

    def second_tile(number, carry):
        rows = pl.ds(pl.multiple_of(number * tile, tile), tile)
        values = hidden[rows, :] + received[rows, :].astype(f32)
        hidden[rows, :] = values
        inverse = lax.rsqrt(jnp.mean(values * values, axis=1, keepdims=True) + norm_eps)
        two_own[rows, :] = (values * inverse * gain_rows[1:2, :]).astype(bf16)
        return carry

    lax.fori_loop(0, half_rows // tile, second_tile, 0)
    two = Spread(places, two_own, two_slots, two_send, two_receive)
    two.start()
    keep_two = pltpu.make_async_copy(two_own, two_slots.at[places.side], local_sem.at[4])
    keep_two.start()
    ring_feed.step(2)
    cot.pass_on()
    for hop in range(3, half + 1):
        ring_feed.step(hop)
    two.pass_on()
    cot.finish()
    two.finish()
    keep_two.wait()
    for copy in gain_copies:
        copy.wait_send()
    ring.finish()
    outputs.finish()
    ring_feed.finish()


def begin(size, tokens, cotangent, gains, attend_shard, output_shard, gate_shard, up_shard):
    half_rows, features = tokens.shape
    rows, width = attend_shard.shape
    columns = output_shard.shape[1]
    heads_width = columns // HEAD * LANES
    groups = 2 * width // (4 * HEAD)
    vmem = pl.BlockSpec(memory_space=pltpu.VMEM)
    anywhere = pl.BlockSpec(memory_space=pl.ANY)
    dma = pltpu.SemaphoreType.DMA
    half = size // 2
    bf16, f32 = jnp.bfloat16, jnp.float32
    cos, sin = rope_tables()
    shape = jax.ShapeDtypeStruct
    return pl.pallas_call(
        functools.partial(begin_kernel, size),
        in_specs=[vmem] * 11,
        out_specs=[vmem, vmem, vmem, vmem, vmem, vmem, vmem, anywhere, anywhere, anywhere, vmem],
        out_shape=[
            shape((2 * half_rows, features), bf16),
            shape((size, rows, 2 * width), bf16),
            shape((features, 2 * heads_width), bf16),
            shape((LENGTH, groups * 4 * LANES), bf16),
            shape((LENGTH, groups * 2 * LANES), bf16),
            shape((groups, 2, LENGTH), f32),
            shape((half_rows, features), f32),
            shape((4, half_rows, features), bf16),
            shape((4, half_rows, features), bf16),
            shape((size, rows, 2 * gate_shard.shape[1]), bf16),
            shape((8, features), f32),
        ],
        scratch_shapes=[
            pltpu.VMEM((size,) + gains.shape, f32),
            pltpu.VMEM((size, rows, 2 * columns), bf16),
            pltpu.VMEM((half_rows, features), bf16),
            pltpu.VMEM((half_rows, features), bf16),
            pltpu.VMEM((half_rows, features), bf16),
            dma((size - 1,)), dma((size - 1,)),
            dma((2, 2, half)), dma((2, 2, half)),
            dma((size,)), dma((size,)),
            dma((2, 2, half)), dma((2, 2, half)),
            dma((2, 2, half)), dma((2, 2, half)),
            dma((6,)),
            dma((3,)), dma((3,)),
            dma((3,)), dma((3,)),
            dma((6,)),
        ],
        compiler_params=pltpu.CompilerParams(collective_id=1, has_side_effects=True, vmem_limit_bytes=56 * 2**20),
        cost_estimate=pl.CostEstimate(flops=10**10, bytes_accessed=400 * 2**20, transcendentals=0),
        name="begin",
    )(
        tokens, cotangent, gains, attend_shard, output_shard, gate_shard, up_shard, jnp.asarray(cos), jnp.asarray(sin),
        jnp.asarray(spread(4, (1, 1, 1, 0)), bf16), jnp.asarray(spread(columns // HEAD, (0,) * 4), bf16),
    )


class RingScatter:
    def __init__(self, places, partial, received, send, receive):
        self.places, self.partial, self.received = places, partial, received
        self.send, self.receive = send, receive
        self.rows = received.shape[2]
        self.cut = self.rows // 32 * 16
        self.sent = []

    def start(self, hop):
        places = self.places
        for way in range(2):
            rows = pl.ds(0, self.rows)
            if hop == 1:
                rows = (pl.ds(0, self.cut), pl.ds(self.cut, self.rows - self.cut))[way]
                source = self.partial(places.index(places.half)).at[rows]
            else:
                source = self.received.at[way, hop - 2]
            copy = remote(
                source,
                self.received.at[way, hop - 1, rows],
                self.send.at[way, hop - 1],
                self.receive.at[way, hop - 1],
                places.on_ring(1 - 2 * way),
            )
            copy.start()
            self.sent.append(copy)

    def wait(self, hop):
        self.sent[2 * hop - 2].wait_recv()
        self.sent[2 * hop - 1].wait_recv()

    def add(self, hop):
        distance = self.places.half - hop
        for way in range(2):
            own = self.partial(self.places.index(distance * (1 - 2 * way)))
            here = self.received.at[way, hop - 1]
            first, last = 0, self.rows // 16
            if hop == 1:
                first, last = ((0, self.cut // 16), (self.cut // 16, last))[way]
                start, count = ((self.cut, self.rows - self.cut), (0, self.cut))[way]
                here[start : start + count, :] = own[start : start + count, :]

            def tile(number, carry, own=own, here=here):
                rows = pl.ds(pl.multiple_of(number * 16, 16), 16)
                here[rows, :] = (here[rows, :].astype(jnp.float32) + own[rows, :].astype(jnp.float32)).astype(jnp.bfloat16)
                return carry

            lax.fori_loop(first, last, tile, 0)

    def step(self, hop):
        self.wait(hop)
        self.add(hop)
        self.start(hop + 1)

    def total(self, rows):
        half = self.places.half
        own = self.partial(self.places.index(0))
        return (
            own[rows, :].astype(jnp.float32)
            + self.received[0, half - 1, rows, :].astype(jnp.float32)
            + self.received[1, half - 1, rows, :].astype(jnp.float32)
        )

    def finish(self):
        for copy in self.sent:
            copy.wait_send()


def middle_kernel(
    size, two_slots, cot_slots, feed, down_shard, hidden_hbm, gain_rows,
    up_grad, gate_sum, down_sum, hidden_grad, branch, far_out, near_out, out_got,
    two, cot, weights, down, inner, grads, down_grad, gate_grad, ring_got, outgoing, far_part, core_far, core_near,
    chip_got, stage, hidden, load_sem, stage_sem, weight_send, weight_receive, down_send, down_receive, gate_send,
    gate_receive, send_sem, receive_sem, store_sem, credit,
):
    bf16, f32 = jnp.bfloat16, jnp.float32
    places = Places(size)
    half = places.half
    half_rows, features = hidden_hbm.shape
    rows = feed.shape[1]
    units = inner.shape[1]
    lane_half = units // 2
    greet([places.on_ring(1), places.on_ring(-1), places.chip(), places.core()])

    def lanes_of(number):
        return pl.ds(number * lane_half, lane_half)

    gather = Parts([
        RingGather(places, down.at[:, :, lanes_of(number)], weight_send.at[number], weight_receive.at[number])
        for number in range(2)
    ])
    gather.start(1, [down_shard.at[:, lanes_of(number)] for number in range(2)])

    order = (2, 3, 0, 1)
    fetch = [pltpu.make_async_copy(feed, weights, load_sem.at[0])]
    for number, slot in enumerate(order):
        here = pl.ds(slot * half_rows, half_rows)
        fetch.append(pltpu.make_async_copy(two_slots.at[slot], two.at[here], load_sem.at[1 + number]))
    fetch.append(pltpu.make_async_copy(down_shard, down.at[places.own], load_sem.at[5]))
    for number, slot in enumerate(order):
        here = pl.ds(slot * half_rows, half_rows)
        fetch.append(pltpu.make_async_copy(cot_slots.at[slot], cot.at[here], load_sem.at[6 + number]))
    for copy in fetch:
        copy.start()
    fetch[0].wait()
    block = 512

    def weight_lanes(start, count):
        return weights[:, :, pl.ds(start, count)].reshape(features, count)

    def forward(slot):
        here = pl.ds(slot * half_rows, half_rows)

        def column(number, carry):
            lane = pl.multiple_of(number * block, block)
            gate = dot(two[here, :], weight_lanes(lane, block))
            up = dot(two[here, :], weight_lanes(pl.multiple_of(units + lane, block), block))
            sigmoid = 1.0 / (1.0 + jnp.exp(-gate))
            silu = gate * sigmoid
            inner[here, pl.ds(lane, block)] = (silu * up).astype(bf16)
            grads[here, pl.ds(lane, block)] = (up * (sigmoid + silu * (1.0 - sigmoid))).astype(bf16)
            grads[here, pl.ds(pl.multiple_of(units + lane, block), block)] = silu.astype(bf16)
            return carry

        lax.fori_loop(0, units // block, column, 0)

    def backward(slot):
        here = pl.ds(slot * half_rows, half_rows)

        def column(number, carry):
            lane = pl.multiple_of(number * block, block)
            weight = down[:, :, pl.ds(lane, block)].reshape(features, block)
            inner_grad = dot(cot[here, :], weight)
            for side in range(2):
                place = pl.ds(pl.multiple_of(side * units + lane, block), block)
                grads[here, place] = (inner_grad * grads[here, place].astype(f32)).astype(bf16)
            return carry

        lax.fori_loop(0, units // block, column, 0)

    big = 256
    mine_start = places.side * half_rows
    theirs_start = (1 - places.side) * half_rows
    both_rows = 2 * half_rows

    def two_terms(place):
        return dot(grads[place, :], weights[...].reshape(features, 2 * units), ((1,), (1,)))

    def out_terms(place):
        return dot(inner[place, :], down[...].reshape(features, units), ((1,), (1,)))

    def terms_to(target, start, terms):
        def tile(number, carry):
            value = terms(pl.ds(pl.multiple_of(start + number * big, big), big))
            target[pl.ds(pl.multiple_of(number * big, big), big), :] = value.astype(bf16)
            return carry

        lax.fori_loop(0, half_rows // big, tile, 0)

    def add_to(target, other):
        def tile(number, carry):
            place = pl.ds(pl.multiple_of(number * 32, 32), 32)
            target[place, :] = (target[place, :].astype(f32) + other[place, :].astype(f32)).astype(bf16)
            return carry

        lax.fori_loop(0, half_rows // 32, tile, 0)

    for number, slot in enumerate(order):
        fetch[1 + number].wait()
        forward(slot)
        if number + 1 < half:
            gather.step(number + 1)
    for copy in fetch[5:]:
        copy.wait()
    for hop in range(5, half):
        gather.step(hop)

    span = 384
    per_span = span // rows

    def down_tile(number, carry):
        lanes = pl.ds(pl.multiple_of(number * span, span), span)
        value = dot(cot[:, lanes], inner[...], ((0,), (0,))).astype(bf16)
        down_grad[pl.ds(number * per_span, per_span)] = value.reshape(per_span, rows, units)
        return carry

    spans = features // span
    lax.fori_loop(0, spans, down_tile, 0)
    gather.step(half)

    def scatter_of(array, send, receive):
        return Parts([
            RingScatter(
                places,
                lambda slot, number=number: array.at[slot, :, lanes_of(number)],
                ring_got.at[:, :, :, lanes_of(number)],
                send.at[number],
                receive.at[number],
            )
            for number in range(2)
        ])

    ring = scatter_of(down_grad, down_send, down_receive)
    ring.start(1)
    for slot in order[:2]:
        backward(slot)
    terms_to(outgoing, both_rows + theirs_start, two_terms)
    far_swap = remote(outgoing, core_far, send_sem.at[0], receive_sem.at[0], places.core())
    far_swap.start()
    ring.step(1)
    terms_to(far_part, both_rows + mine_start, two_terms)
    far_swap.wait()
    add_to(far_part, core_far)
    chip_swap = remote(far_part, chip_got, send_sem.at[1], receive_sem.at[1], places.chip())
    chip_swap.start()
    for slot in order[2:]:
        backward(slot)
    ring.step(2)

    def gate_tile(number, carry):
        lanes = pl.ds(pl.multiple_of(number * span, span), span)
        value = dot(two[:, lanes], grads[:, :units], ((0,), (0,))).astype(bf16)
        gate_grad[pl.ds(number * per_span, per_span)] = value.reshape(per_span, rows, units)
        return carry

    lax.fori_loop(0, spans, gate_tile, 0)
    for hop in range(3, half):
        ring.step(hop)
    terms_to(outgoing, theirs_start, two_terms)
    near_swap = remote(outgoing, core_near, send_sem.at[2], receive_sem.at[2], places.core())
    near_swap.start()
    ring.wait(half)

    def total_to(target, sums):
        def tile(number, carry):
            place = pl.ds(pl.multiple_of(number * 16, 16), 16)
            for part in range(2):
                target[place, part * lane_half : (part + 1) * lane_half] = sums.rings[part].total(place)
            return carry

        lax.fori_loop(0, rows // 16, tile, 0)

    total_to(down_sum, ring)
    ring.finish()
    for step in (1, -1):
        pl.semaphore_signal(credit, inc=1, device_id=places.on_ring(step), device_id_type=MESH)
    pl.semaphore_wait(credit, 2)
    ring = scatter_of(gate_grad, gate_send, gate_receive)
    ring.start(1)

    def stage_copy(number, side):
        place = pl.ds(pl.multiple_of(number * span, span), span)
        return pltpu.make_async_copy(stage.at[side], up_grad.at[place], stage_sem.at[side])

    def up_tile(pair, carry):
        for side in range(2):
            number = 2 * pair + side
            lanes = pl.ds(pl.multiple_of(number * span, span), span)
            value = dot(two[:, lanes], grads[:, units:], ((0,), (0,))).astype(bf16)

            @pl.when(pair > 0)
            def _(side=side, number=number):
                stage_copy(number - 2, side).wait()

            stage[side] = value
            stage_copy(number, side).start()
        return carry

    lax.fori_loop(0, spans // 2, up_tile, 0)
    ring.step(1)

    near_swap.wait()
    terms_to(outgoing, both_rows + theirs_start, out_terms)
    far_swap = remote(outgoing, core_far, send_sem.at[5], receive_sem.at[5], places.core())
    far_swap.start()
    chip_swap.wait()
    terms_to(far_part, both_rows + mine_start, out_terms)
    far_swap.wait()
    add_to(far_part, core_far)
    store_far = pltpu.make_async_copy(far_part, far_out, store_sem.at[0])
    store_far.start()
    out_rows = half_rows // 2
    out_swap = remote(
        far_part.at[pl.ds(0, out_rows)], out_got, send_sem.at[7], receive_sem.at[7], places.chip()
    )
    out_swap.start()
    ring.step(2)

    sends = []
    for number in range(half_rows // big):
        here = pl.ds(number * big, big)
        if number > 0:
            store_grad.wait()
        load_hidden = pltpu.make_async_copy(hidden_hbm.at[here], hidden, load_sem.at[10])
        load_hidden.start()
        place = pl.ds(pl.multiple_of(mine_start + number * big, big), big)
        value = two_terms(place) + core_near[here, :].astype(f32) + chip_got[here, :].astype(f32)
        load_hidden.wait()
        values = hidden[...]
        inverse = lax.rsqrt(jnp.mean(values * values, axis=1, keepdims=True) + norm_eps)
        scaled = value * gain_rows[1:2, :]
        mean = jnp.mean(scaled * values, axis=1, keepdims=True)
        total = cot[place, :].astype(f32) + inverse * scaled - values * (inverse * inverse * inverse) * mean
        hidden[...] = total
        chip_got[here, :] = total.astype(bf16)
        store_grad = pltpu.make_async_copy(hidden, hidden_grad.at[here], store_sem.at[1])
        store_grad.start()
        branch_place = branch.at[place]
        keep = pltpu.make_async_copy(chip_got.at[here], branch_place, store_sem.at[2 + number])
        send = remote(chip_got.at[here], branch_place, send_sem.at[3 + number], receive_sem.at[3 + number], places.core())
        keep.start()
        send.start()
        sends += [keep, send]
    store_grad.wait()

    terms_to(outgoing, theirs_start, out_terms)
    for copy in sends:
        copy.wait()
    near_swap = remote(outgoing, core_near, send_sem.at[6], receive_sem.at[6], places.core())
    near_swap.start()
    for number in range(half_rows // big):
        here = pl.ds(number * big, big)
        if number > 0:
            store_near.wait()
        load_hidden = pltpu.make_async_copy(hidden_hbm.at[here], hidden, load_sem.at[10])
        load_hidden.start()
        value = out_terms(pl.ds(pl.multiple_of(mine_start + number * big, big), big))
        load_hidden.wait()
        if number == 0:
            near_swap.wait()
        hidden[...] = value + hidden[...] + core_near[here, :].astype(f32)
        store_near = pltpu.make_async_copy(hidden, near_out.at[here], store_sem.at[4])
        store_near.start()
    for hop in range(3, half):
        ring.step(hop)
    ring.wait(half)
    total_to(gate_sum, ring)
    ring.finish()
    gather.finish()
    store_near.wait()
    store_far.wait()
    for side in range(2):
        stage_copy(spans - 2 + side, side).wait()
    out_swap.wait()


def middle(size, two_slots, cot_slots, feed, down_shard, hidden_state, gain_rows):
    half_rows, features = hidden_state.shape
    rows, width = feed.shape[1:]
    units = width // 2
    vmem = pl.BlockSpec(memory_space=pltpu.VMEM)
    anywhere = pl.BlockSpec(memory_space=pl.ANY)
    dma = pltpu.SemaphoreType.DMA
    half = size // 2
    bf16, f32 = jnp.bfloat16, jnp.float32
    shape = jax.ShapeDtypeStruct
    buffer = pltpu.VMEM
    return pl.pallas_call(
        functools.partial(middle_kernel, size),
        in_specs=[anywhere] * 5 + [vmem],
        out_specs=[anywhere, vmem, vmem] + [anywhere] * 5,
        out_shape=[
            shape((features, units), bf16),
            shape((rows, units), f32),
            shape((rows, units), f32),
            shape((half_rows, features), f32),
            shape((2 * half_rows, features), bf16),
            shape((half_rows, features), bf16),
            shape((half_rows, features), f32),
            shape((half_rows // 2, features), bf16),
        ],
        scratch_shapes=[
            buffer((4 * half_rows, features), bf16),
            buffer((4 * half_rows, features), bf16),
            buffer(feed.shape, bf16),
            buffer((size, rows, units), bf16),
            buffer((4 * half_rows, units), bf16),
            buffer((4 * half_rows, 2 * units), bf16),
            buffer((size, rows, units), bf16),
            buffer((size, rows, units), bf16),
            buffer((2, half, rows, units), bf16),
            buffer((half_rows, features), bf16),
            buffer((half_rows, features), bf16),
            buffer((half_rows, features), bf16),
            buffer((half_rows, features), bf16),
            buffer((half_rows, features), bf16),
            buffer((2, 384, units), bf16),
            buffer((256, features), f32),
            dma((11,)),
            dma((2,)),
            dma((2, 2, half)), dma((2, 2, half)),
            dma((2, 2, half)), dma((2, 2, half)),
            dma((2, 2, half)), dma((2, 2, half)),
            dma((8,)), dma((8,)),
            dma((5,)),
            pltpu.SemaphoreType.REGULAR,
        ],
        compiler_params=pltpu.CompilerParams(collective_id=3, has_side_effects=True, vmem_limit_bytes=63 * 2**20),
        cost_estimate=pl.CostEstimate(flops=6 * 10**10, bytes_accessed=300 * 2**20, transcendentals=0),
        name="middle",
    )(two_slots, cot_slots, feed, down_shard, hidden_state, gain_rows)


def finish_kernel(
    size, tokens_hbm, hidden_hbm, branch_hbm, normed_hbm, weights_hbm, output_hbm, qkv_hbm, att_hbm, up_hbm, up_shard,
    gate_hbm, gate_shard, far_out, near_hbm, first_out, log_ref, gain_rows, attend_shard, cos_ref, sin_ref,
    rotary_spread, plain_spread,
    tokens_grad, query_sum, key_sum, value_sum, output_sum, up_sum, gain_sum, layer_out,
    branch, grad_ref, back, dq_ref, dk_ref, dv_ref, own_grad, other_grad, crossed, ring_got, output_grad, output_got,
    up_grad, up_got, terms, got_terms, output_own, output_across, gain_parts, gate_sum, gate_part, up_part, second_out,
    normed, weights, output_spread, qkv_two, att_ref, tokens, hidden_grad, load_sem,
    ring_send, ring_receive, out_send, out_receive, up_send, up_receive, cross_send, cross_receive, across,
    gain_send, gain_receive,
):
    bf16, f32 = jnp.bfloat16, jnp.float32
    places = Places(size)
    half, own = places.half, places.own
    half_rows, features = tokens_hbm.shape
    rows = attend_shard.shape[0]
    units = up_got.shape[3]
    lane_half = units // 2
    span = 4 * HEAD
    big = 256
    diagonal = (own, 3 - places.tensor)
    group_order = (2, 3, 0, 1)
    greet([places.on_ring(1), places.on_ring(-1), places.chip(), places.core(), diagonal])

    out_rows = half_rows // 2
    out_swap = remote(
        far_out.at[pl.ds(out_rows, out_rows)], second_out, across.at[0], across.at[1], places.chip()
    )
    out_swap.start()

    def qkv_load(number):
        lanes = pl.ds(group_order[number] * 4 * LANES, 4 * LANES)
        return pltpu.make_async_copy(qkv_hbm.at[:, lanes], qkv_two.at[number % 2], load_sem.at[number])

    def row_loads(first, second, number):
        here = pl.ds(number * big, big)
        return (
            pltpu.make_async_copy(first.at[here], tokens, load_sem.at[4]),
            pltpu.make_async_copy(second.at[here], hidden_grad, load_sem.at[5]),
        )

    fetch = {
        "up": pltpu.make_async_copy(up_hbm, up_grad, load_sem.at[11]),
        "branch": pltpu.make_async_copy(branch_hbm, branch, load_sem.at[6]),
        "output": pltpu.make_async_copy(output_hbm, output_spread, load_sem.at[7]),
        "att": pltpu.make_async_copy(att_hbm, att_ref, load_sem.at[8]),
        "normed": pltpu.make_async_copy(normed_hbm, normed, load_sem.at[9]),
        "weights": pltpu.make_async_copy(weights_hbm, weights, load_sem.at[10]),
        "gate_sum": pltpu.make_async_copy(gate_hbm, gate_sum, load_sem.at[12]),
        "gate_part": pltpu.make_async_copy(gate_shard, gate_part, load_sem.at[13]),
        "up_part": pltpu.make_async_copy(up_shard, up_part, load_sem.at[14]),
    }
    fetch["up"].start()
    fetch["branch"].start()
    fetch["output"].start()
    qkv_loads = [qkv_load(number) for number in range(4)]
    qkv_loads[0].start()
    for name in ("att", "normed", "weights", "gate_sum", "gate_part", "up_part"):
        fetch[name].start()
    token_rows = row_loads(tokens_hbm, hidden_hbm, 0)
    for copy in token_rows:
        copy.start()

    def lanes_of(number, count):
        return pl.ds(number * count, count)

    ups = Parts([
        RingScatter(
            places,
            lambda slot, number=number: up_grad.at[
                pl.ds(pl.multiple_of(slot * rows, rows), rows), lanes_of(number, lane_half)
            ],
            up_got.at[:, :, :, lanes_of(number, lane_half)],
            up_send.at[number],
            up_receive.at[number],
        )
        for number in range(2)
    ])
    fetch["up"].wait()
    ups.start(1)
    fetch["branch"].wait()
    fetch["output"].wait()
    fetch["att"].wait()

    def back_group(number, target, lane):
        group = group_order[number]
        qkv_loads[number].wait()
        if number < 3:
            qkv_loads[number + 1].start()
        qkv_ref = qkv_two.at[number % 2]
        base = 0
        for part in range(2):
            block = pl.ds(part * half_rows, half_rows)
            value = dot(branch[block, :], output_spread[:, group * 2 * LANES : (group + 1) * 2 * LANES])
            grad_ref[block, :] = value.astype(bf16)
        turned = qkv_ref[:, base + 2 * LANES : base + 3 * LANES].T
        cos, sin = cos_ref[...], sin_ref[...]
        scale = HEAD**-0.5

        def unrot(u):
            return (u * cos - pltpu.roll(u, 64, 1) * sin).astype(bf16)

        key_place = lax.broadcasted_iota(jnp.int32, (QB, QB), 0)
        query_place = lax.broadcasted_iota(jnp.int32, (QB, QB), 1)
        for head in range(2):
            lanes = slice(head * LANES, (head + 1) * LANES)
            att_lane = (2 * group + head) * LANES
            prod = grad_ref[:, lanes].astype(f32) * att_ref[:, att_lane : att_lane + LANES].astype(f32)
            delta = jnp.sum(prod.T, axis=0, keepdims=True)
            for block in reversed(range(LENGTH // QB)):
                first, last = block * QB, (block + 1) * QB
                query = qkv_ref[first:last, base + head * LANES : base + (head + 1) * LANES]
                out_grad = grad_ref[first:last, lanes]
                score = dot(qkv_ref[:last, base + 2 * LANES : base + 3 * LANES], query, ((1,), (1,)))
                prob = jnp.exp2(score * C2 - log_ref[group, head : head + 1, first:last])
                edge = jnp.where(key_place <= query_place, prob[first:], 0.0)
                prob = jnp.concatenate([prob[:first], edge], axis=0) if block else edge
                prob_grad = dot(qkv_ref[:last, base + 3 * LANES : base + 4 * LANES], out_grad, ((1,), (1,)))
                score_grad = (prob * (prob_grad - delta[:, first:last])).astype(bf16)
                key_part = dot(score_grad, query)
                value_part = dot(prob.astype(bf16), out_grad)
                if head == 0 and block == LENGTH // QB - 1:
                    dk_ref[...] = key_part
                    dv_ref[...] = value_part
                else:
                    dk_ref[:last] += key_part
                    dv_ref[:last] += value_part
                dq_ref[first:last, lanes] = dot(turned[:, :last], score_grad).T
        wide = jnp.concatenate(
            [
                unrot(dq_ref[:, :LANES] * scale),
                unrot(dq_ref[:, LANES:] * scale),
                unrot(dk_ref[...] * scale),
                dv_ref[...].astype(bf16),
            ],
            axis=1,
        )
        close_back = dot(wide, rotary_spread[...], ((1,), (1,))).astype(bf16)
        back[:, group * span : (group + 1) * span] = close_back
        if number == 0:
            fetch["normed"].wait()
        for part in range(2):
            block = slice(part * features // 2, (part + 1) * features // 2)
            value = dot(normed[:, block], close_back, ((0,), (0,))).astype(bf16)
            target[part * size // 2 : (part + 1) * size // 2, :, lane : lane + span] = value.reshape(
                size // 2, rows, span
            )

    order = [half]
    for step in range(half - 1, 0, -1):
        order += [step, -step]
    order.append(0)
    crossing = {}

    def cross(group):
        for number, step in enumerate(order):
            slot = places.index(step)
            lanes = pl.ds(group * span, span)
            copy = remote(
                other_grad.at[slot, :, lanes], crossed.at[slot, :, lanes],
                cross_send.at[group, number], cross_receive.at[group, number], places.chip(),
            )
            copy.start()
            crossing[(group, step)] = copy

    back_group(0, other_grad, 0)
    cross(0)
    ups.step(1)
    back_group(1, other_grad, span)
    cross(1)
    ups.step(2)

    heads_width = output_spread.shape[1] // 2
    columns = heads_width // LANES * HEAD
    for side in range(2):
        close = dot(
            att_ref[:, side * heads_width : (side + 1) * heads_width], plain_spread[...], ((1,), (1,))
        ).astype(bf16)
        for part in range(2):
            block = slice(part * features // 2, (part + 1) * features // 2)
            value = dot(branch[:, block], close, ((0,), (0,))).astype(bf16)
            output_grad[part * size // 2 : (part + 1) * size // 2, :, side * columns : (side + 1) * columns] = (
                value.reshape(size // 2, rows, columns)
            )
    outputs = Parts([
        RingScatter(
            places,
            lambda slot, number=number: output_grad.at[slot, :, lanes_of(number, columns)],
            output_got.at[:, :, :, lanes_of(number, columns)],
            out_send.at[number],
            out_receive.at[number],
        )
        for number in range(2)
    ])
    outputs.start(1)
    back_group(2, own_grad, 0)
    for hop in range(3, half):
        ups.step(hop)
    outputs.step(1)
    back_group(3, own_grad, span)
    outputs.step(2)

    def prepare(group, step):
        crossing[(group, step)].wait_recv()
        slot = places.index(step)
        lanes = lanes_of(group, span)

        def tile(number, carry):
            place = pl.ds(pl.multiple_of(number * 16, 16), 16)
            value = crossed[slot, place, lanes].astype(f32) + own_grad[slot, place, lanes].astype(f32)
            crossed[slot, place, lanes] = value.astype(bf16)
            return carry

        lax.fori_loop(0, rows // 16, tile, 0)

    attend = [
        RingScatter(
            places,
            lambda slot, number=number: crossed.at[slot, :, lanes_of(number, span)],
            ring_got.at[:, :, :, lanes_of(number, span)],
            ring_send.at[number],
            ring_receive.at[number],
        )
        for number in range(2)
    ]

    def attend_start(group):
        prepare(group, half)
        attend[group].start(1)

    def attend_step(group, hop):
        prepare(group, half - hop)
        prepare(group, hop - half)
        attend[group].step(hop)

    attend_start(0)
    whole = weights.shape[2]
    fetch["weights"].wait()

    def terms_of(block):
        return dot(back[block, :], weights[...].reshape(features, whole), ((1,), (1,)))

    def theirs_tile(number, carry):
        place = (1 - places.side) * half_rows + number * big
        value = terms_of(pl.ds(pl.multiple_of(place, big), big))
        terms[pl.ds(pl.multiple_of(number * big, big), big), :] = value.astype(bf16)
        return carry

    lax.fori_loop(0, half_rows // big, theirs_tile, 0)
    terms_swap = remote(terms, got_terms, across.at[2], across.at[3], places.core())
    terms_swap.start()
    attend_step(0, 1)
    for hop in range(3, half):
        outputs.step(hop)
    terms_swap.wait()
    for number in range(half_rows // big):
        for copy in token_rows:
            copy.wait()
        here = slice(number * big, (number + 1) * big)
        place = places.side * half_rows + number * big
        value = terms_of(pl.ds(pl.multiple_of(place, big), big)) + got_terms[here, :].astype(f32)
        values = tokens[...].astype(f32)
        inverse = lax.rsqrt(jnp.mean(values * values, axis=1, keepdims=True) + norm_eps)
        scaled = value * gain_rows[0:1, :]
        inner = jnp.mean(scaled * values, axis=1, keepdims=True)
        result = hidden_grad[...] + inverse * scaled - values * (inverse * inverse * inverse) * inner
        tokens_grad[here, :] = result.astype(bf16)
        if number < half_rows // big - 1:
            token_rows = row_loads(tokens_hbm, hidden_hbm, number + 1)
            for copy in token_rows:
                copy.start()
        if number == 0 and half > 2:
            attend_step(0, 2)
    attend_start(1)
    for hop in range(3, half):
        attend_step(0, hop)
    prepare(0, 0)

    outputs.wait(half)

    def output_tile(number, carry):
        place = pl.ds(pl.multiple_of(number * 16, 16), 16)
        output_own[place, :] = outputs.rings[0].total(place)
        output_across[0, place, :] = outputs.rings[1].total(place).astype(bf16)
        return carry

    lax.fori_loop(0, rows // 16, output_tile, 0)
    output_swap = remote(output_across.at[0], output_across.at[1], across.at[4], across.at[5], places.chip())
    output_swap.start()
    attend_step(1, 1)
    ups.wait(half)
    for name in ("gate_sum", "gate_part", "up_part"):
        fetch[name].wait()

    def up_tile(number, carry):
        place = pl.ds(pl.multiple_of(number * 16, 16), 16)
        gain = jnp.sum(gate_sum[place, :] * gate_part[place, :].astype(f32), axis=1, keepdims=True)
        for part in range(2):
            lanes = slice(part * lane_half, (part + 1) * lane_half)
            value = ups.rings[part].total(place)
            up_sum[place, lanes] = value
            gain += jnp.sum(value * up_part[place, lanes].astype(f32), axis=1, keepdims=True)
        lane = lax.broadcasted_iota(jnp.int32, (16, LANES), 1)
        gain_parts[0, place, :] = jnp.where(lane == 1, gain, 0.0)
        return carry

    lax.fori_loop(0, rows // 16, up_tile, 0)
    if half > 2:
        attend_step(1, 2)

    out_swap.wait()
    for number in range(half_rows // big):
        here = pl.ds(number * big, big)
        source = first_out if number < half_rows // big // 2 else second_out
        rest = pl.ds(number * big % out_rows, big)
        share = pltpu.make_async_copy(source.at[rest], tokens, load_sem.at[4])
        near = pltpu.make_async_copy(near_hbm.at[here], hidden_grad, load_sem.at[5])
        share.start()
        near.start()
        share.wait()
        near.wait()
        tokens[...] = (hidden_grad[...] + tokens[...].astype(f32)).astype(bf16)
        store = pltpu.make_async_copy(tokens, layer_out.at[here], load_sem.at[15])
        store.start()
        store.wait()
    for hop in range(3, half):
        attend_step(1, hop)
    prepare(1, 0)
    output_swap.wait()
    output_sum[...] = output_own[...] + output_across[1].astype(f32)
    for part in range(2):
        attend[part].wait(half)

    def attend_tile(number, carry):
        place = pl.ds(pl.multiple_of(number * 16, 16), 16)
        gain = jnp.zeros((16, 1), f32)
        for part in range(2):
            value = attend[part].total(place)
            query_sum[place, part * 2 * HEAD : (part + 1) * 2 * HEAD] = value[:, : 2 * HEAD]
            key_sum[place, part * HEAD : (part + 1) * HEAD] = value[:, 2 * HEAD : 3 * HEAD]
            value_sum[place, part * HEAD : (part + 1) * HEAD] = value[:, 3 * HEAD :]
            gain += jnp.sum(
                value * attend_shard[place, part * span : (part + 1) * span].astype(f32), axis=1, keepdims=True
            )
        lane = lax.broadcasted_iota(jnp.int32, (16, LANES), 1)
        gain_parts[0, place, :] += jnp.where(lane == 0, gain, 0.0)
        return carry

    lax.fori_loop(0, rows // 16, attend_tile, 0)
    gain_copies = []
    for number, device in enumerate((places.core(), places.chip(), diagonal)):
        copy = remote(
            gain_parts.at[0], gain_parts.at[1 + number], gain_send.at[number], gain_receive.at[number], device
        )
        copy.start()
        gain_copies.append(copy)
    for copy in crossing.values():
        copy.wait_send()
    ups.finish()
    outputs.finish()
    for ring in attend:
        ring.finish()
    for copy in gain_copies:
        copy.wait()
    gain_sum[...] = (gain_parts[0] + gain_parts[1]) + (gain_parts[2] + gain_parts[3])


def finish(
    size, tokens, hidden_grad, branch, normed, weights, output_spread, qkv, att, logs, gain_rows, up_grad, up_shard,
    gate_sum, gate_shard, attend_shard, far_out, near_out, first_out,
):
    half_rows, features = tokens.shape
    rows, width = attend_shard.shape
    columns = output_spread.shape[1] // 2 // LANES * HEAD
    units = up_shard.shape[1]
    vmem = pl.BlockSpec(memory_space=pltpu.VMEM)
    anywhere = pl.BlockSpec(memory_space=pl.ANY)
    dma = pltpu.SemaphoreType.DMA
    half = size // 2
    bf16, f32 = jnp.bfloat16, jnp.float32
    cos, sin = rope_tables()
    shape = jax.ShapeDtypeStruct
    buffer = pltpu.VMEM
    return pl.pallas_call(
        functools.partial(finish_kernel, size),
        in_specs=[anywhere] * 15 + [vmem] * 7,
        out_specs=[vmem] * 7 + [anywhere],
        out_shape=[
            shape((half_rows, features), bf16),
            shape((rows, width // 2), f32),
            shape((rows, width // 4), f32),
            shape((rows, width // 4), f32),
            shape((rows, columns), f32),
            shape((rows, units), f32),
            shape((rows, LANES), f32),
            shape((half_rows, features), bf16),
        ],
        scratch_shapes=[
            buffer((LENGTH, features), bf16),
            buffer((LENGTH, 2 * LANES), bf16),
            buffer((LENGTH, 2 * width), bf16),
            buffer((LENGTH, 2 * LANES), f32),
            buffer((LENGTH, LANES), f32),
            buffer((LENGTH, LANES), f32),
            buffer((size, rows, width), bf16),
            buffer((size, rows, width), bf16),
            buffer((size, rows, width), bf16),
            buffer((2, half, rows, width), bf16),
            buffer((size, rows, 2 * columns), bf16),
            buffer((2, half, rows, 2 * columns), bf16),
            buffer((features, units), bf16),
            buffer((2, half, rows, units), bf16),
            buffer((half_rows, features), bf16),
            buffer((half_rows, features), bf16),
            buffer((rows, columns), f32),
            buffer((2, rows, columns), bf16),
            buffer((4, rows, LANES), f32),
            buffer((rows, units), f32),
            buffer((rows, units), bf16),
            buffer((rows, units), bf16),
            buffer((half_rows // 2, features), bf16),
            buffer((LENGTH, features), bf16),
            buffer(weights.shape, bf16),
            buffer(output_spread.shape, bf16),
            buffer((2, LENGTH, 4 * LANES), bf16),
            buffer(att.shape, bf16),
            buffer((256, features), bf16),
            buffer((256, features), f32),
            dma((16,)),
            dma((2, 2, half)), dma((2, 2, half)),
            dma((2, 2, half)), dma((2, 2, half)),
            dma((2, 2, half)), dma((2, 2, half)),
            dma((2, size)), dma((2, size)),
            dma((6,)),
            dma((3,)), dma((3,)),
        ],
        compiler_params=pltpu.CompilerParams(collective_id=2, has_side_effects=True, vmem_limit_bytes=63 * 2**20),
        cost_estimate=pl.CostEstimate(flops=3 * 10**10, bytes_accessed=300 * 2**20, transcendentals=0),
        name="finish",
    )(
        tokens, hidden_grad, branch, normed, weights, output_spread, qkv, att, up_grad, up_shard, gate_sum, gate_shard,
        far_out, near_out, first_out, logs, gain_rows, attend_shard, jnp.asarray(cos), jnp.asarray(sin),
        jnp.asarray(spread(4, (1, 1, 1, 0)), bf16), jnp.asarray(spread(4, (0,) * 4), bf16),
    )


def local(
    dp_size,
    tokens,
    first_gain,
    query_weight,
    key_weight,
    value_weight,
    output_weight,
    second_gain,
    gate_weight,
    up_weight,
    down_weight,
    cotangent,
):
    f32 = jnp.float32
    groups = key_weight.shape[1] // HEAD
    packs = []
    for group in range(groups):
        packs.append(query_weight[:, group * 2 * HEAD : (group + 1) * 2 * HEAD])
        packs.append(key_weight[:, group * HEAD : (group + 1) * HEAD])
        packs.append(value_weight[:, group * HEAD : (group + 1) * HEAD])
    attend_shard = jnp.concatenate(packs, axis=1)
    lanes = LANES * pl.cdiv(first_gain.shape[0], LANES)
    both_gains = jnp.stack([first_gain, second_gain]).astype(f32)
    both_gains = jnp.pad(both_gains, ((0, 6), (0, lanes - first_gain.shape[0])))
    (normed, weights, output_spread, qkv, attended, logs, hidden_state, two_slots, cot_slots, feed, gain_rows) = begin(
        dp_size, tokens, cotangent, both_gains, attend_shard, output_weight.T, gate_weight, up_weight
    )
    up_grad, gate_sum, down_sum, hidden_grad, branch, far_out, near_out, first_out = middle(
        dp_size, two_slots, cot_slots, feed, down_weight.T, hidden_state, gain_rows
    )
    tokens_grad, query_sum, key_sum, value_sum, output_sum, up_sum, gain_sums, layer_out = finish(
        dp_size, tokens, hidden_grad, branch, normed, weights, output_spread, qkv, attended, logs, gain_rows,
        up_grad, up_weight, gate_sum, gate_weight, attend_shard, far_out, near_out, first_out,
    )
    return (
        layer_out,
        tokens_grad,
        gain_sums[:, 0] / first_gain.astype(f32),
        query_sum,
        key_sum,
        value_sum,
        output_sum.T,
        gain_sums[:, 1] / second_gain.astype(f32),
        gate_sum,
        up_sum,
        down_sum.T,
    )


def solution(mesh):
    in_specs = (
        P(("dp", "tensor"), None),
        P("dp"),
        P("dp", "tensor"),
        P("dp", "tensor"),
        P("dp", "tensor"),
        P("tensor", "dp"),
        P("dp"),
        P("dp", "tensor"),
        P("dp", "tensor"),
        P("tensor", "dp"),
        P(("dp", "tensor"), None),
    )
    out_specs = (
        P(("dp", "tensor"), None),
        P(("dp", "tensor"), None),
        P("dp"),
        P("dp", "tensor"),
        P("dp", "tensor"),
        P("dp", "tensor"),
        P("tensor", "dp"),
        P("dp"),
        P("dp", "tensor"),
        P("dp", "tensor"),
        P("tensor", "dp"),
    )
    body = functools.partial(local, mesh.shape["dp"])
    return jax.shard_map(body, mesh=mesh, in_specs=in_specs, out_specs=out_specs, check_vma=False)
```

```python
import functools

import jax
import jax.numpy as jnp
import numpy as np
from jax import lax
from jax.experimental import pallas as pl
from jax.experimental.pallas import tpu as pltpu
from jax.sharding import PartitionSpec as P

HEAD = 96
LENGTH = 1024
LANES = 128
QB = 256
norm_eps = 1e-05
rope_base = 100000.0


def rope_tables():
    half = HEAD // 2
    freq = rope_base ** (np.arange(half, dtype=np.float64) * (-2.0 / HEAD))
    turned = np.arange(LENGTH, dtype=np.float64)[:, None] * freq[None, :]
    cos = np.zeros((LENGTH, LANES), np.float32); sin = np.zeros((LENGTH, LANES), np.float32)
    cos[:, :half] = np.cos(turned); cos[:, 64:64+half] = np.cos(turned)
    sin[:, :half] = -np.sin(turned); sin[:, 64:64+half] = np.sin(turned)
    return cos, sin

def spread(heads, rotary):
    e = np.zeros((heads * HEAD, heads * LANES), np.float32)
    for h in range(heads):
        for i in range(HEAD):
            lane = i if (not rotary[h] or i < 48) else i + 16
            e[h * HEAD + i, h * LANES + lane] = 1
    return e

def dot(a, b, dims=((1,), (0,))):
    return lax.dot_general(a, b, (dims, ((), ())), preferred_element_type=jnp.float32)

C2 = float(HEAD ** -0.5 * np.log2(np.e))


MESH = pl.DeviceIdType.MESH


class Places:
    def __init__(self, size):
        self.size = size
        self.half = size // 2
        self.own = lax.axis_index("dp")
        self.tensor = lax.axis_index("tensor")
        self.side = self.tensor % 2
        odd = self.own % 2
        self.place = (1 - odd) * (self.own // 2) + odd * (size - 1 - self.own // 2)

    def index(self, step):
        place = (self.place + step + self.size) % self.size
        late = place // self.half
        return (1 - late) * 2 * place + late * (2 * (self.size - 1 - place) + 1)

    def on_ring(self, step):
        return (self.index(step), self.tensor)

    def peer(self, step):
        return ((self.own + step + self.size) % self.size, self.tensor)

    def chip(self):
        return (self.own, (self.tensor + 2) % 4)

    def core(self):
        return (self.own, self.tensor + 1 - 2 * self.side)


def remote(source, target, send, receive, device):
    return pltpu.make_async_remote_copy(
        src_ref=source,
        dst_ref=target,
        send_sem=send,
        recv_sem=receive,
        device_id=device,
        device_id_type=MESH,
    )


def greet(devices):
    barrier = pltpu.get_barrier_semaphore()
    for device in devices:
        pl.semaphore_signal(barrier, inc=1, device_id=device, device_id_type=MESH)
    pl.semaphore_wait(barrier, len(devices))


class RingGather:
    def __init__(self, places, slots, send, receive):
        self.places, self.slots, self.send, self.receive = places, slots, send, receive
        self.cut = slots.shape[1] // 32 * 16
        self.sent = []

    def start(self, hop, source=None):
        places, half = self.places, self.places.half
        for way, (step, device) in enumerate(
            ((1 - hop, places.on_ring(1)), (hop - 1, places.on_ring(-1)))
        ):
            slot = places.index(step)
            rows = pl.ds(0, self.slots.shape[1])
            if hop == half:
                rows = (pl.ds(0, self.cut), pl.ds(self.cut, self.slots.shape[1] - self.cut))[way]
            view = self.slots.at[slot, rows]
            copy = remote(
                view if source is None else source.at[rows],
                view,
                self.send.at[way, hop - 1],
                self.receive.at[way, hop - 1],
                device,
            )
            copy.start()
            self.sent.append(copy)

    def wait(self, hop):
        self.sent[2 * hop - 2].wait_recv()
        self.sent[2 * hop - 1].wait_recv()

    def step(self, hop):
        self.wait(hop)
        if hop < self.places.half:
            self.start(hop + 1)

    def finish(self):
        for copy in self.sent:
            copy.wait_send()


class Parts:
    def __init__(self, rings):
        self.rings = rings

    def start(self, hop, sources=None):
        for number, ring in enumerate(self.rings):
            ring.start(hop) if sources is None else ring.start(hop, sources[number])

    def wait(self, hop):
        for ring in self.rings:
            ring.wait(hop)

    def step(self, hop):
        for ring in self.rings:
            ring.step(hop)

    def finish(self):
        for ring in self.rings:
            ring.finish()


class Spread:
    def __init__(self, places, own, slots, send, receive):
        self.places, self.slots, self.send, self.receive = places, slots, send, receive
        near, far = slots.at[places.side], slots.at[2 + places.side]
        self.chip = remote(own, far, send.at[0], receive.at[0], places.chip())
        self.core = remote(own, near, send.at[1], receive.at[1], places.core())
        self.far = far

    def start(self):
        self.chip.start()
        self.core.start()

    def pass_on(self):
        self.chip.wait_recv()
        self.last = remote(self.far, self.far, self.send.at[2], self.receive.at[2], self.places.core())
        self.last.start()

    def finish(self):
        self.chip.wait_send()
        self.core.wait()
        self.last.wait()


def hidden_units(source, weights, inner, factors, rows, units, number, block=512):
    features = source.shape[1]

    def lanes(start):
        return weights[:, :, start : start + block].reshape(features, block)

    lane = number * block
    gate = dot(source[...], lanes(lane))
    up = dot(source[...], lanes(units + lane))
    sigmoid = 1.0 / (1.0 + jnp.exp(-gate))
    silu = gate * sigmoid
    inner[rows, lane : lane + block] = (silu * up).astype(jnp.bfloat16)
    factors[rows, lane : lane + block] = (up * (sigmoid + silu * (1.0 - sigmoid))).astype(jnp.bfloat16)
    factors[rows, units + lane : units + lane + block] = silu.astype(jnp.bfloat16)


def begin_kernel(
    size, tokens_hbm, cotangent, attend_shard, output_shard, gate_shard, up_shard, down_shard, cos_hbm, sin_hbm,
    rotary_hbm, plain_hbm, gains,
    normed_hbm, weights_hbm, output_hbm, qkv_hbm, att_hbm, hidden_hbm, two_slots, cot_slots, feed_hbm, down_hbm,
    inner_hbm, factors_hbm, log_ref, gain_rows,
    tokens, cos_ref, sin_ref, rotary_spread, plain_spread, normed, weights, output_spread, qkv_ref, att_ref, hidden,
    feed, inner, factors, down, two_other,
    gain_slots, output_both, terms, received, two_own, gain_send, gain_receive, ring_send, ring_receive,
    pass_send, pass_receive, out_send, out_receive, feed_send, feed_receive, down_send, down_receive, across, two_send,
    two_receive, cot_send, cot_receive, local_sem, load_sem, store_sem,
):
    bf16, f32 = jnp.bfloat16, jnp.float32
    places = Places(size)
    half, own = places.half, places.own
    half_rows = tokens.shape[0]
    columns = output_shard.shape[1]
    width = attend_shard.shape[1]
    units = gate_shard.shape[1]
    loads = [
        pltpu.make_async_copy(source, target, load_sem.at[number])
        for number, (source, target) in enumerate((
            (tokens_hbm, tokens), (cos_hbm, cos_ref), (sin_hbm, sin_ref), (rotary_hbm, rotary_spread),
            (plain_hbm, plain_spread),
        ))
    ]
    for copy in loads:
        copy.start()
    stores = []

    def store(source, target):
        copy = pltpu.make_async_copy(source, target, store_sem.at[len(stores)])
        copy.start()
        stores.append(copy)

    greet([places.peer(step) for step in range(1, size)] + [places.chip(), places.core()])

    def own_side(slot):
        return weights.at[slot, :, pl.ds(0, width)]

    def other_side(slot):
        return weights.at[slot, :, pl.ds(width, width)]

    def lanes_of(number, count):
        return pl.ds(number * count, count)

    ring = Parts([
        RingGather(places, weights.at[:, :, lanes_of(number, width // 2)], ring_send.at[number], ring_receive.at[number])
        for number in range(2)
    ])
    ring.start(1, [attend_shard.at[:, lanes_of(number, width // 2)] for number in range(2)])
    passed = []

    def hand_on(step, number, source=None):
        slot = places.index(step)
        copy = remote(
            own_side(slot) if source is None else source, other_side(slot),
            pass_send.at[number], pass_receive.at[number], places.chip(),
        )
        copy.start()
        passed.append(copy)

    hand_on(0, 0, attend_shard)
    output_pass = remote(
        output_shard, output_both.at[own, :, pl.ds(columns, columns)], across.at[0], across.at[1], places.chip()
    )
    output_pass.start()
    gain_copies = []
    for step in range(1, size):
        copy = remote(gains, gain_slots.at[own], gain_send.at[step - 1], gain_receive.at[step - 1], places.peer(step))
        copy.start()
        gain_copies.append(copy)
    near = cot_slots.at[places.side]
    keep = [
        pltpu.make_async_copy(attend_shard, own_side(own), local_sem.at[0]),
        pltpu.make_async_copy(output_shard, output_both.at[own, :, pl.ds(0, columns)], local_sem.at[1]),
        pltpu.make_async_copy(gate_shard, feed.at[own, :, lanes_of(0, units)], local_sem.at[2]),
        pltpu.make_async_copy(up_shard, feed.at[own, :, lanes_of(1, units)], local_sem.at[5]),
        pltpu.make_async_copy(down_shard, down.at[own], local_sem.at[6]),
        pltpu.make_async_copy(cotangent, near, local_sem.at[3]),
    ]
    for copy in keep:
        copy.start()
    gain_slots[own] = gains[...]

    def ring_step(hop):
        ring.step(hop)
        if hop < half:
            hand_on(-hop, 2 * hop - 1)
            hand_on(hop, 2 * hop)
        else:
            hand_on(half, size - 1)

    for copy in gain_copies:
        copy.wait_recv()
    part = tokens.shape[1] // size
    for index in range(size):
        gain_rows[:, index * part : (index + 1) * part] = gain_slots[index][:, :part]
    tile = 64
    mine_start = places.side * half_rows

    def norm_tile(number, carry):
        rows = pl.ds(pl.multiple_of(number * tile, tile), tile)
        values = tokens[rows, :].astype(f32)
        inverse = lax.rsqrt(jnp.mean(values * values, axis=1, keepdims=True) + norm_eps)
        target = pl.ds(pl.multiple_of(mine_start + number * tile, tile), tile)
        normed[target, :] = (values * inverse * gain_rows[0:1, :]).astype(bf16)
        return carry

    tiles = half_rows // tile
    for copy in loads:
        copy.wait()
    ring_step(1)
    lax.fori_loop(0, tiles // 2, norm_tile, 0)
    ring_step(2)
    lax.fori_loop(tiles // 2, tiles, norm_tile, 0)
    mine = pl.ds(pl.multiple_of(mine_start, half_rows), half_rows)
    swap = remote(normed.at[mine], normed.at[mine], across.at[2], across.at[3], places.core())
    swap.start()
    for hop in range(3, half):
        ring_step(hop)
    outputs = Parts([
        RingGather(places, output_both.at[:, :, lanes_of(number, columns)], out_send.at[number], out_receive.at[number])
        for number in range(2)
    ])
    output_pass.wait()
    for copy in keep:
        copy.wait()
    outputs.start(1)
    ring_step(half)
    swap.wait()
    store(normed, normed_hbm)

    def attend(group):
        lanes = pl.ds(group * 4 * HEAD, 4 * HEAD)
        weight = weights[:, :, lanes].reshape(tokens.shape[1], 4 * HEAD)
        weight = dot(weight, rotary_spread[...]).astype(bf16)
        rows = dot(normed[...], weight)
        cos, sin = cos_ref[...], sin_ref[...]
        base = group * 4 * LANES

        def rot(u):
            return (u * cos + pltpu.roll(u, 64, 1) * sin).astype(bf16)

        for head in range(3):
            lane = head * LANES
            qkv_ref[:, base + lane : base + lane + LANES] = rot(rows[:, lane : lane + LANES])
        qkv_ref[:, base + 3 * LANES : base + 4 * LANES] = rows[:, 3 * LANES :].astype(bf16)
        turned = qkv_ref[:, base + 3 * LANES : base + 4 * LANES].T
        key_place = lax.broadcasted_iota(jnp.int32, (QB, QB), 0)
        query_place = lax.broadcasted_iota(jnp.int32, (QB, QB), 1)
        for head in range(2):
            for block in range(LENGTH // QB):
                first, last = block * QB, (block + 1) * QB
                query = qkv_ref[first:last, base + head * LANES : base + (head + 1) * LANES]
                key = qkv_ref[:last, base + 2 * LANES : base + 3 * LANES]
                score = dot(key, query, ((1,), (1,)))
                edge = jnp.where(key_place <= query_place, score[first:], -1e30)
                score = jnp.concatenate([score[:first], edge], axis=0) if block else edge
                top = jnp.max(score, axis=0, keepdims=True)
                weight = jnp.exp2((score - top) * C2)
                total = jnp.sum(weight, axis=0, keepdims=True)
                result = dot(turned[:, :last], weight.astype(bf16)) / total
                lane = group * 2 * LANES + head * LANES
                att_ref[first:last, lane : lane + LANES] = result.T.astype(bf16)
                log_ref[group, head, pl.ds(first, QB)] = (top * C2 + jnp.log2(total))[0]

    attend(0)
    outputs.step(1)
    attend(1)
    for hop in range(2, half):
        outputs.step(hop)
    ring_feed = Parts([
        RingGather(places, feed.at[:, :, lanes_of(number, units)], feed_send.at[number], feed_receive.at[number])
        for number in range(2)
    ])
    ring_feed.start(1, [gate_shard, up_shard])
    outputs.step(half)
    for copy in passed:
        copy.wait()
    store(weights, weights_hbm)
    cot = Spread(places, cotangent, cot_slots, cot_send, cot_receive)
    cot.start()
    attend(2)
    attend(3)
    store(qkv_ref, qkv_hbm)
    store(att_ref, att_hbm)
    ring_feed.step(1)

    heads_width = columns // HEAD * LANES
    out_rows = output_shard.shape[0]

    def spread_slot(number, carry):
        rows = pl.ds(pl.multiple_of(number * out_rows, out_rows), out_rows)
        for side in range(2):
            value = dot(output_both[number, :, side * columns : (side + 1) * columns], plain_spread[...])
            output_spread[rows, side * heads_width : (side + 1) * heads_width] = value.astype(bf16)
        return carry

    lax.fori_loop(0, size, spread_slot, 0)
    store(output_spread, output_hbm)
    big = 256

    def theirs_tile(number, carry):
        start = (1 - places.side) * half_rows + number * big
        rows = pl.ds(pl.multiple_of(start, big), big)
        value = dot(att_ref[rows, :], output_spread[...], ((1,), (1,)))
        terms[pl.ds(pl.multiple_of(number * big, big), big), :] = value.astype(bf16)
        return carry

    lax.fori_loop(0, half_rows // big, theirs_tile, 0)
    sum_swap = remote(terms, received, across.at[4], across.at[5], places.core())
    sum_swap.start()

    def mine_tile(number, carry):
        rows = pl.ds(pl.multiple_of(mine_start + number * big, big), big)
        value = dot(att_ref[rows, :], output_spread[...], ((1,), (1,)))
        here = pl.ds(pl.multiple_of(number * big, big), big)
        hidden[here, :] = value + tokens[here, :].astype(f32)
        return carry

    lax.fori_loop(0, half_rows // big, mine_tile, 0)
    sum_swap.wait()

    def second_tile(number, carry):
        rows = pl.ds(pl.multiple_of(number * tile, tile), tile)
        values = hidden[rows, :] + received[rows, :].astype(f32)
        hidden[rows, :] = values
        inverse = lax.rsqrt(jnp.mean(values * values, axis=1, keepdims=True) + norm_eps)
        two_own[rows, :] = (values * inverse * gain_rows[1:2, :]).astype(bf16)
        return carry

    lax.fori_loop(0, half_rows // tile, second_tile, 0)
    two = Spread(places, two_own, two_slots, two_send, two_receive)
    two.start()
    store(two_own, two_slots.at[places.side])
    store(hidden, hidden_hbm)
    ring_feed.step(2)
    cot.pass_on()
    for hop in range(3, half):
        ring_feed.step(hop)
    ring_down = Parts([
        RingGather(
            places, down.at[:, :, lanes_of(number, units // 2)], down_send.at[number], down_receive.at[number]
        )
        for number in range(2)
    ])
    ring_down.start(1, [down_shard.at[:, lanes_of(number, units // 2)] for number in range(2)])
    ring_feed.step(half)
    store(feed, feed_hbm)

    mine_rows = pl.ds(pl.multiple_of(mine_start, half_rows), half_rows)
    other_rows = pl.ds(pl.multiple_of(half_rows - mine_start, half_rows), half_rows)
    two.core.wait_recv()
    load_other = pltpu.make_async_copy(two_slots.at[1 - places.side], two_other, local_sem.at[4])
    load_other.start()
    hop = 1
    for source, place in ((two_own, mine_rows), (two_other, other_rows)):
        if source is two_other:
            load_other.wait()
        for number in range(units // 512):
            hidden_units(source, feed, inner, factors, place, units, number)
            if hop < half:
                ring_down.step(hop)
                hop += 1
    store(inner, inner_hbm)
    store(factors, factors_hbm)
    two.pass_on()
    for late in range(hop, half + 1):
        ring_down.step(late)
    store(down, down_hbm)
    cot.finish()
    two.chip.wait_send()
    two.core.wait_send()
    two.last.wait()
    for copy in gain_copies:
        copy.wait_send()
    ring.finish()
    outputs.finish()
    ring_feed.finish()
    ring_down.finish()
    for copy in stores:
        copy.wait()


def begin(size, tokens, cotangent, gains, attend_shard, output_shard, gate_shard, up_shard, down_shard):
    half_rows, features = tokens.shape
    rows, width = attend_shard.shape
    columns = output_shard.shape[1]
    units = gate_shard.shape[1]
    heads_width = columns // HEAD * LANES
    groups = 2 * width // (4 * HEAD)
    vmem = pl.BlockSpec(memory_space=pltpu.VMEM)
    anywhere = pl.BlockSpec(memory_space=pl.ANY)
    dma = pltpu.SemaphoreType.DMA
    half = size // 2
    bf16, f32 = jnp.bfloat16, jnp.float32
    cos, sin = rope_tables()
    shape = jax.ShapeDtypeStruct
    buffer = pltpu.VMEM
    kept = [
        ((2 * half_rows, features), bf16),
        ((size, rows, 2 * width), bf16),
        ((features, 2 * heads_width), bf16),
        ((LENGTH, groups * 4 * LANES), bf16),
        ((LENGTH, groups * 2 * LANES), bf16),
        ((half_rows, features), f32),
    ]
    fed = [
        ((size, rows, 2 * units), bf16),
        ((2 * half_rows, units), bf16),
        ((2 * half_rows, 2 * units), bf16),
    ]
    slots = shape((4, half_rows, features), bf16)
    rotary = jnp.asarray(spread(4, (1, 1, 1, 0)), bf16)
    plain = jnp.asarray(spread(columns // HEAD, (0,) * 4), bf16)
    return pl.pallas_call(
        functools.partial(begin_kernel, size),
        in_specs=[anywhere] + [vmem] * 6 + [anywhere] * 4 + [vmem],
        out_specs=[anywhere] * 12 + [vmem, vmem],
        out_shape=[shape(*one) for one in kept]
        + [slots, slots, shape(*fed[0]), shape((size, rows, units), bf16), shape(*fed[1]), shape(*fed[2])]
        + [shape((groups, 2, LENGTH), f32), shape((8, features), f32)],
        scratch_shapes=[
            buffer((half_rows, features), bf16),
            buffer((LENGTH, LANES), f32),
            buffer((LENGTH, LANES), f32),
            buffer(rotary.shape, bf16),
            buffer(plain.shape, bf16),
        ]
        + [buffer(*one) for one in kept + fed]
        + [
            buffer((size, rows, units), bf16),
            buffer((half_rows, features), bf16),
            buffer((size,) + gains.shape, f32),
            buffer((size, rows, 2 * columns), bf16),
            buffer((half_rows, features), bf16),
            buffer((half_rows, features), bf16),
            buffer((half_rows, features), bf16),
            dma((size - 1,)), dma((size - 1,)),
            dma((2, 2, half)), dma((2, 2, half)),
            dma((size,)), dma((size,)),
            dma((2, 2, half)), dma((2, 2, half)),
            dma((2, 2, half)), dma((2, 2, half)),
            dma((2, 2, half)), dma((2, 2, half)),
            dma((6,)),
            dma((3,)), dma((3,)),
            dma((3,)), dma((3,)),
            dma((7,)), dma((5,)), dma((11,)),
        ],
        compiler_params=pltpu.CompilerParams(collective_id=1, has_side_effects=True, vmem_limit_bytes=60 * 2**20),
        cost_estimate=pl.CostEstimate(flops=10**10, bytes_accessed=400 * 2**20, transcendentals=0),
        name="begin",
    )(
        tokens, cotangent, attend_shard, output_shard, gate_shard, up_shard, down_shard, jnp.asarray(cos),
        jnp.asarray(sin), rotary, plain, gains,
    )


class RingScatter:
    def __init__(self, places, partial, received, send, receive):
        self.places, self.partial, self.received = places, partial, received
        self.send, self.receive = send, receive
        self.rows = received.shape[2]
        self.cut = self.rows // 32 * 16
        self.sent = []

    def start(self, hop):
        places = self.places
        for way in range(2):
            rows = pl.ds(0, self.rows)
            if hop == 1:
                rows = (pl.ds(0, self.cut), pl.ds(self.cut, self.rows - self.cut))[way]
                source = self.partial(places.index(places.half)).at[rows]
            else:
                source = self.received.at[way, hop - 2]
            copy = remote(
                source,
                self.received.at[way, hop - 1, rows],
                self.send.at[way, hop - 1],
                self.receive.at[way, hop - 1],
                places.on_ring(1 - 2 * way),
            )
            copy.start()
            self.sent.append(copy)

    def wait(self, hop):
        self.sent[2 * hop - 2].wait_recv()
        self.sent[2 * hop - 1].wait_recv()

    def add(self, hop):
        distance = self.places.half - hop
        for way in range(2):
            own = self.partial(self.places.index(distance * (1 - 2 * way)))
            here = self.received.at[way, hop - 1]
            first, last = 0, self.rows
            if hop == 1:
                first, last = ((0, self.cut), (self.cut, last))[way]
                start, count = ((self.cut, self.rows - self.cut), (0, self.cut))[way]
                here[start : start + count, :] = own[start : start + count, :]
            size = min(last - first, 48)
            for start in range(first, last, size):
                rows = slice(start, min(start + size, last))
                here[rows, :] = here[rows, :] + own[rows, :]

    def step(self, hop):
        self.wait(hop)
        self.add(hop)
        self.start(hop + 1)

    def total(self, rows):
        half = self.places.half
        own = self.partial(self.places.index(0))
        return (
            own[rows, :].astype(jnp.float32)
            + self.received[0, half - 1, rows, :].astype(jnp.float32)
            + self.received[1, half - 1, rows, :].astype(jnp.float32)
        )

    def finish(self):
        for copy in self.sent:
            copy.wait_send()


def middle_kernel(
    size, two_slots, cot_slots, feed, down_hbm, inner_hbm, factors_hbm, hidden_hbm, gain_rows,
    late_grad, gate_sum, down_sum, hidden_grad, branch, far_out, near_out, out_got,
    two, cot, weights, down, inner, grads, down_grad, gate_grad, ring_got, outgoing, far_part, core_far, core_near,
    chip_got, stage, gate_stage, hidden, out_part, load_sem, stage_sem, down_send, down_receive, gate_send,
    gate_receive, send_sem, receive_sem, store_sem, credit,
):
    bf16, f32 = jnp.bfloat16, jnp.float32
    places = Places(size)
    half = places.half
    half_rows, features = hidden_hbm.shape
    rows = feed.shape[1]
    units = inner.shape[1]
    lane_half = units // 2
    greet([places.on_ring(1), places.on_ring(-1), places.chip(), places.core()])

    def lanes_of(number):
        return pl.ds(number * lane_half, lane_half)

    order = (2, 3, 0, 1)
    both_rows = 2 * half_rows
    near = pl.ds(0, both_rows)

    def rows_of(slot):
        return pl.ds(slot * half_rows, half_rows)

    fetch = {"weights": pltpu.make_async_copy(feed, weights, load_sem.at[0])}
    for number, slot in enumerate(order):
        fetch["two", slot] = pltpu.make_async_copy(two_slots.at[slot], two.at[rows_of(slot)], load_sem.at[1 + number])
        fetch["cot", slot] = pltpu.make_async_copy(cot_slots.at[slot], cot.at[rows_of(slot)], load_sem.at[5 + number])
    fetch["inner"] = pltpu.make_async_copy(inner_hbm, inner.at[near], load_sem.at[9])
    fetch["factors"] = pltpu.make_async_copy(factors_hbm, grads.at[near], load_sem.at[10])
    fetch["down"] = pltpu.make_async_copy(down_hbm, down, load_sem.at[11])
    for name in (
        "weights", ("two", 2), ("two", 3), ("cot", 2), ("cot", 3), "inner", ("cot", 0), ("cot", 1), "down", "factors",
        ("two", 0), ("two", 1),
    ):
        fetch[name].start()
    fetch["weights"].wait()
    block = 512

    def backward(slot):
        here = rows_of(slot)
        for number in range(units // block):
            lane = number * block
            weight = down[:, :, lane : lane + block].reshape(features, block)
            inner_grad = dot(cot[here, :], weight)
            for place in (slice(lane, lane + block), slice(units + lane, units + lane + block)):
                grads[here, place] = (inner_grad * grads[here, place].astype(f32)).astype(bf16)

    big = 256
    mine_start = places.side * half_rows
    theirs_start = (1 - places.side) * half_rows

    def two_terms(place):
        return dot(grads[place, :], weights[...].reshape(features, 2 * units), ((1,), (1,)))

    def out_terms(place):
        return dot(inner[place, :], down[...].reshape(features, units), ((1,), (1,)))

    def terms_to(target, start, terms):
        def tile(number, carry):
            value = terms(pl.ds(pl.multiple_of(start + number * big, big), big))
            target[pl.ds(pl.multiple_of(number * big, big), big), :] = value.astype(bf16)
            return carry

        lax.fori_loop(0, half_rows // big, tile, 0)

    def add_to(target, other):
        def tile(number, carry):
            place = pl.ds(pl.multiple_of(number * 32, 32), 32)
            target[place, :] = (target[place, :].astype(f32) + other[place, :].astype(f32)).astype(bf16)
            return carry

        lax.fori_loop(0, half_rows // 32, tile, 0)

    for slot in order[:2]:
        fetch["two", slot].wait()
        for number in range(units // block):
            hidden_units(two.at[rows_of(slot)], weights, inner, grads, rows_of(slot), units, number)
    fetch["inner"].wait()
    for slot in order:
        fetch["cot", slot].wait()

    span = 384
    per_span = span // rows

    def down_tile(number, carry):
        lanes = pl.ds(pl.multiple_of(number * span, span), span)
        value = dot(cot[:, lanes], inner[...], ((0,), (0,))).astype(bf16)
        down_grad[pl.ds(number * per_span, per_span)] = value.reshape(per_span, rows, units)
        return carry

    spans = features // span
    lax.fori_loop(0, spans, down_tile, 0)

    def scatter_of(array, send, receive, parts=2):
        lane_part = array.shape[2] // parts
        return Parts([
            RingScatter(
                places,
                lambda slot, number=number: array.at[slot, :, pl.ds(number * lane_part, lane_part)],
                ring_got.at[:, :, :, pl.ds(number * lane_part, lane_part)],
                send.at[number],
                receive.at[number],
            )
            for number in range(parts)
        ])

    ring = scatter_of(down_grad, down_send, down_receive)
    ring.start(1)
    fetch["down"].wait()
    for slot in order[:2]:
        backward(slot)
    terms_to(outgoing, both_rows + theirs_start, two_terms)
    far_swap = remote(outgoing, core_far, send_sem.at[0], receive_sem.at[0], places.core())
    far_swap.start()
    ring.step(1)
    terms_to(far_part, both_rows + mine_start, two_terms)
    far_swap.wait()
    add_to(far_part, core_far)
    chip_swap = remote(far_part, chip_got, send_sem.at[1], receive_sem.at[1], places.chip())
    chip_swap.start()
    fetch["factors"].wait()
    for slot in order[2:]:
        backward(slot)
    ring.step(2)
    for slot in order[2:]:
        fetch["two", slot].wait()

    def late_copy(number):
        place = pl.ds(pl.multiple_of(number * span, span), span)
        return pltpu.make_async_copy(gate_stage, late_grad.at[place, pl.ds(0, lane_half)], stage_sem.at[2])

    def gate_tile(number, carry):
        lanes = pl.ds(pl.multiple_of(number * span, span), span)
        value = dot(two[:, lanes], grads[:, :units], ((0,), (0,))).astype(bf16)
        gate_grad[pl.ds(number * per_span, per_span)] = value[:, :lane_half].reshape(per_span, rows, lane_half)

        @pl.when(number > 0)
        def _():
            late_copy(number - 1).wait()

        gate_stage[...] = value[:, lane_half:]
        late_copy(number).start()
        return carry

    lax.fori_loop(0, spans, gate_tile, 0)
    for hop in range(3, half):
        ring.step(hop)
    terms_to(outgoing, theirs_start, two_terms)
    near_swap = remote(outgoing, core_near, send_sem.at[2], receive_sem.at[2], places.core())
    near_swap.start()
    ring.wait(half)

    def total_to(target, sums, lane_part):
        def tile(number, carry):
            place = pl.ds(pl.multiple_of(number * 16, 16), 16)
            for part, one in enumerate(sums.rings):
                target[place, part * lane_part : (part + 1) * lane_part] = one.total(place)
            return carry

        lax.fori_loop(0, rows // 16, tile, 0)

    total_to(down_sum, ring, lane_half)
    ring.finish()
    for step in (1, -1):
        pl.semaphore_signal(credit, inc=1, device_id=places.on_ring(step), device_id_type=MESH)
    pl.semaphore_wait(credit, 2)
    ring = scatter_of(gate_grad, gate_send, gate_receive)
    ring.start(1)

    def stage_copy(number, side):
        place = pl.ds(pl.multiple_of(number * span, span), span)
        return pltpu.make_async_copy(stage.at[side], late_grad.at[place, pl.ds(lane_half, units)], stage_sem.at[side])

    def up_tile(pair, carry):
        for side in range(2):
            number = 2 * pair + side
            lanes = pl.ds(pl.multiple_of(number * span, span), span)
            value = dot(two[:, lanes], grads[:, units:], ((0,), (0,))).astype(bf16)

            @pl.when(pair > 0)
            def _(side=side, number=number):
                stage_copy(number - 2, side).wait()

            stage[side] = value
            stage_copy(number, side).start()
        return carry

    lax.fori_loop(0, spans // 2, up_tile, 0)
    ring.step(1)

    near_swap.wait()
    terms_to(outgoing, both_rows + theirs_start, out_terms)
    far_swap = remote(outgoing, core_far, send_sem.at[5], receive_sem.at[5], places.core())
    far_swap.start()
    chip_swap.wait()
    terms_to(far_part, both_rows + mine_start, out_terms)
    far_swap.wait()
    add_to(far_part, core_far)
    store_far = pltpu.make_async_copy(far_part, far_out, store_sem.at[0])
    store_far.start()
    out_rows = half_rows // 2
    out_swap = remote(
        far_part.at[pl.ds(0, out_rows)], out_part, send_sem.at[7], receive_sem.at[7], places.chip()
    )
    out_swap.start()
    ring.step(2)

    sends = []
    for number in range(half_rows // big):
        here = pl.ds(number * big, big)
        if number > 0:
            store_grad.wait()
        load_hidden = pltpu.make_async_copy(hidden_hbm.at[here], hidden, load_sem.at[12])
        load_hidden.start()
        place = pl.ds(pl.multiple_of(mine_start + number * big, big), big)
        value = two_terms(place) + core_near[here, :].astype(f32) + chip_got[here, :].astype(f32)
        load_hidden.wait()
        values = hidden[...]
        inverse = lax.rsqrt(jnp.mean(values * values, axis=1, keepdims=True) + norm_eps)
        scaled = value * gain_rows[1:2, :]
        mean = jnp.mean(scaled * values, axis=1, keepdims=True)
        total = cot[place, :].astype(f32) + inverse * scaled - values * (inverse * inverse * inverse) * mean
        hidden[...] = total
        chip_got[here, :] = total.astype(bf16)
        store_grad = pltpu.make_async_copy(hidden, hidden_grad.at[here], store_sem.at[1])
        store_grad.start()
        keep = pltpu.make_async_copy(chip_got.at[here], two.at[place], store_sem.at[2 + number])
        send = remote(chip_got.at[here], two.at[place], send_sem.at[3 + number], receive_sem.at[3 + number], places.core())
        keep.start()
        send.start()
        sends += [keep, send]
    store_grad.wait()

    terms_to(outgoing, theirs_start, out_terms)
    for copy in sends:
        copy.wait()
    store_branch = pltpu.make_async_copy(two.at[near], branch, store_sem.at[5])
    store_branch.start()
    near_swap = remote(outgoing, core_near, send_sem.at[6], receive_sem.at[6], places.core())
    near_swap.start()
    for number in range(half_rows // big):
        here = pl.ds(number * big, big)
        if number > 0:
            store_near.wait()
        load_hidden = pltpu.make_async_copy(hidden_hbm.at[here], hidden, load_sem.at[12])
        load_hidden.start()
        value = out_terms(pl.ds(pl.multiple_of(mine_start + number * big, big), big))
        load_hidden.wait()
        if number == 0:
            near_swap.wait()
        hidden[...] = value + hidden[...] + core_near[here, :].astype(f32)
        store_near = pltpu.make_async_copy(hidden, near_out.at[here], store_sem.at[4])
        store_near.start()
    for hop in range(3, half):
        ring.step(hop)
    ring.wait(half)
    total_to(gate_sum, ring, lane_half // 2)
    ring.finish()
    late_copy(spans - 1).wait()
    store_near.wait()
    store_far.wait()
    for side in range(2):
        stage_copy(spans - 2 + side, side).wait()
    store_branch.wait()
    out_swap.wait()
    store_out = pltpu.make_async_copy(out_part, out_got, store_sem.at[6])
    store_out.start()
    store_out.wait()


def middle(size, two_slots, cot_slots, feed, down, inner, factors, hidden_state, gain_rows):
    half_rows, features = hidden_state.shape
    rows, width = feed.shape[1:]
    units = width // 2
    vmem = pl.BlockSpec(memory_space=pltpu.VMEM)
    anywhere = pl.BlockSpec(memory_space=pl.ANY)
    dma = pltpu.SemaphoreType.DMA
    half = size // 2
    bf16, f32 = jnp.bfloat16, jnp.float32
    shape = jax.ShapeDtypeStruct
    buffer = pltpu.VMEM
    return pl.pallas_call(
        functools.partial(middle_kernel, size),
        in_specs=[anywhere] * 7 + [vmem],
        out_specs=[anywhere, vmem, vmem] + [anywhere] * 5,
        out_shape=[
            shape((features, units // 2 + units), bf16),
            shape((rows, units // 2), f32),
            shape((rows, units), f32),
            shape((half_rows, features), f32),
            shape((2 * half_rows, features), bf16),
            shape((half_rows, features), bf16),
            shape((half_rows, features), f32),
            shape((half_rows // 2, features), bf16),
        ],
        scratch_shapes=[
            buffer((4 * half_rows, features), bf16),
            buffer((4 * half_rows, features), bf16),
            buffer(feed.shape, bf16),
            buffer((size, rows, units), bf16),
            buffer((4 * half_rows, units), bf16),
            buffer((4 * half_rows, 2 * units), bf16),
            buffer((size, rows, units), bf16),
            buffer((size, rows, units // 2), bf16),
            buffer((2, half, rows, units), bf16),
            buffer((half_rows, features), bf16),
            buffer((half_rows, features), bf16),
            buffer((half_rows, features), bf16),
            buffer((half_rows, features), bf16),
            buffer((half_rows, features), bf16),
            buffer((2, 384, units), bf16),
            buffer((384, units // 2), bf16),
            buffer((256, features), f32),
            buffer((half_rows // 2, features), bf16),
            dma((13,)),
            dma((3,)),
            dma((2, 2, half)), dma((2, 2, half)),
            dma((2, 2, half)), dma((2, 2, half)),
            dma((8,)), dma((8,)),
            dma((7,)),
            pltpu.SemaphoreType.REGULAR,
        ],
        compiler_params=pltpu.CompilerParams(collective_id=3, has_side_effects=True, vmem_limit_bytes=63 * 2**20),
        cost_estimate=pl.CostEstimate(flops=6 * 10**10, bytes_accessed=300 * 2**20, transcendentals=0),
        name="middle",
    )(two_slots, cot_slots, feed, down, inner, factors, hidden_state, gain_rows)


def finish_kernel(
    size, tokens_hbm, hidden_hbm, branch_hbm, normed_hbm, weights_hbm, output_hbm, qkv_hbm, att_hbm, up_hbm, up_shard,
    gate_hbm, gate_shard, far_out, near_hbm, first_out, log_ref, gain_rows, attend_shard, cos_ref, sin_ref,
    rotary_spread, plain_spread,
    tokens_grad, query_sum, key_sum, value_sum, output_sum, up_sum, gate_out, gain_sum, layer_out, second_out,
    branch, grad_ref, back, dq_ref, dk_ref, dv_ref, own_grad, other_grad, crossed, ring_got, output_grad, output_got,
    output_crossed, up_grad, up_got, terms, got_terms, output_own, output_across, gain_parts, gate_sum, gate_part, up_part,
    normed, weights, output_spread, qkv_two, att_ref, tokens, hidden_grad, load_sem,
    ring_send, ring_receive, out_send, out_receive, up_send, up_receive, cross_send, cross_receive, across,
    gain_send, gain_receive,
):
    bf16, f32 = jnp.bfloat16, jnp.float32
    places = Places(size)
    half, own = places.half, places.own
    half_rows, features = tokens_hbm.shape
    rows = attend_shard.shape[0]
    units = up_hbm.shape[1] * 2 // 3
    lane_half = units // 2
    span = 4 * HEAD
    big = 256
    diagonal = (own, 3 - places.tensor)
    group_order = (2, 3, 0, 1)
    greet([places.on_ring(1), places.on_ring(-1), places.chip(), places.core(), diagonal])

    out_rows = half_rows // 2
    out_swap = remote(
        far_out.at[pl.ds(out_rows, out_rows)], second_out, across.at[0], across.at[1], places.chip()
    )

    out_swap.start()

    def qkv_load(number):
        lanes = pl.ds(group_order[number] * 4 * LANES, 4 * LANES)
        return pltpu.make_async_copy(qkv_hbm.at[:, lanes], qkv_two.at[number % 2], load_sem.at[number])

    def row_loads(first, second, number):
        here = pl.ds(number * big, big)
        return (
            pltpu.make_async_copy(first.at[here], tokens, load_sem.at[4]),
            pltpu.make_async_copy(second.at[here], hidden_grad, load_sem.at[5]),
        )

    fetch = {
        "up": pltpu.make_async_copy(up_hbm, up_grad, load_sem.at[11]),
        "branch": pltpu.make_async_copy(branch_hbm, branch, load_sem.at[6]),
        "output": pltpu.make_async_copy(output_hbm, output_spread, load_sem.at[7]),
        "att": pltpu.make_async_copy(att_hbm, att_ref, load_sem.at[8]),
        "normed": pltpu.make_async_copy(normed_hbm, normed, load_sem.at[9]),
        "weights": pltpu.make_async_copy(weights_hbm, weights, load_sem.at[10]),
        "gate_sum": pltpu.make_async_copy(gate_hbm, gate_sum, load_sem.at[12]),
        "gate_part": pltpu.make_async_copy(gate_shard, gate_part, load_sem.at[13]),
        "up_part": pltpu.make_async_copy(up_shard, up_part, load_sem.at[14]),
    }
    fetch["up"].start()
    fetch["branch"].start()
    fetch["output"].start()
    qkv_loads = [qkv_load(number) for number in range(4)]
    qkv_loads[0].start()
    for name in ("att", "normed", "weights", "gate_sum", "gate_part", "up_part"):
        fetch[name].start()
    token_rows = row_loads(tokens_hbm, hidden_hbm, 0)
    for copy in token_rows:
        copy.start()

    def lanes_of(number, count):
        return pl.ds(number * count, count)

    ups = Parts([
        RingScatter(
            places,
            lambda slot, number=number: up_grad.at[
                pl.ds(pl.multiple_of(slot * rows, rows), rows), lanes_of(number, lane_half)
            ],
            up_got.at[:, :, :, lanes_of(number, lane_half)],
            up_send.at[number],
            up_receive.at[number],
        )
        for number in range(3)
    ])
    fetch["up"].wait()
    ups.start(1)
    fetch["branch"].wait()
    fetch["output"].wait()
    fetch["att"].wait()

    def back_group(number, target, lane, between):
        group = group_order[number]
        qkv_loads[number].wait()
        if number < 3:
            qkv_loads[number + 1].start()
        qkv_ref = qkv_two.at[number % 2]
        base = 0
        for part in range(2):
            block = pl.ds(part * half_rows, half_rows)
            value = dot(branch[block, :], output_spread[:, group * 2 * LANES : (group + 1) * 2 * LANES])
            grad_ref[block, :] = value.astype(bf16)
        turned = qkv_ref[:, base + 2 * LANES : base + 3 * LANES].T
        cos, sin = cos_ref[...], sin_ref[...]
        scale = HEAD**-0.5

        def unrot(u):
            return (u * cos - pltpu.roll(u, 64, 1) * sin).astype(bf16)

        key_place = lax.broadcasted_iota(jnp.int32, (QB, QB), 0)
        query_place = lax.broadcasted_iota(jnp.int32, (QB, QB), 1)
        for head in range(2):
            lanes = slice(head * LANES, (head + 1) * LANES)
            att_lane = (2 * group + head) * LANES
            prod = grad_ref[:, lanes].astype(f32) * att_ref[:, att_lane : att_lane + LANES].astype(f32)
            delta = jnp.sum(prod.T, axis=0, keepdims=True)
            for block in reversed(range(LENGTH // QB)):
                first, last = block * QB, (block + 1) * QB
                query = qkv_ref[first:last, base + head * LANES : base + (head + 1) * LANES]
                out_grad = grad_ref[first:last, lanes]
                score = dot(qkv_ref[:last, base + 2 * LANES : base + 3 * LANES], query, ((1,), (1,)))
                prob = jnp.exp2(score * C2 - log_ref[group, head : head + 1, first:last])
                edge = jnp.where(key_place <= query_place, prob[first:], 0.0)
                prob = jnp.concatenate([prob[:first], edge], axis=0) if block else edge
                prob_grad = dot(qkv_ref[:last, base + 3 * LANES : base + 4 * LANES], out_grad, ((1,), (1,)))
                score_grad = (prob * (prob_grad - delta[:, first:last])).astype(bf16)
                key_part = dot(score_grad, query)
                value_part = dot(prob.astype(bf16), out_grad)
                if head == 0 and block == LENGTH // QB - 1:
                    dk_ref[...] = key_part
                    dv_ref[...] = value_part
                else:
                    dk_ref[:last] += key_part
                    dv_ref[:last] += value_part
                dq_ref[first:last, lanes] = dot(turned[:, :last], score_grad).T
            if head == 0:
                between()
        wide = jnp.concatenate(
            [
                unrot(dq_ref[:, :LANES] * scale),
                unrot(dq_ref[:, LANES:] * scale),
                unrot(dk_ref[...] * scale),
                dv_ref[...].astype(bf16),
            ],
            axis=1,
        )
        close_back = dot(wide, rotary_spread[...], ((1,), (1,))).astype(bf16)
        back[:, group * span : (group + 1) * span] = close_back
        if number == 0:
            fetch["normed"].wait()
        for part in range(2):
            block = slice(part * features // 2, (part + 1) * features // 2)
            value = dot(normed[:, block], close_back, ((0,), (0,))).astype(bf16)
            target[part * size // 2 : (part + 1) * size // 2, :, lane : lane + span] = value.reshape(
                size // 2, rows, span
            )

    order = [half]
    for step in range(half - 1, 0, -1):
        order += [step, -step]
    order.append(0)
    crossing = {}

    def cross(group):
        for number, step in enumerate(order):
            slot = places.index(step)
            lanes = pl.ds(group * span, span)
            copy = remote(
                other_grad.at[slot, :, lanes], crossed.at[slot, :, lanes],
                cross_send.at[group, number], cross_receive.at[group, number], places.chip(),
            )
            copy.start()
            crossing[(group, step)] = copy

    heads_width = output_spread.shape[1] // 2
    columns = heads_width // LANES * HEAD
    kept = LANES
    sent_on = columns - kept
    for side in (1, 0):
        close = dot(
            att_ref[:, side * heads_width : (side + 1) * heads_width], plain_spread[...], ((1,), (1,))
        ).astype(bf16)
        for part in range(2):
            block = slice(part * features // 2, (part + 1) * features // 2)
            value = dot(branch[:, block], close, ((0,), (0,))).astype(bf16)
            output_grad[part * size // 2 : (part + 1) * size // 2, :, side * columns : (side + 1) * columns] = (
                value.reshape(size // 2, rows, columns)
            )
    out_crossing = {}
    for number, step in enumerate(order):
        slot = places.index(step)
        copy = remote(
            output_grad.at[slot, :, pl.ds(columns + kept, sent_on)], output_crossed.at[slot],
            cross_send.at[2, number], cross_receive.at[2, number], places.chip(),
        )
        copy.start()
        out_crossing[step] = copy

    def prepare_output(step):
        out_crossing[step].wait_recv()
        slot = places.index(step)
        for start in range(0, rows, 48):
            place = slice(start, start + 48)
            output_grad[slot, place, kept:columns] = output_grad[slot, place, kept:columns] + output_crossed[slot, place, :]

    ring_width = (columns + kept) // 2
    outputs = Parts([
        RingScatter(
            places,
            lambda slot, number=number: output_grad.at[slot, :, lanes_of(number, ring_width)],
            output_got.at[:, :, :, lanes_of(number, ring_width)],
            out_send.at[number],
            out_receive.at[number],
        )
        for number in range(2)
    ])

    def output_step(hop):
        prepare_output(half - hop)
        prepare_output(hop - half)
        outputs.step(hop)

    micro = [(ring, hop) for hop in range(1, half) for ring in ups.rings]

    def serve(count):
        for _ in range(min(count, len(micro))):
            ring, hop = micro.pop(0)
            ring.step(hop)

    serve(1)
    back_group(0, other_grad, 0, lambda: serve(2))
    cross(0)
    serve(1)
    back_group(1, other_grad, span, lambda: serve(2))
    cross(1)
    serve(1)

    def late_start():
        serve(1)
        prepare_output(half)
        outputs.start(1)

    back_group(2, own_grad, 0, late_start)
    serve(len(micro))
    back_group(3, own_grad, span, lambda: output_step(1))
    if half > 2:
        output_step(2)

    def prepare(group, step):
        crossing[(group, step)].wait_recv()
        slot = places.index(step)
        lanes = slice(group * span, (group + 1) * span)
        for start in range(0, rows, 48):
            place = slice(start, start + 48)
            crossed[slot, place, lanes] = crossed[slot, place, lanes] + own_grad[slot, place, lanes]

    attend = [
        RingScatter(
            places,
            lambda slot, number=number: crossed.at[slot, :, lanes_of(number, span)],
            ring_got.at[:, :, :, lanes_of(number, span)],
            ring_send.at[number],
            ring_receive.at[number],
        )
        for number in range(2)
    ]

    def attend_start(group):
        prepare(group, half)
        attend[group].start(1)

    def attend_step(group, hop):
        prepare(group, half - hop)
        prepare(group, hop - half)
        attend[group].step(hop)

    attend_start(0)
    whole = weights.shape[2]
    fetch["weights"].wait()

    def terms_of(block):
        return dot(back[block, :], weights[...].reshape(features, whole), ((1,), (1,)))

    def theirs_tile(number, carry):
        place = (1 - places.side) * half_rows + number * big
        value = terms_of(pl.ds(pl.multiple_of(place, big), big))
        terms[pl.ds(pl.multiple_of(number * big, big), big), :] = value.astype(bf16)
        return carry

    lax.fori_loop(0, half_rows // big, theirs_tile, 0)
    terms_swap = remote(terms, got_terms, across.at[2], across.at[3], places.core())
    terms_swap.start()
    attend_step(0, 1)
    for hop in range(3, half):
        output_step(hop)
    terms_swap.wait()
    for number in range(half_rows // big):
        for copy in token_rows:
            copy.wait()
        here = slice(number * big, (number + 1) * big)
        place = places.side * half_rows + number * big
        value = terms_of(pl.ds(pl.multiple_of(place, big), big)) + got_terms[here, :].astype(f32)
        values = tokens[...].astype(f32)
        inverse = lax.rsqrt(jnp.mean(values * values, axis=1, keepdims=True) + norm_eps)
        scaled = value * gain_rows[0:1, :]
        inner = jnp.mean(scaled * values, axis=1, keepdims=True)
        result = hidden_grad[...] + inverse * scaled - values * (inverse * inverse * inverse) * inner
        tokens_grad[here, :] = result.astype(bf16)
        if number < half_rows // big - 1:
            token_rows = row_loads(tokens_hbm, hidden_hbm, number + 1)
            for copy in token_rows:
                copy.start()
        if number == 0 and half > 2:
            attend_step(0, 2)
    attend_start(1)
    for hop in range(3, half):
        attend_step(0, hop)
    prepare(0, 0)

    prepare_output(0)
    outputs.wait(half)

    for start in range(0, rows, 48):
        place = slice(start, start + 48)
        late = outputs.rings[1].total(place)
        output_own[place, :ring_width] = outputs.rings[0].total(place)
        output_own[place, ring_width:] = late[:, : columns - ring_width]
        output_across[0, place, :] = late[:, columns - ring_width :].astype(bf16)
    output_swap = remote(output_across.at[0], output_across.at[1], across.at[4], across.at[5], places.chip())
    output_swap.start()
    attend_step(1, 1)
    ups.wait(half)
    for name in ("gate_sum", "gate_part", "up_part"):
        fetch[name].wait()

    def up_tile(number, carry):
        place = pl.ds(pl.multiple_of(number * 16, 16), 16)
        early = gate_sum[place, :]
        gate_out[place, :lane_half] = early
        gain = jnp.sum(early * gate_part[place, :lane_half].astype(f32), axis=1, keepdims=True)
        late = (
            (gate_out, gate_part, lane_half, 0), (up_sum, up_part, 0, 1), (up_sum, up_part, lane_half, 2),
        )
        for target, weight, lane, part in late:
            lanes = slice(lane, lane + lane_half)
            value = ups.rings[part].total(place)
            target[place, lanes] = value
            gain += jnp.sum(value * weight[place, lanes].astype(f32), axis=1, keepdims=True)
        lane = lax.broadcasted_iota(jnp.int32, (16, LANES), 1)
        gain_parts[0, place, :] = jnp.where(lane == 1, gain, 0.0)
        return carry

    lax.fori_loop(0, rows // 16, up_tile, 0)
    if half > 2:
        attend_step(1, 2)
    for hop in range(3, half):
        attend_step(1, hop)
    prepare(1, 0)

    out_swap.wait()
    for number in range(half_rows // big):
        here = pl.ds(number * big, big)
        source = first_out if number < half_rows // big // 2 else second_out
        rest = pl.ds(number * big % out_rows, big)
        share = pltpu.make_async_copy(source.at[rest], tokens, load_sem.at[4])
        near = pltpu.make_async_copy(near_hbm.at[here], hidden_grad, load_sem.at[5])
        share.start()
        near.start()
        share.wait()
        near.wait()
        tokens[...] = (hidden_grad[...] + tokens[...].astype(f32)).astype(bf16)
        store = pltpu.make_async_copy(tokens, layer_out.at[here], load_sem.at[15])
        store.start()
        store.wait()
    output_swap.wait()
    output_sum[:, :kept] = output_own[:, :kept] + output_across[1].astype(f32)
    output_sum[:, kept:] = output_own[:, kept:]
    for part in range(2):
        attend[part].wait(half)

    def attend_tile(number, carry):
        place = pl.ds(pl.multiple_of(number * 16, 16), 16)
        gain = jnp.zeros((16, 1), f32)
        for part in range(2):
            value = attend[part].total(place)
            query_sum[place, part * 2 * HEAD : (part + 1) * 2 * HEAD] = value[:, : 2 * HEAD]
            key_sum[place, part * HEAD : (part + 1) * HEAD] = value[:, 2 * HEAD : 3 * HEAD]
            value_sum[place, part * HEAD : (part + 1) * HEAD] = value[:, 3 * HEAD :]
            gain += jnp.sum(
                value * attend_shard[place, part * span : (part + 1) * span].astype(f32), axis=1, keepdims=True
            )
        lane = lax.broadcasted_iota(jnp.int32, (16, LANES), 1)
        gain_parts[0, place, :] += jnp.where(lane == 0, gain, 0.0)
        return carry

    lax.fori_loop(0, rows // 16, attend_tile, 0)
    gain_copies = []
    for number, device in enumerate((places.core(), places.chip(), diagonal)):
        copy = remote(
            gain_parts.at[0], gain_parts.at[1 + number], gain_send.at[number], gain_receive.at[number], device
        )
        copy.start()
        gain_copies.append(copy)
    for copy in list(crossing.values()) + list(out_crossing.values()):
        copy.wait_send()
    ups.finish()
    outputs.finish()
    for ring in attend:
        ring.finish()
    for copy in gain_copies:
        copy.wait()
    gain_sum[...] = (gain_parts[0] + gain_parts[1]) + (gain_parts[2] + gain_parts[3])


def finish(
    size, tokens, hidden_grad, branch, normed, weights, output_spread, qkv, att, logs, gain_rows, up_grad, up_shard,
    gate_sum, gate_shard, attend_shard, far_out, near_out, first_out,
):
    half_rows, features = tokens.shape
    rows, width = attend_shard.shape
    columns = output_spread.shape[1] // 2 // LANES * HEAD
    units = up_shard.shape[1]
    vmem = pl.BlockSpec(memory_space=pltpu.VMEM)
    anywhere = pl.BlockSpec(memory_space=pl.ANY)
    dma = pltpu.SemaphoreType.DMA
    half = size // 2
    bf16, f32 = jnp.bfloat16, jnp.float32
    cos, sin = rope_tables()
    shape = jax.ShapeDtypeStruct
    buffer = pltpu.VMEM
    return pl.pallas_call(
        functools.partial(finish_kernel, size),
        in_specs=[anywhere] * 15 + [vmem] * 7,
        out_specs=[vmem] * 8 + [anywhere] * 2,
        out_shape=[
            shape((half_rows, features), bf16),
            shape((rows, width // 2), f32),
            shape((rows, width // 4), f32),
            shape((rows, width // 4), f32),
            shape((rows, columns), f32),
            shape((rows, units), f32),
            shape((rows, units), f32),
            shape((rows, LANES), f32),
            shape((half_rows, features), bf16),
            shape((half_rows // 2, features), bf16),
        ],
        scratch_shapes=[
            buffer((LENGTH, features), bf16),
            buffer((LENGTH, 2 * LANES), bf16),
            buffer((LENGTH, 2 * width), bf16),
            buffer((LENGTH, 2 * LANES), f32),
            buffer((LENGTH, LANES), f32),
            buffer((LENGTH, LANES), f32),
            buffer((size, rows, width), bf16),
            buffer((size, rows, width), bf16),
            buffer((size, rows, width), bf16),
            buffer((2, half, rows, width), bf16),
            buffer((size, rows, 2 * columns), bf16),
            buffer((2, half, rows, columns + LANES), bf16),
            buffer((size, rows, columns - LANES), bf16),
            buffer(up_grad.shape, bf16),
            buffer((2, half, rows, up_grad.shape[1]), bf16),
            buffer((half_rows, features), bf16),
            buffer((half_rows, features), bf16),
            buffer((rows, columns), f32),
            buffer((2, rows, LANES), bf16),
            buffer((4, rows, LANES), f32),
            buffer(gate_sum.shape, f32),
            buffer((rows, units), bf16),
            buffer((rows, units), bf16),
            buffer((LENGTH, features), bf16),
            buffer(weights.shape, bf16),
            buffer(output_spread.shape, bf16),
            buffer((2, LENGTH, 4 * LANES), bf16),
            buffer(att.shape, bf16),
            buffer((256, features), bf16),
            buffer((256, features), f32),
            dma((16,)),
            dma((2, 2, half)), dma((2, 2, half)),
            dma((2, 2, half)), dma((2, 2, half)),
            dma((3, 2, half)), dma((3, 2, half)),
            dma((3, size)), dma((3, size)),
            dma((6,)),
            dma((3,)), dma((3,)),
        ],
        compiler_params=pltpu.CompilerParams(collective_id=2, has_side_effects=True, vmem_limit_bytes=63 * 2**20),
        cost_estimate=pl.CostEstimate(flops=3 * 10**10, bytes_accessed=300 * 2**20, transcendentals=0),
        name="finish",
    )(
        tokens, hidden_grad, branch, normed, weights, output_spread, qkv, att, up_grad, up_shard, gate_sum, gate_shard,
        far_out, near_out, first_out, logs, gain_rows, attend_shard, jnp.asarray(cos), jnp.asarray(sin),
        jnp.asarray(spread(4, (1, 1, 1, 0)), bf16), jnp.asarray(spread(4, (0,) * 4), bf16),
    )


def local(
    dp_size,
    tokens,
    first_gain,
    query_weight,
    key_weight,
    value_weight,
    output_weight,
    second_gain,
    gate_weight,
    up_weight,
    down_weight,
    cotangent,
):
    f32 = jnp.float32
    groups = key_weight.shape[1] // HEAD
    packs = []
    for group in range(groups):
        packs.append(query_weight[:, group * 2 * HEAD : (group + 1) * 2 * HEAD])
        packs.append(key_weight[:, group * HEAD : (group + 1) * HEAD])
        packs.append(value_weight[:, group * HEAD : (group + 1) * HEAD])
    attend_shard = jnp.concatenate(packs, axis=1)
    lanes = LANES * pl.cdiv(first_gain.shape[0], LANES)
    both_gains = jnp.stack([first_gain, second_gain]).astype(f32)
    both_gains = jnp.pad(both_gains, ((0, 6), (0, lanes - first_gain.shape[0])))
    (
        normed, weights, output_spread, qkv, attended, hidden_state, two_slots, cot_slots, feed, down, inner, factors,
        logs, gain_rows,
    ) = begin(
        dp_size, tokens, cotangent, both_gains, attend_shard, output_weight.T, gate_weight, up_weight, down_weight.T
    )
    late_grad, gate_sum, down_sum, hidden_grad, branch, far_out, near_out, first_out = middle(
        dp_size, two_slots, cot_slots, feed, down, inner, factors, hidden_state, gain_rows
    )
    tokens_grad, query_sum, key_sum, value_sum, output_sum, up_sum, gate_sum, gain_sums, layer_out, _ = finish(
        dp_size, tokens, hidden_grad, branch, normed, weights, output_spread, qkv, attended, logs, gain_rows,
        late_grad, up_weight, gate_sum, gate_weight, attend_shard, far_out, near_out, first_out,
    )
    return (
        layer_out,
        tokens_grad,
        gain_sums[:, 0] / first_gain.astype(f32),
        query_sum,
        key_sum,
        value_sum,
        output_sum.T,
        gain_sums[:, 1] / second_gain.astype(f32),
        gate_sum,
        up_sum,
        down_sum.T,
    )


def solution(mesh):
    in_specs = (
        P(("dp", "tensor"), None),
        P("dp"),
        P("dp", "tensor"),
        P("dp", "tensor"),
        P("dp", "tensor"),
        P("tensor", "dp"),
        P("dp"),
        P("dp", "tensor"),
        P("dp", "tensor"),
        P("tensor", "dp"),
        P(("dp", "tensor"), None),
    )
    out_specs = (
        P(("dp", "tensor"), None),
        P(("dp", "tensor"), None),
        P("dp"),
        P("dp", "tensor"),
        P("dp", "tensor"),
        P("dp", "tensor"),
        P("tensor", "dp"),
        P("dp"),
        P("dp", "tensor"),
        P("dp", "tensor"),
        P("tensor", "dp"),
    )
    body = functools.partial(local, mesh.shape["dp"])
    return jax.shard_map(body, mesh=mesh, in_specs=in_specs, out_specs=out_specs, check_vma=False)
```

```python
import functools

import jax
import jax.numpy as jnp
import numpy as np
from jax import lax
from jax.experimental import pallas as pl
from jax.experimental.pallas import tpu as pltpu
from jax.sharding import PartitionSpec as P

HEAD = 96
LENGTH = 1024
LANES = 128
QB = 256
norm_eps = 1e-05
rope_base = 100000.0


def rope_tables():
    half = HEAD // 2
    freq = rope_base ** (np.arange(half, dtype=np.float64) * (-2.0 / HEAD))
    turned = np.arange(LENGTH, dtype=np.float64)[:, None] * freq[None, :]
    cos = np.zeros((LENGTH, LANES), np.float32); sin = np.zeros((LENGTH, LANES), np.float32)
    cos[:, :half] = np.cos(turned); cos[:, 64:64+half] = np.cos(turned)
    sin[:, :half] = -np.sin(turned); sin[:, 64:64+half] = np.sin(turned)
    return cos, sin

def spread(heads, rotary):
    e = np.zeros((heads * HEAD, heads * LANES), np.float32)
    for h in range(heads):
        for i in range(HEAD):
            lane = i if (not rotary[h] or i < 48) else i + 16
            e[h * HEAD + i, h * LANES + lane] = 1
    return e

def dot(a, b, dims=((1,), (0,))):
    return lax.dot_general(a, b, (dims, ((), ())), preferred_element_type=jnp.float32)

C2 = float(HEAD ** -0.5 * np.log2(np.e))


MESH = pl.DeviceIdType.MESH


class Places:
    def __init__(self, size):
        self.size = size
        self.half = size // 2
        self.own = lax.axis_index("dp")
        self.tensor = lax.axis_index("tensor")
        self.side = self.tensor % 2
        odd = self.own % 2
        self.place = (1 - odd) * (self.own // 2) + odd * (size - 1 - self.own // 2)

    def index(self, step):
        place = (self.place + step + self.size) % self.size
        late = place // self.half
        return (1 - late) * 2 * place + late * (2 * (self.size - 1 - place) + 1)

    def on_ring(self, step):
        return (self.index(step), self.tensor)

    def peer(self, step):
        return ((self.own + step + self.size) % self.size, self.tensor)

    def chip(self):
        return (self.own, (self.tensor + 2) % 4)

    def core(self):
        return (self.own, self.tensor + 1 - 2 * self.side)


def remote(source, target, send, receive, device):
    return pltpu.make_async_remote_copy(
        src_ref=source,
        dst_ref=target,
        send_sem=send,
        recv_sem=receive,
        device_id=device,
        device_id_type=MESH,
    )


def greet(devices):
    barrier = pltpu.get_barrier_semaphore()
    for device in devices:
        pl.semaphore_signal(barrier, inc=1, device_id=device, device_id_type=MESH)
    pl.semaphore_wait(barrier, len(devices))


class RingGather:
    def __init__(self, places, slots, send, receive):
        self.places, self.slots, self.send, self.receive = places, slots, send, receive
        self.cut = slots.shape[1] // 32 * 16
        self.sent = []

    def start(self, hop, source=None):
        places, half = self.places, self.places.half
        for way, (step, device) in enumerate(
            ((1 - hop, places.on_ring(1)), (hop - 1, places.on_ring(-1)))
        ):
            slot = places.index(step)
            rows = pl.ds(0, self.slots.shape[1])
            if hop == half:
                rows = (pl.ds(0, self.cut), pl.ds(self.cut, self.slots.shape[1] - self.cut))[way]
            view = self.slots.at[slot, rows]
            copy = remote(
                view if source is None else source.at[rows],
                view,
                self.send.at[way, hop - 1],
                self.receive.at[way, hop - 1],
                device,
            )
            copy.start()
            self.sent.append(copy)

    def wait(self, hop):
        self.sent[2 * hop - 2].wait_recv()
        self.sent[2 * hop - 1].wait_recv()

    def step(self, hop):
        self.wait(hop)
        if hop < self.places.half:
            self.start(hop + 1)

    def finish(self):
        for copy in self.sent:
            copy.wait_send()


class Parts:
    def __init__(self, rings):
        self.rings = rings

    def start(self, hop, sources=None):
        for number, ring in enumerate(self.rings):
            ring.start(hop) if sources is None else ring.start(hop, sources[number])

    def wait(self, hop):
        for ring in self.rings:
            ring.wait(hop)

    def step(self, hop):
        for ring in self.rings:
            ring.step(hop)

    def finish(self):
        for ring in self.rings:
            ring.finish()


class Spread:
    def __init__(self, places, own, slots, send, receive):
        self.places, self.slots, self.send, self.receive = places, slots, send, receive
        near, far = slots.at[places.side], slots.at[2 + places.side]
        self.chip = remote(own, far, send.at[0], receive.at[0], places.chip())
        self.core = remote(own, near, send.at[1], receive.at[1], places.core())
        self.far = far

    def start(self):
        self.chip.start()
        self.core.start()

    def pass_on(self):
        self.chip.wait_recv()
        self.last = remote(self.far, self.far, self.send.at[2], self.receive.at[2], self.places.core())
        self.last.start()

    def finish(self):
        self.chip.wait_send()
        self.core.wait()
        self.last.wait()


def hidden_units(source, weights, inner, factors, rows, units, number, block=512):
    features = source.shape[1]

    def lanes(start):
        return weights[:, :, start : start + block].reshape(features, block)

    lane = number * block
    gate = dot(source[...], lanes(lane))
    up = dot(source[...], lanes(units + lane))
    sigmoid = 1.0 / (1.0 + jnp.exp(-gate))
    silu = gate * sigmoid
    inner[rows, lane : lane + block] = (silu * up).astype(jnp.bfloat16)
    factors[rows, lane : lane + block] = (up * (sigmoid + silu * (1.0 - sigmoid))).astype(jnp.bfloat16)
    factors[rows, units + lane : units + lane + block] = silu.astype(jnp.bfloat16)


def begin_kernel(
    size, tokens_hbm, cotangent, query_shard, key_shard, value_shard, output_shard, gate_shard, up_shard, down_shard,
    cos_hbm, sin_hbm, rotary_hbm, plain_hbm, first_gain, second_gain,
    normed_hbm, weights_hbm, output_hbm, qkv_hbm, att_hbm, hidden_hbm, two_slots, cot_slots, feed_hbm, down_hbm,
    inner_hbm, factors_hbm, log_ref, gain_rows, attend_shard,
    tokens, cos_ref, sin_ref, rotary_spread, plain_spread, normed, weights, output_spread, qkv_ref, att_ref, hidden,
    feed, inner, factors, down, two_other,
    gains, gain_slots, output_both, terms, received, two_own, gain_send, gain_receive, ring_send, ring_receive,
    pass_send, pass_receive, out_send, out_receive, feed_send, feed_receive, down_send, down_receive, across, two_send,
    two_receive, cot_send, cot_receive, local_sem, load_sem, store_sem,
):
    bf16, f32 = jnp.bfloat16, jnp.float32
    places = Places(size)
    half, own = places.half, places.own
    half_rows = tokens.shape[0]
    columns = output_shard.shape[1]
    width = attend_shard.shape[1]
    units = gate_shard.shape[1]
    loads = [
        pltpu.make_async_copy(source, target, load_sem.at[number])
        for number, (source, target) in enumerate((
            (tokens_hbm, tokens), (cos_hbm, cos_ref), (sin_hbm, sin_ref), (rotary_hbm, rotary_spread),
            (plain_hbm, plain_spread),
        ))
    ]
    for copy in loads:
        copy.start()
    for group in range(2):
        lane = group * 4 * HEAD
        attend_shard[:, lane : lane + 2 * HEAD] = query_shard[:, group * 2 * HEAD : (group + 1) * 2 * HEAD]
        attend_shard[:, lane + 2 * HEAD : lane + 3 * HEAD] = key_shard[:, group * HEAD : (group + 1) * HEAD]
        attend_shard[:, lane + 3 * HEAD : lane + 4 * HEAD] = value_shard[:, group * HEAD : (group + 1) * HEAD]
    gains[0:1, : first_gain.shape[1]] = first_gain[...].astype(f32)
    gains[1:2, : first_gain.shape[1]] = second_gain[...].astype(f32)
    stores = []

    def store(source, target):
        copy = pltpu.make_async_copy(source, target, store_sem.at[len(stores)])
        copy.start()
        stores.append(copy)

    greet([places.peer(step) for step in range(1, size)] + [places.chip(), places.core()])

    def own_side(slot):
        return weights.at[slot, :, pl.ds(0, width)]

    def other_side(slot):
        return weights.at[slot, :, pl.ds(width, width)]

    def lanes_of(number, count):
        return pl.ds(number * count, count)

    ring = Parts([
        RingGather(places, weights.at[:, :, lanes_of(number, width // 2)], ring_send.at[number], ring_receive.at[number])
        for number in range(2)
    ])
    ring.start(1, [attend_shard.at[:, lanes_of(number, width // 2)] for number in range(2)])
    passed = []

    def hand_on(step, number, source=None):
        slot = places.index(step)
        copy = remote(
            own_side(slot) if source is None else source, other_side(slot),
            pass_send.at[number], pass_receive.at[number], places.chip(),
        )
        copy.start()
        passed.append(copy)

    hand_on(0, 0, attend_shard)
    output_pass = remote(
        output_shard, output_both.at[own, :, pl.ds(columns, columns)], across.at[0], across.at[1], places.chip()
    )
    output_pass.start()
    gain_copies = []
    for step in range(1, size):
        copy = remote(gains, gain_slots.at[own], gain_send.at[step - 1], gain_receive.at[step - 1], places.peer(step))
        copy.start()
        gain_copies.append(copy)
    near = cot_slots.at[places.side]
    keep = [
        pltpu.make_async_copy(attend_shard, own_side(own), local_sem.at[0]),
        pltpu.make_async_copy(output_shard, output_both.at[own, :, pl.ds(0, columns)], local_sem.at[1]),
        pltpu.make_async_copy(gate_shard, feed.at[own, :, lanes_of(0, units)], local_sem.at[2]),
        pltpu.make_async_copy(up_shard, feed.at[own, :, lanes_of(1, units)], local_sem.at[5]),
        pltpu.make_async_copy(down_shard, down.at[own], local_sem.at[6]),
        pltpu.make_async_copy(cotangent, near, local_sem.at[3]),
    ]
    for copy in keep:
        copy.start()
    gain_slots[own] = gains[...]

    def ring_step(hop):
        ring.step(hop)
        if hop < half:
            hand_on(-hop, 2 * hop - 1)
            hand_on(hop, 2 * hop)
        else:
            hand_on(half, size - 1)

    for copy in gain_copies:
        copy.wait_recv()
    part = tokens.shape[1] // size
    for index in range(size):
        gain_rows[:, index * part : (index + 1) * part] = gain_slots[index][:, :part]
    tile = 64
    mine_start = places.side * half_rows

    def norm_tile(number, carry):
        rows = pl.ds(pl.multiple_of(number * tile, tile), tile)
        values = tokens[rows, :].astype(f32)
        inverse = lax.rsqrt(jnp.mean(values * values, axis=1, keepdims=True) + norm_eps)
        target = pl.ds(pl.multiple_of(mine_start + number * tile, tile), tile)
        normed[target, :] = (values * inverse * gain_rows[0:1, :]).astype(bf16)
        return carry

    tiles = half_rows // tile
    for copy in loads:
        copy.wait()
    ring_step(1)
    lax.fori_loop(0, tiles // 2, norm_tile, 0)
    ring_step(2)
    lax.fori_loop(tiles // 2, tiles, norm_tile, 0)
    mine = pl.ds(pl.multiple_of(mine_start, half_rows), half_rows)
    swap = remote(normed.at[mine], normed.at[mine], across.at[2], across.at[3], places.core())
    swap.start()
    for hop in range(3, half):
        ring_step(hop)
    outputs = Parts([
        RingGather(places, output_both.at[:, :, lanes_of(number, columns)], out_send.at[number], out_receive.at[number])
        for number in range(2)
    ])
    output_pass.wait()
    for copy in keep:
        copy.wait()
    ring_feed = Parts([
        RingGather(places, feed.at[:, :, lanes_of(number, units)], feed_send.at[number], feed_receive.at[number])
        for number in range(2)
    ])
    outputs.start(1)
    ring_feed.start(1, [gate_shard, up_shard])
    ring_step(half)
    swap.wait()
    store(normed, normed_hbm)

    def attend(group):
        lanes = pl.ds(group * 4 * HEAD, 4 * HEAD)
        weight = weights[:, :, lanes].reshape(tokens.shape[1], 4 * HEAD)
        weight = dot(weight, rotary_spread[...]).astype(bf16)
        rows = dot(normed[...], weight)
        cos, sin = cos_ref[...], sin_ref[...]
        base = group * 4 * LANES

        def rot(u):
            return (u * cos + pltpu.roll(u, 64, 1) * sin).astype(bf16)

        for head in range(3):
            lane = head * LANES
            qkv_ref[:, base + lane : base + lane + LANES] = rot(rows[:, lane : lane + LANES])
        qkv_ref[:, base + 3 * LANES : base + 4 * LANES] = rows[:, 3 * LANES :].astype(bf16)
        turned = qkv_ref[:, base + 3 * LANES : base + 4 * LANES].T
        key_place = lax.broadcasted_iota(jnp.int32, (QB, QB), 0)
        query_place = lax.broadcasted_iota(jnp.int32, (QB, QB), 1)
        for head in range(2):
            for block in range(LENGTH // QB):
                first, last = block * QB, (block + 1) * QB
                query = qkv_ref[first:last, base + head * LANES : base + (head + 1) * LANES]
                key = qkv_ref[:last, base + 2 * LANES : base + 3 * LANES]
                score = dot(key, query, ((1,), (1,)))
                edge = jnp.where(key_place <= query_place, score[first:], -1e30)
                score = jnp.concatenate([score[:first], edge], axis=0) if block else edge
                top = jnp.max(score, axis=0, keepdims=True)
                weight = jnp.exp2((score - top) * C2)
                total = jnp.sum(weight, axis=0, keepdims=True)
                result = dot(turned[:, :last], weight.astype(bf16)) / total
                lane = group * 2 * LANES + head * LANES
                att_ref[first:last, lane : lane + LANES] = result.T.astype(bf16)
                log_ref[group, head, pl.ds(first, QB)] = (top * C2 + jnp.log2(total))[0]

    attend(0)
    outputs.step(1)
    attend(1)
    outputs.step(2)
    ring_feed.step(1)
    for copy in passed:
        copy.wait()
    store(weights, weights_hbm)
    cot = Spread(places, cotangent, cot_slots, cot_send, cot_receive)
    cot.start()
    attend(2)
    for hop in range(3, half):
        outputs.step(hop)
    attend(3)
    store(qkv_ref, qkv_hbm)
    store(att_ref, att_hbm)
    outputs.step(half)

    heads_width = columns // HEAD * LANES
    out_rows = output_shard.shape[0]

    def spread_slot(number, carry):
        rows = pl.ds(pl.multiple_of(number * out_rows, out_rows), out_rows)
        for side in range(2):
            value = dot(output_both[number, :, side * columns : (side + 1) * columns], plain_spread[...])
            output_spread[rows, side * heads_width : (side + 1) * heads_width] = value.astype(bf16)
        return carry

    lax.fori_loop(0, size, spread_slot, 0)
    store(output_spread, output_hbm)
    ring_feed.step(2)
    ring_down = Parts([
        RingGather(
            places, down.at[:, :, lanes_of(number, units // 2)], down_send.at[number], down_receive.at[number]
        )
        for number in range(2)
    ])
    ring_down.start(1, [down_shard.at[:, lanes_of(number, units // 2)] for number in range(2)])
    big = 256

    def theirs_tile(number, carry):
        start = (1 - places.side) * half_rows + number * big
        rows = pl.ds(pl.multiple_of(start, big), big)
        value = dot(att_ref[rows, :], output_spread[...], ((1,), (1,)))
        terms[pl.ds(pl.multiple_of(number * big, big), big), :] = value.astype(bf16)
        return carry

    lax.fori_loop(0, half_rows // big, theirs_tile, 0)
    sum_swap = remote(terms, received, across.at[4], across.at[5], places.core())
    sum_swap.start()

    def mine_tile(number, carry):
        rows = pl.ds(pl.multiple_of(mine_start + number * big, big), big)
        value = dot(att_ref[rows, :], output_spread[...], ((1,), (1,)))
        here = pl.ds(pl.multiple_of(number * big, big), big)
        hidden[here, :] = value + tokens[here, :].astype(f32)
        return carry

    lax.fori_loop(0, half_rows // big, mine_tile, 0)
    sum_swap.wait()

    def second_tile(number, carry):
        rows = pl.ds(pl.multiple_of(number * tile, tile), tile)
        values = hidden[rows, :] + received[rows, :].astype(f32)
        hidden[rows, :] = values
        inverse = lax.rsqrt(jnp.mean(values * values, axis=1, keepdims=True) + norm_eps)
        two_own[rows, :] = (values * inverse * gain_rows[1:2, :]).astype(bf16)
        return carry

    lax.fori_loop(0, half_rows // tile, second_tile, 0)
    two = Spread(places, two_own, two_slots, two_send, two_receive)
    two.start()
    store(two_own, two_slots.at[places.side])
    store(hidden, hidden_hbm)
    cot.pass_on()
    for hop in range(3, half):
        ring_feed.step(hop)
    ring_down.step(1)
    ring_feed.step(half)
    store(feed, feed_hbm)

    mine_rows = pl.ds(pl.multiple_of(mine_start, half_rows), half_rows)
    other_rows = pl.ds(pl.multiple_of(half_rows - mine_start, half_rows), half_rows)
    two.core.wait_recv()
    load_other = pltpu.make_async_copy(two_slots.at[1 - places.side], two_other, local_sem.at[4])
    load_other.start()
    hop = 2
    for source, place in ((two_own, mine_rows), (two_other, other_rows)):
        if source is two_other:
            load_other.wait()
        for number in range(units // 512):
            hidden_units(source, feed, inner, factors, place, units, number)
            if hop < half:
                ring_down.step(hop)
                hop += 1
    store(inner, inner_hbm)
    store(factors, factors_hbm)
    two.pass_on()
    for late in range(hop, half + 1):
        ring_down.step(late)
    store(down, down_hbm)
    cot.finish()
    two.chip.wait_send()
    two.core.wait_send()
    two.last.wait()
    for copy in gain_copies:
        copy.wait_send()
    ring.finish()
    outputs.finish()
    ring_feed.finish()
    ring_down.finish()
    for copy in stores:
        copy.wait()


def begin(
    size, tokens, cotangent, first_gain, second_gain, query_shard, key_shard, value_shard, output_shard, gate_shard,
    up_shard, down_shard,
):
    half_rows, features = tokens.shape
    rows = query_shard.shape[0]
    width = query_shard.shape[1] + key_shard.shape[1] + value_shard.shape[1]
    gain_block = (8, LANES * pl.cdiv(rows, LANES))
    columns = output_shard.shape[1]
    units = gate_shard.shape[1]
    heads_width = columns // HEAD * LANES
    groups = 2 * width // (4 * HEAD)
    vmem = pl.BlockSpec(memory_space=pltpu.VMEM)
    anywhere = pl.BlockSpec(memory_space=pl.ANY)
    dma = pltpu.SemaphoreType.DMA
    half = size // 2
    bf16, f32 = jnp.bfloat16, jnp.float32
    cos, sin = rope_tables()
    shape = jax.ShapeDtypeStruct
    buffer = pltpu.VMEM
    kept = [
        ((2 * half_rows, features), bf16),
        ((size, rows, 2 * width), bf16),
        ((features, 2 * heads_width), bf16),
        ((LENGTH, groups * 4 * LANES), bf16),
        ((LENGTH, groups * 2 * LANES), bf16),
        ((half_rows, features), f32),
    ]
    fed = [
        ((size, rows, 2 * units), bf16),
        ((2 * half_rows, units), bf16),
        ((2 * half_rows, 2 * units), bf16),
    ]
    slots = shape((4, half_rows, features), bf16)
    rotary = jnp.asarray(spread(4, (1, 1, 1, 0)), bf16)
    plain = jnp.asarray(spread(columns // HEAD, (0,) * 4), bf16)
    return pl.pallas_call(
        functools.partial(begin_kernel, size),
        in_specs=[anywhere] + [vmem] * 8 + [anywhere] * 4 + [vmem] * 2,
        out_specs=[anywhere] * 12 + [vmem] * 3,
        out_shape=[shape(*one) for one in kept]
        + [slots, slots, shape(*fed[0]), shape((size, rows, units), bf16), shape(*fed[1]), shape(*fed[2])]
        + [shape((groups, 2, LENGTH), f32), shape((8, features), f32), shape((rows, width), bf16)],
        scratch_shapes=[
            buffer((half_rows, features), bf16),
            buffer((LENGTH, LANES), f32),
            buffer((LENGTH, LANES), f32),
            buffer(rotary.shape, bf16),
            buffer(plain.shape, bf16),
        ]
        + [buffer(*one) for one in kept + fed]
        + [
            buffer((size, rows, units), bf16),
            buffer((half_rows, features), bf16),
            buffer(gain_block, f32),
            buffer((size,) + gain_block, f32),
            buffer((size, rows, 2 * columns), bf16),
            buffer((half_rows, features), bf16),
            buffer((half_rows, features), bf16),
            buffer((half_rows, features), bf16),
            dma((size - 1,)), dma((size - 1,)),
            dma((2, 2, half)), dma((2, 2, half)),
            dma((size,)), dma((size,)),
            dma((2, 2, half)), dma((2, 2, half)),
            dma((2, 2, half)), dma((2, 2, half)),
            dma((2, 2, half)), dma((2, 2, half)),
            dma((6,)),
            dma((3,)), dma((3,)),
            dma((3,)), dma((3,)),
            dma((7,)), dma((5,)), dma((11,)),
        ],
        compiler_params=pltpu.CompilerParams(collective_id=1, has_side_effects=True, vmem_limit_bytes=60 * 2**20),
        cost_estimate=pl.CostEstimate(flops=10**10, bytes_accessed=400 * 2**20, transcendentals=0),
        name="begin",
    )(
        tokens, cotangent, query_shard, key_shard, value_shard, output_shard, gate_shard, up_shard, down_shard,
        jnp.asarray(cos), jnp.asarray(sin), rotary, plain, first_gain.reshape(1, -1), second_gain.reshape(1, -1),
    )


class RingScatter:
    def __init__(self, places, partial, received, send, receive):
        self.places, self.partial, self.received = places, partial, received
        self.send, self.receive = send, receive
        self.rows = received.shape[2]
        self.cut = self.rows // 32 * 16
        self.sent = []

    def start(self, hop):
        places = self.places
        for way in range(2):
            rows = pl.ds(0, self.rows)
            if hop == 1:
                rows = (pl.ds(0, self.cut), pl.ds(self.cut, self.rows - self.cut))[way]
                source = self.partial(places.index(places.half)).at[rows]
            else:
                source = self.received.at[way, hop - 2]
            copy = remote(
                source,
                self.received.at[way, hop - 1, rows],
                self.send.at[way, hop - 1],
                self.receive.at[way, hop - 1],
                places.on_ring(1 - 2 * way),
            )
            copy.start()
            self.sent.append(copy)

    def wait(self, hop):
        self.sent[2 * hop - 2].wait_recv()
        self.sent[2 * hop - 1].wait_recv()

    def add(self, hop):
        distance = self.places.half - hop
        for way in range(2):
            own = self.partial(self.places.index(distance * (1 - 2 * way)))
            here = self.received.at[way, hop - 1]
            first, last = 0, self.rows
            if hop == 1:
                first, last = ((0, self.cut), (self.cut, last))[way]
                start, count = ((self.cut, self.rows - self.cut), (0, self.cut))[way]
                here[start : start + count, :] = own[start : start + count, :]
            size = min(last - first, 48)
            for start in range(first, last, size):
                rows = slice(start, min(start + size, last))
                here[rows, :] = here[rows, :] + own[rows, :]

    def step(self, hop):
        self.wait(hop)
        self.add(hop)
        self.start(hop + 1)

    def total(self, rows):
        half = self.places.half
        own = self.partial(self.places.index(0))
        return (
            own[rows, :].astype(jnp.float32)
            + self.received[0, half - 1, rows, :].astype(jnp.float32)
            + self.received[1, half - 1, rows, :].astype(jnp.float32)
        )

    def finish(self):
        for copy in self.sent:
            copy.wait_send()


def middle_kernel(
    size, two_slots, cot_slots, feed, down_hbm, inner_hbm, factors_hbm, hidden_hbm, gain_rows,
    late_grad, gate_sum, down_sum, hidden_grad, branch, far_out, near_out, out_got,
    two, cot, weights, down, inner, grads, down_grad, gate_grad, ring_got, outgoing, far_part, core_far, core_near,
    chip_got, stage, gate_stage, hidden, out_part, load_sem, stage_sem, down_send, down_receive, gate_send,
    gate_receive, send_sem, receive_sem, store_sem, credit,
):
    bf16, f32 = jnp.bfloat16, jnp.float32
    places = Places(size)
    half = places.half
    half_rows, features = hidden_hbm.shape
    rows = feed.shape[1]
    units = inner.shape[1]
    lane_half = units // 2
    greet([places.on_ring(1), places.on_ring(-1), places.chip(), places.core()])

    def lanes_of(number):
        return pl.ds(number * lane_half, lane_half)

    order = (2, 3, 0, 1)
    both_rows = 2 * half_rows
    near = pl.ds(0, both_rows)

    def rows_of(slot):
        return pl.ds(slot * half_rows, half_rows)

    fetch = {"weights": pltpu.make_async_copy(feed, weights, load_sem.at[0])}
    for number, slot in enumerate(order):
        fetch["two", slot] = pltpu.make_async_copy(two_slots.at[slot], two.at[rows_of(slot)], load_sem.at[1 + number])
        fetch["cot", slot] = pltpu.make_async_copy(cot_slots.at[slot], cot.at[rows_of(slot)], load_sem.at[5 + number])
    fetch["inner"] = pltpu.make_async_copy(inner_hbm, inner.at[near], load_sem.at[9])
    fetch["factors"] = pltpu.make_async_copy(factors_hbm, grads.at[near], load_sem.at[10])
    fetch["down"] = pltpu.make_async_copy(down_hbm, down, load_sem.at[11])
    for name in (
        "weights", ("two", 2), ("two", 3), ("cot", 2), ("cot", 3), "inner", ("cot", 0), ("cot", 1), "down", "factors",
        ("two", 0), ("two", 1),
    ):
        fetch[name].start()
    fetch["weights"].wait()
    block = 512

    def backward(slot):
        here = rows_of(slot)
        for number in range(units // block):
            lane = number * block
            weight = down[:, :, lane : lane + block].reshape(features, block)
            inner_grad = dot(cot[here, :], weight)
            for place in (slice(lane, lane + block), slice(units + lane, units + lane + block)):
                grads[here, place] = (inner_grad * grads[here, place].astype(f32)).astype(bf16)

    big = 256
    mine_start = places.side * half_rows
    theirs_start = (1 - places.side) * half_rows

    def two_terms(place):
        return dot(grads[place, :], weights[...].reshape(features, 2 * units), ((1,), (1,)))

    def out_terms(place):
        return dot(inner[place, :], down[...].reshape(features, units), ((1,), (1,)))

    def terms_to(target, start, terms):
        def tile(number, carry):
            value = terms(pl.ds(pl.multiple_of(start + number * big, big), big))
            target[pl.ds(pl.multiple_of(number * big, big), big), :] = value.astype(bf16)
            return carry

        lax.fori_loop(0, half_rows // big, tile, 0)

    def add_to(target, other):
        def tile(number, carry):
            place = pl.ds(pl.multiple_of(number * 32, 32), 32)
            target[place, :] = (target[place, :].astype(f32) + other[place, :].astype(f32)).astype(bf16)
            return carry

        lax.fori_loop(0, half_rows // 32, tile, 0)

    for slot in order[:2]:
        fetch["two", slot].wait()
        for number in range(units // block):
            hidden_units(two.at[rows_of(slot)], weights, inner, grads, rows_of(slot), units, number)
    fetch["inner"].wait()
    for slot in order:
        fetch["cot", slot].wait()

    span = 384
    per_span = span // rows

    def down_tile(number, carry):
        lanes = pl.ds(pl.multiple_of(number * span, span), span)
        value = dot(cot[:, lanes], inner[...], ((0,), (0,))).astype(bf16)
        down_grad[pl.ds(number * per_span, per_span)] = value.reshape(per_span, rows, units)
        return carry

    spans = features // span
    lax.fori_loop(0, spans, down_tile, 0)

    def scatter_of(array, send, receive, parts=2):
        lane_part = array.shape[2] // parts
        return Parts([
            RingScatter(
                places,
                lambda slot, number=number: array.at[slot, :, pl.ds(number * lane_part, lane_part)],
                ring_got.at[:, :, :, pl.ds(number * lane_part, lane_part)],
                send.at[number],
                receive.at[number],
            )
            for number in range(parts)
        ])

    ring = scatter_of(down_grad, down_send, down_receive)
    ring.start(1)
    fetch["down"].wait()
    for slot in order[:2]:
        backward(slot)
    terms_to(outgoing, both_rows + theirs_start, two_terms)
    far_swap = remote(outgoing, core_far, send_sem.at[0], receive_sem.at[0], places.core())
    far_swap.start()
    ring.step(1)
    terms_to(far_part, both_rows + mine_start, two_terms)
    far_swap.wait()
    add_to(far_part, core_far)
    chip_swap = remote(far_part, chip_got, send_sem.at[1], receive_sem.at[1], places.chip())
    chip_swap.start()
    fetch["factors"].wait()
    for slot in order[2:]:
        backward(slot)
    ring.step(2)
    for slot in order[2:]:
        fetch["two", slot].wait()

    def late_copy(number):
        place = pl.ds(pl.multiple_of(number * span, span), span)
        return pltpu.make_async_copy(gate_stage, late_grad.at[place, pl.ds(0, lane_half)], stage_sem.at[2])

    def gate_tile(number, carry):
        lanes = pl.ds(pl.multiple_of(number * span, span), span)
        value = dot(two[:, lanes], grads[:, :units], ((0,), (0,))).astype(bf16)
        gate_grad[pl.ds(number * per_span, per_span)] = value[:, :lane_half].reshape(per_span, rows, lane_half)

        @pl.when(number > 0)
        def _():
            late_copy(number - 1).wait()

        gate_stage[...] = value[:, lane_half:]
        late_copy(number).start()
        return carry

    lax.fori_loop(0, spans, gate_tile, 0)
    for hop in range(3, half):
        ring.step(hop)
    terms_to(outgoing, theirs_start, two_terms)
    near_swap = remote(outgoing, core_near, send_sem.at[2], receive_sem.at[2], places.core())
    near_swap.start()
    ring.wait(half)

    def total_to(target, sums, lane_part):
        def tile(number, carry):
            place = pl.ds(pl.multiple_of(number * 16, 16), 16)
            for part, one in enumerate(sums.rings):
                target[place, part * lane_part : (part + 1) * lane_part] = one.total(place)
            return carry

        lax.fori_loop(0, rows // 16, tile, 0)

    total_to(down_sum, ring, lane_half)
    ring.finish()
    for step in (1, -1):
        pl.semaphore_signal(credit, inc=1, device_id=places.on_ring(step), device_id_type=MESH)
    pl.semaphore_wait(credit, 2)
    ring = scatter_of(gate_grad, gate_send, gate_receive)
    ring.start(1)

    def stage_copy(number, side):
        place = pl.ds(pl.multiple_of(number * span, span), span)
        return pltpu.make_async_copy(stage.at[side], late_grad.at[place, pl.ds(lane_half, units)], stage_sem.at[side])

    def up_tile(pair, carry):
        for side in range(2):
            number = 2 * pair + side
            lanes = pl.ds(pl.multiple_of(number * span, span), span)
            value = dot(two[:, lanes], grads[:, units:], ((0,), (0,))).astype(bf16)

            @pl.when(pair > 0)
            def _(side=side, number=number):
                stage_copy(number - 2, side).wait()

            stage[side] = value
            stage_copy(number, side).start()
        return carry

    lax.fori_loop(0, spans // 2, up_tile, 0)
    ring.step(1)

    near_swap.wait()
    terms_to(outgoing, both_rows + theirs_start, out_terms)
    far_swap = remote(outgoing, core_far, send_sem.at[5], receive_sem.at[5], places.core())
    far_swap.start()
    chip_swap.wait()
    terms_to(far_part, both_rows + mine_start, out_terms)
    far_swap.wait()
    add_to(far_part, core_far)
    store_far = pltpu.make_async_copy(far_part, far_out, store_sem.at[0])
    store_far.start()
    out_rows = half_rows // 2
    out_swap = remote(
        far_part.at[pl.ds(0, out_rows)], out_part, send_sem.at[7], receive_sem.at[7], places.chip()
    )
    out_swap.start()
    ring.step(2)

    sends = []
    for number in range(half_rows // big):
        here = pl.ds(number * big, big)
        if number > 0:
            store_grad.wait()
        load_hidden = pltpu.make_async_copy(hidden_hbm.at[here], hidden, load_sem.at[12])
        load_hidden.start()
        place = pl.ds(pl.multiple_of(mine_start + number * big, big), big)
        value = two_terms(place) + core_near[here, :].astype(f32) + chip_got[here, :].astype(f32)
        load_hidden.wait()
        values = hidden[...]
        inverse = lax.rsqrt(jnp.mean(values * values, axis=1, keepdims=True) + norm_eps)
        scaled = value * gain_rows[1:2, :]
        mean = jnp.mean(scaled * values, axis=1, keepdims=True)
        total = cot[place, :].astype(f32) + inverse * scaled - values * (inverse * inverse * inverse) * mean
        hidden[...] = total
        chip_got[here, :] = total.astype(bf16)
        store_grad = pltpu.make_async_copy(hidden, hidden_grad.at[here], store_sem.at[1])
        store_grad.start()
        keep = pltpu.make_async_copy(chip_got.at[here], two.at[place], store_sem.at[2 + number])
        send = remote(chip_got.at[here], two.at[place], send_sem.at[3 + number], receive_sem.at[3 + number], places.core())
        keep.start()
        send.start()
        sends += [keep, send]
    store_grad.wait()

    terms_to(outgoing, theirs_start, out_terms)
    for copy in sends:
        copy.wait()
    store_branch = pltpu.make_async_copy(two.at[near], branch, store_sem.at[5])
    store_branch.start()
    near_swap = remote(outgoing, core_near, send_sem.at[6], receive_sem.at[6], places.core())
    near_swap.start()
    for number in range(half_rows // big):
        here = pl.ds(number * big, big)
        if number > 0:
            store_near.wait()
        load_hidden = pltpu.make_async_copy(hidden_hbm.at[here], hidden, load_sem.at[12])
        load_hidden.start()
        value = out_terms(pl.ds(pl.multiple_of(mine_start + number * big, big), big))
        load_hidden.wait()
        if number == 0:
            near_swap.wait()
        hidden[...] = value + hidden[...] + core_near[here, :].astype(f32)
        store_near = pltpu.make_async_copy(hidden, near_out.at[here], store_sem.at[4])
        store_near.start()
    for hop in range(3, half):
        ring.step(hop)
    ring.wait(half)
    total_to(gate_sum, ring, lane_half // 2)
    ring.finish()
    late_copy(spans - 1).wait()
    store_near.wait()
    store_far.wait()
    for side in range(2):
        stage_copy(spans - 2 + side, side).wait()
    store_branch.wait()
    out_swap.wait()
    store_out = pltpu.make_async_copy(out_part, out_got, store_sem.at[6])
    store_out.start()
    store_out.wait()


def middle(size, two_slots, cot_slots, feed, down, inner, factors, hidden_state, gain_rows):
    half_rows, features = hidden_state.shape
    rows, width = feed.shape[1:]
    units = width // 2
    vmem = pl.BlockSpec(memory_space=pltpu.VMEM)
    anywhere = pl.BlockSpec(memory_space=pl.ANY)
    dma = pltpu.SemaphoreType.DMA
    half = size // 2
    bf16, f32 = jnp.bfloat16, jnp.float32
    shape = jax.ShapeDtypeStruct
    buffer = pltpu.VMEM
    return pl.pallas_call(
        functools.partial(middle_kernel, size),
        in_specs=[anywhere] * 7 + [vmem],
        out_specs=[anywhere, vmem, vmem] + [anywhere] * 5,
        out_shape=[
            shape((features, units // 2 + units), bf16),
            shape((rows, units // 2), f32),
            shape((rows, units), f32),
            shape((half_rows, features), f32),
            shape((2 * half_rows, features), bf16),
            shape((half_rows, features), bf16),
            shape((half_rows, features), f32),
            shape((half_rows // 2, features), bf16),
        ],
        scratch_shapes=[
            buffer((4 * half_rows, features), bf16),
            buffer((4 * half_rows, features), bf16),
            buffer(feed.shape, bf16),
            buffer((size, rows, units), bf16),
            buffer((4 * half_rows, units), bf16),
            buffer((4 * half_rows, 2 * units), bf16),
            buffer((size, rows, units), bf16),
            buffer((size, rows, units // 2), bf16),
            buffer((2, half, rows, units), bf16),
            buffer((half_rows, features), bf16),
            buffer((half_rows, features), bf16),
            buffer((half_rows, features), bf16),
            buffer((half_rows, features), bf16),
            buffer((half_rows, features), bf16),
            buffer((2, 384, units), bf16),
            buffer((384, units // 2), bf16),
            buffer((256, features), f32),
            buffer((half_rows // 2, features), bf16),
            dma((13,)),
            dma((3,)),
            dma((2, 2, half)), dma((2, 2, half)),
            dma((2, 2, half)), dma((2, 2, half)),
            dma((8,)), dma((8,)),
            dma((7,)),
            pltpu.SemaphoreType.REGULAR,
        ],
        compiler_params=pltpu.CompilerParams(collective_id=3, has_side_effects=True, vmem_limit_bytes=63 * 2**20),
        cost_estimate=pl.CostEstimate(flops=6 * 10**10, bytes_accessed=300 * 2**20, transcendentals=0),
        name="middle",
    )(two_slots, cot_slots, feed, down, inner, factors, hidden_state, gain_rows)


def finish_kernel(
    size, tokens_hbm, hidden_hbm, branch_hbm, normed_hbm, weights_hbm, output_hbm, qkv_hbm, att_hbm, up_hbm, up_shard,
    gate_hbm, gate_shard, far_out, near_hbm, first_out, log_ref, gain_rows, attend_shard, cos_ref, sin_ref,
    rotary_spread, plain_spread,
    tokens_grad, query_sum, key_sum, value_sum, output_sum, up_sum, gate_out, gain_sum, layer_out, second_out,
    branch, grad_ref, back, dq_ref, dk_ref, dv_ref, own_grad, other_grad, crossed, ring_got, output_grad, output_got,
    output_crossed, up_grad, up_got, terms, got_terms, output_own, output_across, gain_parts, gate_sum, gate_part, up_part,
    normed, weights, output_spread, qkv_two, att_ref, tokens, hidden_grad, load_sem,
    ring_send, ring_receive, out_send, out_receive, up_send, up_receive, cross_send, cross_receive, across,
    gain_send, gain_receive,
):
    bf16, f32 = jnp.bfloat16, jnp.float32
    places = Places(size)
    half, own = places.half, places.own
    half_rows, features = tokens_hbm.shape
    rows = attend_shard.shape[0]
    units = up_hbm.shape[1] * 2 // 3
    lane_half = units // 2
    span = 4 * HEAD
    big = 256
    diagonal = (own, 3 - places.tensor)
    group_order = (2, 3, 0, 1)
    greet([places.on_ring(1), places.on_ring(-1), places.chip(), places.core(), diagonal])

    out_rows = half_rows // 2
    out_swap = remote(
        far_out.at[pl.ds(out_rows, out_rows)], second_out, across.at[0], across.at[1], places.chip()
    )

    out_swap.start()

    def qkv_load(number):
        lanes = pl.ds(group_order[number] * 4 * LANES, 4 * LANES)
        return pltpu.make_async_copy(qkv_hbm.at[:, lanes], qkv_two.at[number % 2], load_sem.at[number])

    def row_loads(first, second, number):
        here = pl.ds(number * big, big)
        return (
            pltpu.make_async_copy(first.at[here], tokens, load_sem.at[4]),
            pltpu.make_async_copy(second.at[here], hidden_grad, load_sem.at[5]),
        )

    fetch = {
        "up": pltpu.make_async_copy(up_hbm, up_grad, load_sem.at[11]),
        "branch": pltpu.make_async_copy(branch_hbm, branch, load_sem.at[6]),
        "output": pltpu.make_async_copy(output_hbm, output_spread, load_sem.at[7]),
        "att": pltpu.make_async_copy(att_hbm, att_ref, load_sem.at[8]),
        "normed": pltpu.make_async_copy(normed_hbm, normed, load_sem.at[9]),
        "weights": pltpu.make_async_copy(weights_hbm, weights, load_sem.at[10]),
        "gate_sum": pltpu.make_async_copy(gate_hbm, gate_sum, load_sem.at[12]),
        "gate_part": pltpu.make_async_copy(gate_shard, gate_part, load_sem.at[13]),
        "up_part": pltpu.make_async_copy(up_shard, up_part, load_sem.at[14]),
    }
    fetch["up"].start()
    fetch["branch"].start()
    fetch["output"].start()
    qkv_loads = [qkv_load(number) for number in range(4)]
    qkv_loads[0].start()
    for name in ("att", "normed", "weights", "gate_sum", "gate_part", "up_part"):
        fetch[name].start()
    token_rows = row_loads(tokens_hbm, hidden_hbm, 0)
    for copy in token_rows:
        copy.start()

    def lanes_of(number, count):
        return pl.ds(number * count, count)

    ups = Parts([
        RingScatter(
            places,
            lambda slot, number=number: up_grad.at[
                pl.ds(pl.multiple_of(slot * rows, rows), rows), lanes_of(number, lane_half)
            ],
            up_got.at[:, :, :, lanes_of(number, lane_half)],
            up_send.at[number],
            up_receive.at[number],
        )
        for number in range(3)
    ])
    fetch["up"].wait()
    ups.start(1)
    fetch["branch"].wait()
    fetch["output"].wait()
    fetch["att"].wait()

    def back_group(number, target, lane, between):
        group = group_order[number]
        qkv_loads[number].wait()
        if number < 3:
            qkv_loads[number + 1].start()
        qkv_ref = qkv_two.at[number % 2]
        base = 0
        for part in range(2):
            block = pl.ds(part * half_rows, half_rows)
            value = dot(branch[block, :], output_spread[:, group * 2 * LANES : (group + 1) * 2 * LANES])
            grad_ref[block, :] = value.astype(bf16)
        turned = qkv_ref[:, base + 2 * LANES : base + 3 * LANES].T
        cos, sin = cos_ref[...], sin_ref[...]
        scale = HEAD**-0.5

        def unrot(u):
            return (u * cos - pltpu.roll(u, 64, 1) * sin).astype(bf16)

        key_place = lax.broadcasted_iota(jnp.int32, (QB, QB), 0)
        query_place = lax.broadcasted_iota(jnp.int32, (QB, QB), 1)
        for head in range(2):
            lanes = slice(head * LANES, (head + 1) * LANES)
            att_lane = (2 * group + head) * LANES
            prod = grad_ref[:, lanes].astype(f32) * att_ref[:, att_lane : att_lane + LANES].astype(f32)
            delta = jnp.sum(prod.T, axis=0, keepdims=True)
            for block in reversed(range(LENGTH // QB)):
                first, last = block * QB, (block + 1) * QB
                query = qkv_ref[first:last, base + head * LANES : base + (head + 1) * LANES]
                out_grad = grad_ref[first:last, lanes]
                score = dot(qkv_ref[:last, base + 2 * LANES : base + 3 * LANES], query, ((1,), (1,)))
                prob = jnp.exp2(score * C2 - log_ref[group, head : head + 1, first:last])
                edge = jnp.where(key_place <= query_place, prob[first:], 0.0)
                prob = jnp.concatenate([prob[:first], edge], axis=0) if block else edge
                prob_grad = dot(qkv_ref[:last, base + 3 * LANES : base + 4 * LANES], out_grad, ((1,), (1,)))
                score_grad = (prob * (prob_grad - delta[:, first:last])).astype(bf16)
                key_part = dot(score_grad, query)
                value_part = dot(prob.astype(bf16), out_grad)
                if head == 0 and block == LENGTH // QB - 1:
                    dk_ref[...] = key_part
                    dv_ref[...] = value_part
                else:
                    dk_ref[:last] += key_part
                    dv_ref[:last] += value_part
                dq_ref[first:last, lanes] = dot(turned[:, :last], score_grad).T
            if head == 0:
                between()
        wide = jnp.concatenate(
            [
                unrot(dq_ref[:, :LANES] * scale),
                unrot(dq_ref[:, LANES:] * scale),
                unrot(dk_ref[...] * scale),
                dv_ref[...].astype(bf16),
            ],
            axis=1,
        )
        close_back = dot(wide, rotary_spread[...], ((1,), (1,))).astype(bf16)
        back[:, group * span : (group + 1) * span] = close_back
        if number == 0:
            fetch["normed"].wait()
        for part in range(2):
            block = slice(part * features // 2, (part + 1) * features // 2)
            value = dot(normed[:, block], close_back, ((0,), (0,))).astype(bf16)
            target[part * size // 2 : (part + 1) * size // 2, :, lane : lane + span] = value.reshape(
                size // 2, rows, span
            )

    order = [half]
    for step in range(half - 1, 0, -1):
        order += [step, -step]
    order.append(0)
    crossing = {}

    def cross(group):
        for number, step in enumerate(order):
            slot = places.index(step)
            lanes = pl.ds(group * span, span)
            copy = remote(
                other_grad.at[slot, :, lanes], crossed.at[slot, :, lanes],
                cross_send.at[group, number], cross_receive.at[group, number], places.chip(),
            )
            copy.start()
            crossing[(group, step)] = copy

    heads_width = output_spread.shape[1] // 2
    columns = heads_width // LANES * HEAD
    kept = LANES
    sent_on = columns - kept
    for side in (1, 0):
        close = dot(
            att_ref[:, side * heads_width : (side + 1) * heads_width], plain_spread[...], ((1,), (1,))
        ).astype(bf16)
        for part in range(2):
            block = slice(part * features // 2, (part + 1) * features // 2)
            value = dot(branch[:, block], close, ((0,), (0,))).astype(bf16)
            output_grad[part * size // 2 : (part + 1) * size // 2, :, side * columns : (side + 1) * columns] = (
                value.reshape(size // 2, rows, columns)
            )
    out_crossing = {}
    for number, step in enumerate(order):
        slot = places.index(step)
        copy = remote(
            output_grad.at[slot, :, pl.ds(columns + kept, sent_on)], output_crossed.at[slot],
            cross_send.at[2, number], cross_receive.at[2, number], places.chip(),
        )
        copy.start()
        out_crossing[step] = copy

    def prepare_output(step):
        out_crossing[step].wait_recv()
        slot = places.index(step)
        for start in range(0, rows, 48):
            place = slice(start, start + 48)
            output_grad[slot, place, kept:columns] = output_grad[slot, place, kept:columns] + output_crossed[slot, place, :]

    ring_width = (columns + kept) // 2
    outputs = Parts([
        RingScatter(
            places,
            lambda slot, number=number: output_grad.at[slot, :, lanes_of(number, ring_width)],
            output_got.at[:, :, :, lanes_of(number, ring_width)],
            out_send.at[number],
            out_receive.at[number],
        )
        for number in range(2)
    ])

    def output_step(hop):
        prepare_output(half - hop)
        prepare_output(hop - half)
        outputs.step(hop)

    micro = [(ring, hop) for hop in range(1, half) for ring in ups.rings]

    def serve(count):
        for _ in range(min(count, len(micro))):
            ring, hop = micro.pop(0)
            ring.step(hop)

    serve(1)
    back_group(0, other_grad, 0, lambda: serve(2))
    cross(0)
    serve(1)
    back_group(1, other_grad, span, lambda: serve(2))
    cross(1)
    serve(1)

    def late_start():
        serve(1)
        prepare_output(half)
        outputs.start(1)

    back_group(2, own_grad, 0, late_start)
    serve(len(micro))
    back_group(3, own_grad, span, lambda: output_step(1))
    if half > 2:
        output_step(2)

    def prepare(group, step):
        crossing[(group, step)].wait_recv()
        slot = places.index(step)
        lanes = slice(group * span, (group + 1) * span)
        for start in range(0, rows, 48):
            place = slice(start, start + 48)
            crossed[slot, place, lanes] = crossed[slot, place, lanes] + own_grad[slot, place, lanes]

    attend = [
        RingScatter(
            places,
            lambda slot, number=number: crossed.at[slot, :, lanes_of(number, span)],
            ring_got.at[:, :, :, lanes_of(number, span)],
            ring_send.at[number],
            ring_receive.at[number],
        )
        for number in range(2)
    ]

    def attend_start(group):
        prepare(group, half)
        attend[group].start(1)

    def attend_step(group, hop):
        prepare(group, half - hop)
        prepare(group, hop - half)
        attend[group].step(hop)

    attend_start(0)
    whole = weights.shape[2]
    fetch["weights"].wait()

    def terms_of(block):
        return dot(back[block, :], weights[...].reshape(features, whole), ((1,), (1,)))

    def theirs_tile(number, carry):
        place = (1 - places.side) * half_rows + number * big
        value = terms_of(pl.ds(pl.multiple_of(place, big), big))
        terms[pl.ds(pl.multiple_of(number * big, big), big), :] = value.astype(bf16)
        return carry

    lax.fori_loop(0, half_rows // big, theirs_tile, 0)
    terms_swap = remote(terms, got_terms, across.at[2], across.at[3], places.core())
    terms_swap.start()
    attend_step(0, 1)
    for hop in range(3, half):
        output_step(hop)
    terms_swap.wait()
    for number in range(half_rows // big):
        for copy in token_rows:
            copy.wait()
        here = slice(number * big, (number + 1) * big)
        place = places.side * half_rows + number * big
        value = terms_of(pl.ds(pl.multiple_of(place, big), big)) + got_terms[here, :].astype(f32)
        values = tokens[...].astype(f32)
        inverse = lax.rsqrt(jnp.mean(values * values, axis=1, keepdims=True) + norm_eps)
        scaled = value * gain_rows[0:1, :]
        inner = jnp.mean(scaled * values, axis=1, keepdims=True)
        result = hidden_grad[...] + inverse * scaled - values * (inverse * inverse * inverse) * inner
        tokens_grad[here, :] = result.astype(bf16)
        if number < half_rows // big - 1:
            token_rows = row_loads(tokens_hbm, hidden_hbm, number + 1)
            for copy in token_rows:
                copy.start()
        if number == 0 and half > 2:
            attend_step(0, 2)
    attend_start(1)
    for hop in range(3, half):
        attend_step(0, hop)
    prepare(0, 0)

    prepare_output(0)
    outputs.wait(half)

    for start in range(0, rows, 48):
        place = slice(start, start + 48)
        late = outputs.rings[1].total(place)
        output_own[place, :ring_width] = outputs.rings[0].total(place)
        output_own[place, ring_width:] = late[:, : columns - ring_width]
        output_across[0, place, :] = late[:, columns - ring_width :].astype(bf16)
    output_swap = remote(output_across.at[0], output_across.at[1], across.at[4], across.at[5], places.chip())
    output_swap.start()
    attend_step(1, 1)
    ups.wait(half)
    for name in ("gate_sum", "gate_part", "up_part"):
        fetch[name].wait()

    def up_tile(number, carry):
        place = pl.ds(pl.multiple_of(number * 16, 16), 16)
        early = gate_sum[place, :]
        gate_out[place, :lane_half] = early
        gain = jnp.sum(early * gate_part[place, :lane_half].astype(f32), axis=1, keepdims=True)
        late = (
            (gate_out, gate_part, lane_half, 0), (up_sum, up_part, 0, 1), (up_sum, up_part, lane_half, 2),
        )
        for target, weight, lane, part in late:
            lanes = slice(lane, lane + lane_half)
            value = ups.rings[part].total(place)
            target[place, lanes] = value
            gain += jnp.sum(value * weight[place, lanes].astype(f32), axis=1, keepdims=True)
        lane = lax.broadcasted_iota(jnp.int32, (16, LANES), 1)
        gain_parts[0, place, :] = jnp.where(lane == 1, gain, 0.0)
        return carry

    lax.fori_loop(0, rows // 16, up_tile, 0)

    out_swap.wait()
    for number in range(half_rows // big):
        here = slice(number * big, (number + 1) * big)
        source = first_out if number < half_rows // big // 2 else second_out
        share = pltpu.make_async_copy(source.at[pl.ds(number * big % out_rows, big)], tokens, load_sem.at[4])
        near = pltpu.make_async_copy(near_hbm.at[pl.ds(number * big, big)], hidden_grad, load_sem.at[5])
        share.start()
        near.start()
        share.wait()
        near.wait()
        layer_out[here, :] = (hidden_grad[...] + tokens[...].astype(f32)).astype(bf16)
    if half > 2:
        attend_step(1, 2)

    def attend_total(part):
        attend[part].wait(half)
        for start in range(0, rows, 48):
            place = slice(start, start + 48)
            value = attend[part].total(place)
            query_sum[place, part * 2 * HEAD : (part + 1) * 2 * HEAD] = value[:, : 2 * HEAD]
            key_sum[place, part * HEAD : (part + 1) * HEAD] = value[:, 2 * HEAD : 3 * HEAD]
            value_sum[place, part * HEAD : (part + 1) * HEAD] = value[:, 3 * HEAD :]
            weight = attend_shard[place, part * span : (part + 1) * span].astype(f32)
            gain = jnp.sum(value * weight, axis=1, keepdims=True)
            lane = lax.broadcasted_iota(jnp.int32, (48, LANES), 1)
            gain_parts[0, place, :] += jnp.where(lane == 0, gain, 0.0)

    attend_total(0)
    for hop in range(3, half):
        attend_step(1, hop)
    prepare(1, 0)
    output_swap.wait()
    output_sum[:, :kept] = output_own[:, :kept] + output_across[1].astype(f32)
    output_sum[:, kept:] = output_own[:, kept:]
    attend_total(1)
    gain_copies = []
    for number, device in enumerate((places.core(), places.chip(), diagonal)):
        copy = remote(
            gain_parts.at[0], gain_parts.at[1 + number], gain_send.at[number], gain_receive.at[number], device
        )
        copy.start()
        gain_copies.append(copy)
    for copy in list(crossing.values()) + list(out_crossing.values()):
        copy.wait_send()
    ups.finish()
    outputs.finish()
    for ring in attend:
        ring.finish()
    for copy in gain_copies:
        copy.wait()
    gain_sum[...] = (gain_parts[0] + gain_parts[1]) + (gain_parts[2] + gain_parts[3])


def finish(
    size, tokens, hidden_grad, branch, normed, weights, output_spread, qkv, att, logs, gain_rows, up_grad, up_shard,
    gate_sum, gate_shard, attend_shard, far_out, near_out, first_out,
):
    half_rows, features = tokens.shape
    rows, width = attend_shard.shape
    columns = output_spread.shape[1] // 2 // LANES * HEAD
    units = up_shard.shape[1]
    vmem = pl.BlockSpec(memory_space=pltpu.VMEM)
    anywhere = pl.BlockSpec(memory_space=pl.ANY)
    dma = pltpu.SemaphoreType.DMA
    half = size // 2
    bf16, f32 = jnp.bfloat16, jnp.float32
    cos, sin = rope_tables()
    shape = jax.ShapeDtypeStruct
    buffer = pltpu.VMEM
    return pl.pallas_call(
        functools.partial(finish_kernel, size),
        in_specs=[anywhere] * 15 + [vmem] * 7,
        out_specs=[vmem] * 9 + [anywhere],
        out_shape=[
            shape((half_rows, features), bf16),
            shape((rows, width // 2), f32),
            shape((rows, width // 4), f32),
            shape((rows, width // 4), f32),
            shape((rows, columns), f32),
            shape((rows, units), f32),
            shape((rows, units), f32),
            shape((rows, LANES), f32),
            shape((half_rows, features), bf16),
            shape((half_rows // 2, features), bf16),
        ],
        scratch_shapes=[
            buffer((LENGTH, features), bf16),
            buffer((LENGTH, 2 * LANES), bf16),
            buffer((LENGTH, 2 * width), bf16),
            buffer((LENGTH, 2 * LANES), f32),
            buffer((LENGTH, LANES), f32),
            buffer((LENGTH, LANES), f32),
            buffer((size, rows, width), bf16),
            buffer((size, rows, width), bf16),
            buffer((size, rows, width), bf16),
            buffer((2, half, rows, width), bf16),
            buffer((size, rows, 2 * columns), bf16),
            buffer((2, half, rows, columns + LANES), bf16),
            buffer((size, rows, columns - LANES), bf16),
            buffer(up_grad.shape, bf16),
            buffer((2, half, rows, up_grad.shape[1]), bf16),
            buffer((half_rows, features), bf16),
            buffer((half_rows, features), bf16),
            buffer((rows, columns), f32),
            buffer((2, rows, LANES), bf16),
            buffer((4, rows, LANES), f32),
            buffer(gate_sum.shape, f32),
            buffer((rows, units), bf16),
            buffer((rows, units), bf16),
            buffer((LENGTH, features), bf16),
            buffer(weights.shape, bf16),
            buffer(output_spread.shape, bf16),
            buffer((2, LENGTH, 4 * LANES), bf16),
            buffer(att.shape, bf16),
            buffer((256, features), bf16),
            buffer((256, features), f32),
            dma((16,)),
            dma((2, 2, half)), dma((2, 2, half)),
            dma((2, 2, half)), dma((2, 2, half)),
            dma((3, 2, half)), dma((3, 2, half)),
            dma((3, size)), dma((3, size)),
            dma((6,)),
            dma((3,)), dma((3,)),
        ],
        compiler_params=pltpu.CompilerParams(collective_id=2, has_side_effects=True, vmem_limit_bytes=63 * 2**20),
        cost_estimate=pl.CostEstimate(flops=3 * 10**10, bytes_accessed=300 * 2**20, transcendentals=0),
        name="finish",
    )(
        tokens, hidden_grad, branch, normed, weights, output_spread, qkv, att, up_grad, up_shard, gate_sum, gate_shard,
        far_out, near_out, first_out, logs, gain_rows, attend_shard, jnp.asarray(cos), jnp.asarray(sin),
        jnp.asarray(spread(4, (1, 1, 1, 0)), bf16), jnp.asarray(spread(4, (0,) * 4), bf16),
    )


def local(
    dp_size,
    tokens,
    first_gain,
    query_weight,
    key_weight,
    value_weight,
    output_weight,
    second_gain,
    gate_weight,
    up_weight,
    down_weight,
    cotangent,
):
    f32 = jnp.float32
    (
        normed, weights, output_spread, qkv, attended, hidden_state, two_slots, cot_slots, feed, down, inner, factors,
        logs, gain_rows, attend_shard,
    ) = begin(
        dp_size, tokens, cotangent, first_gain, second_gain, query_weight, key_weight, value_weight, output_weight.T,
        gate_weight, up_weight, down_weight.T,
    )
    late_grad, gate_sum, down_sum, hidden_grad, branch, far_out, near_out, first_out = middle(
        dp_size, two_slots, cot_slots, feed, down, inner, factors, hidden_state, gain_rows
    )
    tokens_grad, query_sum, key_sum, value_sum, output_sum, up_sum, gate_sum, gain_sums, layer_out, _ = finish(
        dp_size, tokens, hidden_grad, branch, normed, weights, output_spread, qkv, attended, logs, gain_rows,
        late_grad, up_weight, gate_sum, gate_weight, attend_shard, far_out, near_out, first_out,
    )
    return (
        layer_out,
        tokens_grad,
        gain_sums[:, 0] / first_gain.astype(f32),
        query_sum,
        key_sum,
        value_sum,
        output_sum.T,
        gain_sums[:, 1] / second_gain.astype(f32),
        gate_sum,
        up_sum,
        down_sum.T,
    )


def solution(mesh):
    in_specs = (
        P(("dp", "tensor"), None),
        P("dp"),
        P("dp", "tensor"),
        P("dp", "tensor"),
        P("dp", "tensor"),
        P("tensor", "dp"),
        P("dp"),
        P("dp", "tensor"),
        P("dp", "tensor"),
        P("tensor", "dp"),
        P(("dp", "tensor"), None),
    )
    out_specs = (
        P(("dp", "tensor"), None),
        P(("dp", "tensor"), None),
        P("dp"),
        P("dp", "tensor"),
        P("dp", "tensor"),
        P("dp", "tensor"),
        P("tensor", "dp"),
        P("dp"),
        P("dp", "tensor"),
        P("dp", "tensor"),
        P("tensor", "dp"),
    )
    body = functools.partial(local, mesh.shape["dp"])
    return jax.shard_map(body, mesh=mesh, in_specs=in_specs, out_specs=out_specs, check_vma=False)
```

```python
import functools

import jax
import jax.numpy as jnp
import numpy as np
from jax import lax
from jax.experimental import pallas as pl
from jax.experimental.pallas import tpu as pltpu
from jax.sharding import PartitionSpec as P

HEAD = 96
LENGTH = 1024
LANES = 128
QB = 256
norm_eps = 1e-05
rope_base = 100000.0


def rope_tables():
    half = HEAD // 2
    freq = rope_base ** (np.arange(half, dtype=np.float64) * (-2.0 / HEAD))
    turned = np.arange(LENGTH, dtype=np.float64)[:, None] * freq[None, :]
    cos = np.zeros((LENGTH, LANES), np.float32); sin = np.zeros((LENGTH, LANES), np.float32)
    cos[:, :half] = np.cos(turned); cos[:, 64:64+half] = np.cos(turned)
    sin[:, :half] = -np.sin(turned); sin[:, 64:64+half] = np.sin(turned)
    return cos, sin

def spread(heads, rotary):
    e = np.zeros((heads * HEAD, heads * LANES), np.float32)
    for h in range(heads):
        for i in range(HEAD):
            lane = i if (not rotary[h] or i < 48) else i + 16
            e[h * HEAD + i, h * LANES + lane] = 1
    return e

def dot(a, b, dims=((1,), (0,))):
    return lax.dot_general(a, b, (dims, ((), ())), preferred_element_type=jnp.float32)

C2 = float(HEAD ** -0.5 * np.log2(np.e))


MESH = pl.DeviceIdType.MESH


class Places:
    def __init__(self, size):
        self.size = size
        self.half = size // 2
        self.own = lax.axis_index("dp")
        self.tensor = lax.axis_index("tensor")
        self.side = self.tensor % 2
        odd = self.own % 2
        self.place = (1 - odd) * (self.own // 2) + odd * (size - 1 - self.own // 2)

    def index(self, step):
        place = (self.place + step + self.size) % self.size
        late = place // self.half
        return (1 - late) * 2 * place + late * (2 * (self.size - 1 - place) + 1)

    def on_ring(self, step):
        return (self.index(step), self.tensor)

    def peer(self, step):
        return ((self.own + step + self.size) % self.size, self.tensor)

    def chip(self):
        return (self.own, (self.tensor + 2) % 4)

    def core(self):
        return (self.own, self.tensor + 1 - 2 * self.side)


def remote(source, target, send, receive, device):
    return pltpu.make_async_remote_copy(
        src_ref=source,
        dst_ref=target,
        send_sem=send,
        recv_sem=receive,
        device_id=device,
        device_id_type=MESH,
    )


def greet(devices):
    barrier = pltpu.get_barrier_semaphore()
    for device in devices:
        pl.semaphore_signal(barrier, inc=1, device_id=device, device_id_type=MESH)
    pl.semaphore_wait(barrier, len(devices))


class RingGather:
    def __init__(self, places, slots, send, receive):
        self.places, self.slots, self.send, self.receive = places, slots, send, receive
        self.cut = slots.shape[1] // 32 * 16
        self.sent = []

    def start(self, hop, source=None):
        places, half = self.places, self.places.half
        for way, (step, device) in enumerate(
            ((1 - hop, places.on_ring(1)), (hop - 1, places.on_ring(-1)))
        ):
            slot = places.index(step)
            rows = pl.ds(0, self.slots.shape[1])
            if hop == half:
                rows = (pl.ds(0, self.cut), pl.ds(self.cut, self.slots.shape[1] - self.cut))[way]
            view = self.slots.at[slot, rows]
            copy = remote(
                view if source is None else source.at[rows],
                view,
                self.send.at[way, hop - 1],
                self.receive.at[way, hop - 1],
                device,
            )
            copy.start()
            self.sent.append(copy)

    def wait(self, hop):
        self.sent[2 * hop - 2].wait_recv()
        self.sent[2 * hop - 1].wait_recv()

    def step(self, hop):
        self.wait(hop)
        if hop < self.places.half:
            self.start(hop + 1)

    def finish(self):
        for copy in self.sent:
            copy.wait_send()


class Parts:
    def __init__(self, rings):
        self.rings = rings

    def start(self, hop, sources=None):
        for number, ring in enumerate(self.rings):
            ring.start(hop) if sources is None else ring.start(hop, sources[number])

    def wait(self, hop):
        for ring in self.rings:
            ring.wait(hop)

    def step(self, hop):
        for ring in self.rings:
            ring.step(hop)

    def finish(self):
        for ring in self.rings:
            ring.finish()


class Spread:
    def __init__(self, places, own, slots, send, receive):
        self.places, self.slots, self.send, self.receive = places, slots, send, receive
        near, far = slots.at[places.side], slots.at[2 + places.side]
        self.chip = remote(own, far, send.at[0], receive.at[0], places.chip())
        self.core = remote(own, near, send.at[1], receive.at[1], places.core())
        self.far = far

    def start(self):
        self.chip.start()
        self.core.start()

    def pass_on(self):
        self.chip.wait_recv()
        self.last = remote(self.far, self.far, self.send.at[2], self.receive.at[2], self.places.core())
        self.last.start()

    def finish(self):
        self.chip.wait_send()
        self.core.wait()
        self.last.wait()


def hidden_units(source, weights, inner, factors, rows, units, number, block=512):
    features = source.shape[1]

    def lanes(start):
        return weights[:, :, start : start + block].reshape(features, block)

    lane = number * block
    gate = dot(source[...], lanes(lane))
    up = dot(source[...], lanes(units + lane))
    sigmoid = 1.0 / (1.0 + jnp.exp(-gate))
    silu = gate * sigmoid
    inner[rows, lane : lane + block] = (silu * up).astype(jnp.bfloat16)
    factors[rows, lane : lane + block] = (up * (sigmoid + silu * (1.0 - sigmoid))).astype(jnp.bfloat16)
    factors[rows, units + lane : units + lane + block] = silu.astype(jnp.bfloat16)


def begin_kernel(
    size, tokens_hbm, cotangent, query_shard, key_shard, value_shard, output_shard, gate_shard, up_shard, down_shard,
    cos_hbm, sin_hbm, rotary_hbm, plain_hbm, first_gain, second_gain,
    normed_hbm, weights_hbm, output_hbm, qkv_hbm, att_hbm, hidden_hbm, two_slots, cot_slots, feed_hbm, down_hbm,
    inner_hbm, factors_hbm, log_ref, gain_rows, attend_shard,
    tokens, cos_ref, sin_ref, rotary_spread, plain_spread, normed, weights, output_spread, qkv_ref, att_ref, hidden,
    feed, inner, factors, down, two_other,
    gains, gain_slots, output_both, terms, received, two_own, gain_send, gain_receive, ring_send, ring_receive,
    pass_send, pass_receive, out_send, out_receive, feed_send, feed_receive, down_send, down_receive, across, two_send,
    two_receive, cot_send, cot_receive, local_sem, load_sem, store_sem,
):
    bf16, f32 = jnp.bfloat16, jnp.float32
    places = Places(size)
    half, own = places.half, places.own
    half_rows = tokens.shape[0]
    columns = output_shard.shape[1]
    width = attend_shard.shape[1]
    units = gate_shard.shape[1]
    loads = [
        pltpu.make_async_copy(source, target, load_sem.at[number])
        for number, (source, target) in enumerate((
            (tokens_hbm, tokens), (cos_hbm, cos_ref), (sin_hbm, sin_ref), (rotary_hbm, rotary_spread),
            (plain_hbm, plain_spread),
        ))
    ]
    for copy in loads:
        copy.start()
    for group in range(2):
        lane = group * 4 * HEAD
        attend_shard[:, lane : lane + 2 * HEAD] = query_shard[:, group * 2 * HEAD : (group + 1) * 2 * HEAD]
        attend_shard[:, lane + 2 * HEAD : lane + 3 * HEAD] = key_shard[:, group * HEAD : (group + 1) * HEAD]
        attend_shard[:, lane + 3 * HEAD : lane + 4 * HEAD] = value_shard[:, group * HEAD : (group + 1) * HEAD]
    gains[0:1, : first_gain.shape[1]] = first_gain[...].astype(f32)
    gains[1:2, : first_gain.shape[1]] = second_gain[...].astype(f32)
    stores = []

    def store(source, target):
        copy = pltpu.make_async_copy(source, target, store_sem.at[len(stores)])
        copy.start()
        stores.append(copy)

    greet([places.peer(step) for step in range(1, size)] + [places.chip(), places.core()])

    def own_side(slot):
        return weights.at[slot, :, pl.ds(0, width)]

    def other_side(slot):
        return weights.at[slot, :, pl.ds(width, width)]

    def lanes_of(number, count):
        return pl.ds(number * count, count)

    ring = Parts([
        RingGather(places, weights.at[:, :, lanes_of(number, width // 2)], ring_send.at[number], ring_receive.at[number])
        for number in range(2)
    ])
    ring.start(1, [attend_shard.at[:, lanes_of(number, width // 2)] for number in range(2)])
    passed = []

    def hand_on(step, number, source=None):
        slot = places.index(step)
        copy = remote(
            own_side(slot) if source is None else source, other_side(slot),
            pass_send.at[number], pass_receive.at[number], places.chip(),
        )
        copy.start()
        passed.append(copy)

    hand_on(0, 0, attend_shard)
    output_pass = remote(
        output_shard, output_both.at[own, :, pl.ds(columns, columns)], across.at[0], across.at[1], places.chip()
    )
    output_pass.start()
    gain_copies = []
    for step in range(1, size):
        copy = remote(gains, gain_slots.at[own], gain_send.at[step - 1], gain_receive.at[step - 1], places.peer(step))
        copy.start()
        gain_copies.append(copy)
    near = cot_slots.at[places.side]
    keep = [
        pltpu.make_async_copy(attend_shard, own_side(own), local_sem.at[0]),
        pltpu.make_async_copy(output_shard, output_both.at[own, :, pl.ds(0, columns)], local_sem.at[1]),
        pltpu.make_async_copy(gate_shard, feed.at[own, :, lanes_of(0, units)], local_sem.at[2]),
        pltpu.make_async_copy(up_shard, feed.at[own, :, lanes_of(1, units)], local_sem.at[5]),
        pltpu.make_async_copy(down_shard, down.at[own], local_sem.at[6]),
        pltpu.make_async_copy(cotangent, near, local_sem.at[3]),
    ]
    for copy in keep:
        copy.start()
    gain_slots[own] = gains[...]

    def ring_step(hop):
        ring.step(hop)
        if hop < half:
            hand_on(-hop, 2 * hop - 1)
            hand_on(hop, 2 * hop)
        else:
            hand_on(half, size - 1)

    for copy in gain_copies:
        copy.wait_recv()
    part = tokens.shape[1] // size
    for index in range(size):
        gain_rows[:, index * part : (index + 1) * part] = gain_slots[index][:, :part]
    tile = 64
    mine_start = places.side * half_rows

    def norm_tile(number, carry):
        rows = pl.ds(pl.multiple_of(number * tile, tile), tile)
        values = tokens[rows, :].astype(f32)
        inverse = lax.rsqrt(jnp.mean(values * values, axis=1, keepdims=True) + norm_eps)
        target = pl.ds(pl.multiple_of(mine_start + number * tile, tile), tile)
        normed[target, :] = (values * inverse * gain_rows[0:1, :]).astype(bf16)
        return carry

    tiles = half_rows // tile
    for copy in loads:
        copy.wait()
    ring_step(1)
    lax.fori_loop(0, tiles // 2, norm_tile, 0)
    ring_step(2)
    lax.fori_loop(tiles // 2, tiles, norm_tile, 0)
    mine = pl.ds(pl.multiple_of(mine_start, half_rows), half_rows)
    swap = remote(normed.at[mine], normed.at[mine], across.at[2], across.at[3], places.core())
    swap.start()
    for hop in range(3, half):
        ring_step(hop)
    outputs = Parts([
        RingGather(places, output_both.at[:, :, lanes_of(number, columns)], out_send.at[number], out_receive.at[number])
        for number in range(2)
    ])
    output_pass.wait()
    for copy in keep:
        copy.wait()
    ring_feed = Parts([
        RingGather(places, feed.at[:, :, lanes_of(number, units)], feed_send.at[number], feed_receive.at[number])
        for number in range(2)
    ])
    outputs.start(1)
    ring_feed.start(1, [gate_shard, up_shard])
    ring_step(half)
    swap.wait()
    store(normed, normed_hbm)

    def attend(group):
        lanes = pl.ds(group * 4 * HEAD, 4 * HEAD)
        weight = weights[:, :, lanes].reshape(tokens.shape[1], 4 * HEAD)
        weight = dot(weight, rotary_spread[...]).astype(bf16)
        rows = dot(normed[...], weight)
        cos, sin = cos_ref[...], sin_ref[...]
        base = group * 4 * LANES

        def rot(u):
            return (u * cos + pltpu.roll(u, 64, 1) * sin).astype(bf16)

        for head in range(3):
            lane = head * LANES
            qkv_ref[:, base + lane : base + lane + LANES] = rot(rows[:, lane : lane + LANES])
        qkv_ref[:, base + 3 * LANES : base + 4 * LANES] = rows[:, 3 * LANES :].astype(bf16)
        turned = qkv_ref[:, base + 3 * LANES : base + 4 * LANES].T
        key_place = lax.broadcasted_iota(jnp.int32, (QB, QB), 0)
        query_place = lax.broadcasted_iota(jnp.int32, (QB, QB), 1)
        for head in range(2):
            for block in range(LENGTH // QB):
                first, last = block * QB, (block + 1) * QB
                query = qkv_ref[first:last, base + head * LANES : base + (head + 1) * LANES]
                key = qkv_ref[:last, base + 2 * LANES : base + 3 * LANES]
                score = dot(key, query, ((1,), (1,)))
                edge = jnp.where(key_place <= query_place, score[first:], -1e30)
                score = jnp.concatenate([score[:first], edge], axis=0) if block else edge
                top = jnp.max(score, axis=0, keepdims=True)
                weight = jnp.exp2((score - top) * C2)
                total = jnp.sum(weight, axis=0, keepdims=True)
                result = dot(turned[:, :last], weight.astype(bf16)) / total
                lane = group * 2 * LANES + head * LANES
                att_ref[first:last, lane : lane + LANES] = result.T.astype(bf16)
                log_ref[group, head, pl.ds(first, QB)] = (top * C2 + jnp.log2(total))[0]

    attend(0)
    outputs.step(1)
    attend(1)
    outputs.step(2)
    ring_feed.step(1)
    for copy in passed:
        copy.wait()
    store(weights, weights_hbm)
    cot = Spread(places, cotangent, cot_slots, cot_send, cot_receive)
    cot.start()
    attend(2)
    for hop in range(3, half):
        outputs.step(hop)
    attend(3)
    store(qkv_ref, qkv_hbm)
    store(att_ref, att_hbm)
    outputs.step(half)

    heads_width = columns // HEAD * LANES
    out_rows = output_shard.shape[0]

    def spread_slot(number, carry):
        rows = pl.ds(pl.multiple_of(number * out_rows, out_rows), out_rows)
        for side in range(2):
            value = dot(output_both[number, :, side * columns : (side + 1) * columns], plain_spread[...])
            output_spread[rows, side * heads_width : (side + 1) * heads_width] = value.astype(bf16)
        return carry

    lax.fori_loop(0, size, spread_slot, 0)
    store(output_spread, output_hbm)
    ring_feed.step(2)
    ring_down = Parts([
        RingGather(
            places, down.at[:, :, lanes_of(number, units // 2)], down_send.at[number], down_receive.at[number]
        )
        for number in range(2)
    ])
    ring_down.start(1, [down_shard.at[:, lanes_of(number, units // 2)] for number in range(2)])
    big = 256

    def theirs_tile(number, carry):
        start = (1 - places.side) * half_rows + number * big
        rows = pl.ds(pl.multiple_of(start, big), big)
        value = dot(att_ref[rows, :], output_spread[...], ((1,), (1,)))
        terms[pl.ds(pl.multiple_of(number * big, big), big), :] = value.astype(bf16)
        return carry

    lax.fori_loop(0, half_rows // big, theirs_tile, 0)
    sum_swap = remote(terms, received, across.at[4], across.at[5], places.core())
    sum_swap.start()

    def mine_tile(number, carry):
        rows = pl.ds(pl.multiple_of(mine_start + number * big, big), big)
        value = dot(att_ref[rows, :], output_spread[...], ((1,), (1,)))
        here = pl.ds(pl.multiple_of(number * big, big), big)
        hidden[here, :] = value + tokens[here, :].astype(f32)
        return carry

    lax.fori_loop(0, half_rows // big, mine_tile, 0)
    sum_swap.wait()

    def second_tile(number, carry):
        rows = pl.ds(pl.multiple_of(number * tile, tile), tile)
        values = hidden[rows, :] + received[rows, :].astype(f32)
        hidden[rows, :] = values
        inverse = lax.rsqrt(jnp.mean(values * values, axis=1, keepdims=True) + norm_eps)
        two_own[rows, :] = (values * inverse * gain_rows[1:2, :]).astype(bf16)
        return carry

    lax.fori_loop(0, half_rows // tile, second_tile, 0)
    two = Spread(places, two_own, two_slots, two_send, two_receive)
    two.start()
    store(two_own, two_slots.at[places.side])
    store(hidden, hidden_hbm)
    cot.pass_on()
    for hop in range(3, half):
        ring_feed.step(hop)
    ring_down.step(1)
    ring_feed.step(half)
    store(feed, feed_hbm)

    mine_rows = pl.ds(pl.multiple_of(mine_start, half_rows), half_rows)
    other_rows = pl.ds(pl.multiple_of(half_rows - mine_start, half_rows), half_rows)
    two.core.wait_recv()
    load_other = pltpu.make_async_copy(two_slots.at[1 - places.side], two_other, local_sem.at[4])
    load_other.start()
    hop = 2
    for source, place in ((two_own, mine_rows), (two_other, other_rows)):
        if source is two_other:
            load_other.wait()
        for number in range(units // 512):
            hidden_units(source, feed, inner, factors, place, units, number)
            if hop < half:
                ring_down.step(hop)
                hop += 1
    store(inner, inner_hbm)
    store(factors, factors_hbm)
    two.pass_on()
    for late in range(hop, half + 1):
        ring_down.step(late)
    store(down, down_hbm)
    cot.finish()
    two.chip.wait_send()
    two.core.wait_send()
    two.last.wait()
    for copy in gain_copies:
        copy.wait_send()
    ring.finish()
    outputs.finish()
    ring_feed.finish()
    ring_down.finish()
    for copy in stores:
        copy.wait()


def begin(
    size, tokens, cotangent, first_gain, second_gain, query_shard, key_shard, value_shard, output_shard, gate_shard,
    up_shard, down_shard,
):
    half_rows, features = tokens.shape
    rows = query_shard.shape[0]
    width = query_shard.shape[1] + key_shard.shape[1] + value_shard.shape[1]
    gain_block = (8, LANES * pl.cdiv(rows, LANES))
    columns = output_shard.shape[1]
    units = gate_shard.shape[1]
    heads_width = columns // HEAD * LANES
    groups = 2 * width // (4 * HEAD)
    vmem = pl.BlockSpec(memory_space=pltpu.VMEM)
    anywhere = pl.BlockSpec(memory_space=pl.ANY)
    dma = pltpu.SemaphoreType.DMA
    half = size // 2
    bf16, f32 = jnp.bfloat16, jnp.float32
    cos, sin = rope_tables()
    shape = jax.ShapeDtypeStruct
    buffer = pltpu.VMEM
    kept = [
        ((2 * half_rows, features), bf16),
        ((size, rows, 2 * width), bf16),
        ((features, 2 * heads_width), bf16),
        ((LENGTH, groups * 4 * LANES), bf16),
        ((LENGTH, groups * 2 * LANES), bf16),
        ((half_rows, features), f32),
    ]
    fed = [
        ((size, rows, 2 * units), bf16),
        ((2 * half_rows, units), bf16),
        ((2 * half_rows, 2 * units), bf16),
    ]
    slots = shape((4, half_rows, features), bf16)
    rotary = jnp.asarray(spread(4, (1, 1, 1, 0)), bf16)
    plain = jnp.asarray(spread(columns // HEAD, (0,) * 4), bf16)
    return pl.pallas_call(
        functools.partial(begin_kernel, size),
        in_specs=[anywhere] + [vmem] * 8 + [anywhere] * 4 + [vmem] * 2,
        out_specs=[anywhere] * 12 + [vmem] * 3,
        out_shape=[shape(*one) for one in kept]
        + [slots, slots, shape(*fed[0]), shape((size, rows, units), bf16), shape(*fed[1]), shape(*fed[2])]
        + [shape((groups, 2, LENGTH), f32), shape((8, features), f32), shape((rows, width), bf16)],
        scratch_shapes=[
            buffer((half_rows, features), bf16),
            buffer((LENGTH, LANES), f32),
            buffer((LENGTH, LANES), f32),
            buffer(rotary.shape, bf16),
            buffer(plain.shape, bf16),
        ]
        + [buffer(*one) for one in kept + fed]
        + [
            buffer((size, rows, units), bf16),
            buffer((half_rows, features), bf16),
            buffer(gain_block, f32),
            buffer((size,) + gain_block, f32),
            buffer((size, rows, 2 * columns), bf16),
            buffer((half_rows, features), bf16),
            buffer((half_rows, features), bf16),
            buffer((half_rows, features), bf16),
            dma((size - 1,)), dma((size - 1,)),
            dma((2, 2, half)), dma((2, 2, half)),
            dma((size,)), dma((size,)),
            dma((2, 2, half)), dma((2, 2, half)),
            dma((2, 2, half)), dma((2, 2, half)),
            dma((2, 2, half)), dma((2, 2, half)),
            dma((6,)),
            dma((3,)), dma((3,)),
            dma((3,)), dma((3,)),
            dma((7,)), dma((5,)), dma((11,)),
        ],
        compiler_params=pltpu.CompilerParams(collective_id=1, has_side_effects=True, vmem_limit_bytes=60 * 2**20),
        cost_estimate=pl.CostEstimate(flops=10**10, bytes_accessed=400 * 2**20, transcendentals=0),
        name="begin",
    )(
        tokens, cotangent, query_shard, key_shard, value_shard, output_shard, gate_shard, up_shard, down_shard,
        jnp.asarray(cos), jnp.asarray(sin), rotary, plain, first_gain.reshape(1, -1), second_gain.reshape(1, -1),
    )


class RingScatter:
    def __init__(self, places, partial, received, send, receive):
        self.places, self.partial, self.received = places, partial, received
        self.send, self.receive = send, receive
        self.rows = received.shape[2]
        self.cut = self.rows // 32 * 16
        self.sent = []

    def start(self, hop):
        places = self.places
        for way in range(2):
            rows = pl.ds(0, self.rows)
            if hop == 1:
                rows = (pl.ds(0, self.cut), pl.ds(self.cut, self.rows - self.cut))[way]
                source = self.partial(places.index(places.half)).at[rows]
            else:
                source = self.received.at[way, hop - 2]
            copy = remote(
                source,
                self.received.at[way, hop - 1, rows],
                self.send.at[way, hop - 1],
                self.receive.at[way, hop - 1],
                places.on_ring(1 - 2 * way),
            )
            copy.start()
            self.sent.append(copy)

    def wait(self, hop):
        self.sent[2 * hop - 2].wait_recv()
        self.sent[2 * hop - 1].wait_recv()

    def add(self, hop):
        distance = self.places.half - hop
        for way in range(2):
            own = self.partial(self.places.index(distance * (1 - 2 * way)))
            here = self.received.at[way, hop - 1]
            first, last = 0, self.rows
            if hop == 1:
                first, last = ((0, self.cut), (self.cut, last))[way]
                start, count = ((self.cut, self.rows - self.cut), (0, self.cut))[way]
                here[start : start + count, :] = own[start : start + count, :]
            size = min(last - first, 48)
            for start in range(first, last, size):
                rows = slice(start, min(start + size, last))
                here[rows, :] = here[rows, :] + own[rows, :]

    def step(self, hop):
        self.wait(hop)
        self.add(hop)
        self.start(hop + 1)

    def total(self, rows):
        half = self.places.half
        own = self.partial(self.places.index(0))
        return (
            own[rows, :].astype(jnp.float32)
            + self.received[0, half - 1, rows, :].astype(jnp.float32)
            + self.received[1, half - 1, rows, :].astype(jnp.float32)
        )

    def finish(self):
        for copy in self.sent:
            copy.wait_send()


def middle_kernel(
    size, two_slots, cot_slots, feed, down_hbm, inner_hbm, factors_hbm, hidden_hbm, gain_rows,
    late_grad, gate_sum, down_sum, hidden_grad, branch, far_out, near_out, out_got,
    two, cot, weights, down, inner, grads, down_grad, gate_grad, ring_got, outgoing, far_part, core_far, core_near,
    chip_got, stage, gate_stage, hidden, out_part, load_sem, stage_sem, down_send, down_receive, gate_send,
    gate_receive, send_sem, receive_sem, store_sem, credit,
):
    bf16, f32 = jnp.bfloat16, jnp.float32
    places = Places(size)
    half = places.half
    half_rows, features = hidden_hbm.shape
    rows = feed.shape[1]
    units = inner.shape[1]
    lane_half = units // 2
    greet([places.on_ring(1), places.on_ring(-1), places.chip(), places.core()])

    def lanes_of(number):
        return pl.ds(number * lane_half, lane_half)

    order = (2, 3, 0, 1)
    both_rows = 2 * half_rows
    near = pl.ds(0, both_rows)

    def rows_of(slot):
        return pl.ds(slot * half_rows, half_rows)

    fetch = {}
    for number, (column, side) in enumerate(((0, 0), (0, 1), (1, 0), (1, 1))):
        lanes = pl.ds(side * units + column * lane_half, lane_half)
        fetch["weights", column, side] = pltpu.make_async_copy(
            feed.at[:, :, lanes], weights.at[:, :, lanes], load_sem.at[13 + number]
        )
    for number, slot in enumerate(order):
        fetch["two", slot] = pltpu.make_async_copy(two_slots.at[slot], two.at[rows_of(slot)], load_sem.at[1 + number])
        fetch["cot", slot] = pltpu.make_async_copy(cot_slots.at[slot], cot.at[rows_of(slot)], load_sem.at[5 + number])
    fetch["inner"] = pltpu.make_async_copy(inner_hbm, inner.at[near], load_sem.at[9])
    fetch["factors"] = pltpu.make_async_copy(factors_hbm, grads.at[near], load_sem.at[10])
    fetch["down"] = pltpu.make_async_copy(down_hbm, down, load_sem.at[11])
    for name in (
        ("two", 2), ("weights", 0, 0), ("weights", 0, 1), ("weights", 1, 0), ("weights", 1, 1), ("two", 3), ("cot", 2), ("cot", 3), "inner", ("cot", 0), ("cot", 1), "down", "factors",
        ("two", 0), ("two", 1),
    ):
        fetch[name].start()
    block = 512

    def backward(slot):
        here = rows_of(slot)
        for number in range(units // block):
            lane = number * block
            weight = down[:, :, lane : lane + block].reshape(features, block)
            inner_grad = dot(cot[here, :], weight)
            for place in (slice(lane, lane + block), slice(units + lane, units + lane + block)):
                grads[here, place] = (inner_grad * grads[here, place].astype(f32)).astype(bf16)

    big = 256
    mine_start = places.side * half_rows
    theirs_start = (1 - places.side) * half_rows

    def two_terms(place):
        return dot(grads[place, :], weights[...].reshape(features, 2 * units), ((1,), (1,)))

    def out_terms(place):
        return dot(inner[place, :], down[...].reshape(features, units), ((1,), (1,)))

    def terms_to(target, start, terms):
        def tile(number, carry):
            value = terms(pl.ds(pl.multiple_of(start + number * big, big), big))
            target[pl.ds(pl.multiple_of(number * big, big), big), :] = value.astype(bf16)
            return carry

        lax.fori_loop(0, half_rows // big, tile, 0)

    def add_to(target, other):
        def tile(number, carry):
            place = pl.ds(pl.multiple_of(number * 32, 32), 32)
            target[place, :] = (target[place, :].astype(f32) + other[place, :].astype(f32)).astype(bf16)
            return carry

        lax.fori_loop(0, half_rows // 32, tile, 0)

    for slot in order[:2]:
        fetch["two", slot].wait()
        for number in range(units // block):
            if slot == order[0] and number < 2:
                for side in range(2):
                    fetch["weights", number, side].wait()
            hidden_units(two.at[rows_of(slot)], weights, inner, grads, rows_of(slot), units, number)
    fetch["inner"].wait()
    for slot in order:
        fetch["cot", slot].wait()

    span = 384
    per_span = span // rows

    def down_tile(number, carry):
        lanes = pl.ds(pl.multiple_of(number * span, span), span)
        value = dot(cot[:, lanes], inner[...], ((0,), (0,))).astype(bf16)
        down_grad[pl.ds(number * per_span, per_span)] = value.reshape(per_span, rows, units)
        return carry

    spans = features // span
    lax.fori_loop(0, spans, down_tile, 0)

    def scatter_of(array, send, receive, parts=2):
        lane_part = array.shape[2] // parts
        return Parts([
            RingScatter(
                places,
                lambda slot, number=number: array.at[slot, :, pl.ds(number * lane_part, lane_part)],
                ring_got.at[:, :, :, pl.ds(number * lane_part, lane_part)],
                send.at[number],
                receive.at[number],
            )
            for number in range(parts)
        ])

    ring = scatter_of(down_grad, down_send, down_receive)
    ring.start(1)
    fetch["down"].wait()
    for slot in order[:2]:
        backward(slot)
    terms_to(outgoing, both_rows + theirs_start, two_terms)
    far_swap = remote(outgoing, core_far, send_sem.at[0], receive_sem.at[0], places.core())
    far_swap.start()
    ring.step(1)
    terms_to(far_part, both_rows + mine_start, two_terms)
    far_swap.wait()
    add_to(far_part, core_far)
    chip_swap = remote(far_part, chip_got, send_sem.at[1], receive_sem.at[1], places.chip())
    chip_swap.start()
    fetch["factors"].wait()
    for slot in order[2:]:
        backward(slot)
    ring.step(2)
    for slot in order[2:]:
        fetch["two", slot].wait()

    def late_copy(number):
        place = pl.ds(pl.multiple_of(number * span, span), span)
        return pltpu.make_async_copy(gate_stage, late_grad.at[place, pl.ds(0, lane_half)], stage_sem.at[2])

    def gate_tile(number, carry):
        lanes = pl.ds(pl.multiple_of(number * span, span), span)
        value = dot(two[:, lanes], grads[:, :units], ((0,), (0,))).astype(bf16)
        gate_grad[pl.ds(number * per_span, per_span)] = value[:, :lane_half].reshape(per_span, rows, lane_half)

        @pl.when(number > 0)
        def _():
            late_copy(number - 1).wait()

        gate_stage[...] = value[:, lane_half:]
        late_copy(number).start()
        return carry

    lax.fori_loop(0, spans, gate_tile, 0)
    for hop in range(3, half):
        ring.step(hop)
    terms_to(outgoing, theirs_start, two_terms)
    near_swap = remote(outgoing, core_near, send_sem.at[2], receive_sem.at[2], places.core())
    near_swap.start()
    ring.wait(half)

    def total_to(target, sums, lane_part):
        def tile(number, carry):
            place = pl.ds(pl.multiple_of(number * 16, 16), 16)
            for part, one in enumerate(sums.rings):
                target[place, part * lane_part : (part + 1) * lane_part] = one.total(place)
            return carry

        lax.fori_loop(0, rows // 16, tile, 0)

    total_to(down_sum, ring, lane_half)
    ring.finish()
    for step in (1, -1):
        pl.semaphore_signal(credit, inc=1, device_id=places.on_ring(step), device_id_type=MESH)
    pl.semaphore_wait(credit, 2)
    ring = scatter_of(gate_grad, gate_send, gate_receive)
    ring.start(1)

    def stage_copy(number, side):
        place = pl.ds(pl.multiple_of(number * span, span), span)
        return pltpu.make_async_copy(stage.at[side], late_grad.at[place, pl.ds(lane_half, units)], stage_sem.at[side])

    def up_tile(pair, carry):
        for side in range(2):
            number = 2 * pair + side
            lanes = pl.ds(pl.multiple_of(number * span, span), span)
            value = dot(two[:, lanes], grads[:, units:], ((0,), (0,))).astype(bf16)

            @pl.when(pair > 0)
            def _(side=side, number=number):
                stage_copy(number - 2, side).wait()

            stage[side] = value
            stage_copy(number, side).start()
        return carry

    lax.fori_loop(0, spans // 2, up_tile, 0)
    ring.step(1)

    near_swap.wait()
    terms_to(outgoing, both_rows + theirs_start, out_terms)
    far_swap = remote(outgoing, core_far, send_sem.at[5], receive_sem.at[5], places.core())
    far_swap.start()
    chip_swap.wait()
    terms_to(far_part, both_rows + mine_start, out_terms)
    far_swap.wait()
    add_to(far_part, core_far)
    store_far = pltpu.make_async_copy(far_part, far_out, store_sem.at[0])
    store_far.start()
    out_rows = half_rows // 2
    out_swap = remote(
        far_part.at[pl.ds(0, out_rows)], out_part, send_sem.at[7], receive_sem.at[7], places.chip()
    )
    out_swap.start()
    ring.step(2)

    sends = []
    for number in range(half_rows // big):
        here = pl.ds(number * big, big)
        if number > 0:
            store_grad.wait()
        load_hidden = pltpu.make_async_copy(hidden_hbm.at[here], hidden, load_sem.at[12])
        load_hidden.start()
        place = pl.ds(pl.multiple_of(mine_start + number * big, big), big)
        value = two_terms(place) + core_near[here, :].astype(f32) + chip_got[here, :].astype(f32)
        load_hidden.wait()
        values = hidden[...]
        inverse = lax.rsqrt(jnp.mean(values * values, axis=1, keepdims=True) + norm_eps)
        scaled = value * gain_rows[1:2, :]
        mean = jnp.mean(scaled * values, axis=1, keepdims=True)
        total = cot[place, :].astype(f32) + inverse * scaled - values * (inverse * inverse * inverse) * mean
        hidden[...] = total
        chip_got[here, :] = total.astype(bf16)
        store_grad = pltpu.make_async_copy(hidden, hidden_grad.at[here], store_sem.at[1])
        store_grad.start()
        keep = pltpu.make_async_copy(chip_got.at[here], two.at[place], store_sem.at[2 + number])
        send = remote(chip_got.at[here], two.at[place], send_sem.at[3 + number], receive_sem.at[3 + number], places.core())
        keep.start()
        send.start()
        sends += [keep, send]
    store_grad.wait()

    terms_to(outgoing, theirs_start, out_terms)
    for copy in sends:
        copy.wait()
    store_branch = pltpu.make_async_copy(two.at[near], branch, store_sem.at[5])
    store_branch.start()
    near_swap = remote(outgoing, core_near, send_sem.at[6], receive_sem.at[6], places.core())
    near_swap.start()
    for number in range(half_rows // big):
        here = pl.ds(number * big, big)
        if number > 0:
            store_near.wait()
        load_hidden = pltpu.make_async_copy(hidden_hbm.at[here], hidden, load_sem.at[12])
        load_hidden.start()
        value = out_terms(pl.ds(pl.multiple_of(mine_start + number * big, big), big))
        load_hidden.wait()
        if number == 0:
            near_swap.wait()
        hidden[...] = value + hidden[...] + core_near[here, :].astype(f32)
        store_near = pltpu.make_async_copy(hidden, near_out.at[here], store_sem.at[4])
        store_near.start()
    for hop in range(3, half):
        ring.step(hop)
    ring.wait(half)
    total_to(gate_sum, ring, lane_half // 2)
    ring.finish()
    late_copy(spans - 1).wait()
    store_near.wait()
    store_far.wait()
    for side in range(2):
        stage_copy(spans - 2 + side, side).wait()
    store_branch.wait()
    out_swap.wait()
    store_out = pltpu.make_async_copy(out_part, out_got, store_sem.at[6])
    store_out.start()
    store_out.wait()


def middle(size, two_slots, cot_slots, feed, down, inner, factors, hidden_state, gain_rows):
    half_rows, features = hidden_state.shape
    rows, width = feed.shape[1:]
    units = width // 2
    vmem = pl.BlockSpec(memory_space=pltpu.VMEM)
    anywhere = pl.BlockSpec(memory_space=pl.ANY)
    dma = pltpu.SemaphoreType.DMA
    half = size // 2
    bf16, f32 = jnp.bfloat16, jnp.float32
    shape = jax.ShapeDtypeStruct
    buffer = pltpu.VMEM
    return pl.pallas_call(
        functools.partial(middle_kernel, size),
        in_specs=[anywhere] * 7 + [vmem],
        out_specs=[anywhere, vmem, vmem] + [anywhere] * 5,
        out_shape=[
            shape((features, units // 2 + units), bf16),
            shape((rows, units // 2), f32),
            shape((rows, units), f32),
            shape((half_rows, features), f32),
            shape((2 * half_rows, features), bf16),
            shape((half_rows, features), bf16),
            shape((half_rows, features), f32),
            shape((half_rows // 2, features), bf16),
        ],
        scratch_shapes=[
            buffer((4 * half_rows, features), bf16),
            buffer((4 * half_rows, features), bf16),
            buffer(feed.shape, bf16),
            buffer((size, rows, units), bf16),
            buffer((4 * half_rows, units), bf16),
            buffer((4 * half_rows, 2 * units), bf16),
            buffer((size, rows, units), bf16),
            buffer((size, rows, units // 2), bf16),
            buffer((2, half, rows, units), bf16),
            buffer((half_rows, features), bf16),
            buffer((half_rows, features), bf16),
            buffer((half_rows, features), bf16),
            buffer((half_rows, features), bf16),
            buffer((half_rows, features), bf16),
            buffer((2, 384, units), bf16),
            buffer((384, units // 2), bf16),
            buffer((256, features), f32),
            buffer((half_rows // 2, features), bf16),
            dma((17,)),
            dma((3,)),
            dma((2, 2, half)), dma((2, 2, half)),
            dma((2, 2, half)), dma((2, 2, half)),
            dma((8,)), dma((8,)),
            dma((7,)),
            pltpu.SemaphoreType.REGULAR,
        ],
        compiler_params=pltpu.CompilerParams(collective_id=3, has_side_effects=True, vmem_limit_bytes=63 * 2**20),
        cost_estimate=pl.CostEstimate(flops=6 * 10**10, bytes_accessed=300 * 2**20, transcendentals=0),
        name="middle",
    )(two_slots, cot_slots, feed, down, inner, factors, hidden_state, gain_rows)


def finish_kernel(
    size, tokens_hbm, hidden_hbm, branch_hbm, normed_hbm, weights_hbm, output_hbm, qkv_hbm, att_hbm, up_hbm, up_shard,
    gate_hbm, gate_shard, far_out, near_hbm, first_out, log_ref, gain_rows, attend_shard, cos_ref, sin_ref,
    rotary_spread, plain_spread,
    tokens_grad, query_sum, key_sum, value_sum, output_sum, up_sum, gate_out, gain_sum, layer_out, second_out,
    branch, grad_ref, back, dq_ref, dk_ref, dv_ref, own_grad, other_grad, crossed, ring_got, output_grad, output_got,
    output_crossed, up_grad, up_got, terms, got_terms, output_own, output_across, gain_parts, gate_sum, gate_part, up_part,
    normed, weights, output_spread, qkv_two, att_ref, tokens, hidden_grad, load_sem,
    ring_send, ring_receive, out_send, out_receive, up_send, up_receive, cross_send, cross_receive, across,
    gain_send, gain_receive,
):
    bf16, f32 = jnp.bfloat16, jnp.float32
    places = Places(size)
    half, own = places.half, places.own
    half_rows, features = tokens_hbm.shape
    rows = attend_shard.shape[0]
    units = up_hbm.shape[1] * 2 // 3
    lane_half = units // 2
    span = 4 * HEAD
    big = 256
    diagonal = (own, 3 - places.tensor)
    group_order = (2, 3, 0, 1)
    greet([places.on_ring(1), places.on_ring(-1), places.chip(), places.core(), diagonal])

    out_rows = half_rows // 2
    out_swap = remote(
        far_out.at[pl.ds(out_rows, out_rows)], second_out, across.at[0], across.at[1], places.chip()
    )

    out_swap.start()

    def qkv_load(number):
        lanes = pl.ds(group_order[number] * 4 * LANES, 4 * LANES)
        return pltpu.make_async_copy(qkv_hbm.at[:, lanes], qkv_two.at[number % 2], load_sem.at[number])

    def row_loads(first, second, number):
        here = pl.ds(number * big, big)
        return (
            pltpu.make_async_copy(first.at[here], tokens, load_sem.at[4]),
            pltpu.make_async_copy(second.at[here], hidden_grad, load_sem.at[5]),
        )

    fetch = {
        "up": pltpu.make_async_copy(up_hbm, up_grad, load_sem.at[11]),
        "branch": pltpu.make_async_copy(branch_hbm, branch, load_sem.at[6]),
        "output": pltpu.make_async_copy(output_hbm, output_spread, load_sem.at[7]),
        "att": pltpu.make_async_copy(att_hbm, att_ref, load_sem.at[8]),
        "normed": pltpu.make_async_copy(normed_hbm, normed, load_sem.at[9]),
        "weights": pltpu.make_async_copy(weights_hbm, weights, load_sem.at[10]),
        "gate_sum": pltpu.make_async_copy(gate_hbm, gate_sum, load_sem.at[12]),
        "gate_part": pltpu.make_async_copy(gate_shard, gate_part, load_sem.at[13]),
        "up_part": pltpu.make_async_copy(up_shard, up_part, load_sem.at[14]),
    }
    fetch["up"].start()
    fetch["branch"].start()
    fetch["output"].start()
    qkv_loads = [qkv_load(number) for number in range(4)]
    qkv_loads[0].start()
    for name in ("att", "normed", "weights", "gate_sum", "gate_part", "up_part"):
        fetch[name].start()
    token_rows = row_loads(tokens_hbm, hidden_hbm, 0)
    for copy in token_rows:
        copy.start()

    def lanes_of(number, count):
        return pl.ds(number * count, count)

    ups = Parts([
        RingScatter(
            places,
            lambda slot, number=number: up_grad.at[
                pl.ds(pl.multiple_of(slot * rows, rows), rows), lanes_of(number, lane_half)
            ],
            up_got.at[:, :, :, lanes_of(number, lane_half)],
            up_send.at[number],
            up_receive.at[number],
        )
        for number in range(3)
    ])
    fetch["up"].wait()
    ups.start(1)
    fetch["branch"].wait()
    fetch["output"].wait()
    fetch["att"].wait()

    def back_group(number, target, lane, between):
        group = group_order[number]
        qkv_loads[number].wait()
        if number < 3:
            qkv_loads[number + 1].start()
        qkv_ref = qkv_two.at[number % 2]
        base = 0
        for part in range(2):
            block = pl.ds(part * half_rows, half_rows)
            value = dot(branch[block, :], output_spread[:, group * 2 * LANES : (group + 1) * 2 * LANES])
            grad_ref[block, :] = value.astype(bf16)
        turned = qkv_ref[:, base + 2 * LANES : base + 3 * LANES].T
        cos, sin = cos_ref[...], sin_ref[...]
        scale = HEAD**-0.5

        def unrot(u):
            return (u * cos - pltpu.roll(u, 64, 1) * sin).astype(bf16)

        key_place = lax.broadcasted_iota(jnp.int32, (QB, QB), 0)
        query_place = lax.broadcasted_iota(jnp.int32, (QB, QB), 1)
        for head in range(2):
            lanes = slice(head * LANES, (head + 1) * LANES)
            att_lane = (2 * group + head) * LANES
            prod = grad_ref[:, lanes].astype(f32) * att_ref[:, att_lane : att_lane + LANES].astype(f32)
            delta = jnp.sum(prod.T, axis=0, keepdims=True)
            for block in reversed(range(LENGTH // QB)):
                first, last = block * QB, (block + 1) * QB
                query = qkv_ref[first:last, base + head * LANES : base + (head + 1) * LANES]
                out_grad = grad_ref[first:last, lanes]
                score = dot(qkv_ref[:last, base + 2 * LANES : base + 3 * LANES], query, ((1,), (1,)))
                prob = jnp.exp2(score * C2 - log_ref[group, head : head + 1, first:last])
                edge = jnp.where(key_place <= query_place, prob[first:], 0.0)
                prob = jnp.concatenate([prob[:first], edge], axis=0) if block else edge
                prob_grad = dot(qkv_ref[:last, base + 3 * LANES : base + 4 * LANES], out_grad, ((1,), (1,)))
                score_grad = (prob * (prob_grad - delta[:, first:last])).astype(bf16)
                key_part = dot(score_grad, query)
                value_part = dot(prob.astype(bf16), out_grad)
                if head == 0 and block == LENGTH // QB - 1:
                    dk_ref[...] = key_part
                    dv_ref[...] = value_part
                else:
                    dk_ref[:last] += key_part
                    dv_ref[:last] += value_part
                dq_ref[first:last, lanes] = dot(turned[:, :last], score_grad).T
            if head == 0:
                between()
        wide = jnp.concatenate(
            [
                unrot(dq_ref[:, :LANES] * scale),
                unrot(dq_ref[:, LANES:] * scale),
                unrot(dk_ref[...] * scale),
                dv_ref[...].astype(bf16),
            ],
            axis=1,
        )
        close_back = dot(wide, rotary_spread[...], ((1,), (1,))).astype(bf16)
        back[:, group * span : (group + 1) * span] = close_back
        if number == 0:
            fetch["normed"].wait()
        for part in range(2):
            block = slice(part * features // 2, (part + 1) * features // 2)
            value = dot(normed[:, block], close_back, ((0,), (0,))).astype(bf16)
            target[part * size // 2 : (part + 1) * size // 2, :, lane : lane + span] = value.reshape(
                size // 2, rows, span
            )

    order = [half]
    for step in range(half - 1, 0, -1):
        order += [step, -step]
    order.append(0)
    crossing = {}

    def cross(group):
        for number, step in enumerate(order):
            slot = places.index(step)
            lanes = pl.ds(group * span, span)
            copy = remote(
                other_grad.at[slot, :, lanes], crossed.at[slot, :, lanes],
                cross_send.at[group, number], cross_receive.at[group, number], places.chip(),
            )
            copy.start()
            crossing[(group, step)] = copy

    heads_width = output_spread.shape[1] // 2
    columns = heads_width // LANES * HEAD
    kept = LANES
    sent_on = columns - kept
    for side in (1, 0):
        close = dot(
            att_ref[:, side * heads_width : (side + 1) * heads_width], plain_spread[...], ((1,), (1,))
        ).astype(bf16)
        for part in range(2):
            block = slice(part * features // 2, (part + 1) * features // 2)
            value = dot(branch[:, block], close, ((0,), (0,))).astype(bf16)
            output_grad[part * size // 2 : (part + 1) * size // 2, :, side * columns : (side + 1) * columns] = (
                value.reshape(size // 2, rows, columns)
            )
    out_crossing = {}
    for number, step in enumerate(order):
        slot = places.index(step)
        copy = remote(
            output_grad.at[slot, :, pl.ds(columns + kept, sent_on)], output_crossed.at[slot],
            cross_send.at[2, number], cross_receive.at[2, number], places.chip(),
        )
        copy.start()
        out_crossing[step] = copy

    def prepare_output(step):
        out_crossing[step].wait_recv()
        slot = places.index(step)
        for start in range(0, rows, 48):
            place = slice(start, start + 48)
            output_grad[slot, place, kept:columns] = output_grad[slot, place, kept:columns] + output_crossed[slot, place, :]

    ring_width = (columns + kept) // 2
    outputs = Parts([
        RingScatter(
            places,
            lambda slot, number=number: output_grad.at[slot, :, lanes_of(number, ring_width)],
            output_got.at[:, :, :, lanes_of(number, ring_width)],
            out_send.at[number],
            out_receive.at[number],
        )
        for number in range(2)
    ])

    def output_step(hop):
        prepare_output(half - hop)
        prepare_output(hop - half)
        outputs.step(hop)

    micro = [(ring, hop) for hop in range(1, half) for ring in ups.rings]

    def serve(count):
        for _ in range(min(count, len(micro))):
            ring, hop = micro.pop(0)
            ring.step(hop)

    serve(1)
    back_group(0, other_grad, 0, lambda: serve(2))
    cross(0)
    serve(1)
    back_group(1, other_grad, span, lambda: serve(2))
    cross(1)
    serve(1)

    def late_start():
        serve(1)
        prepare_output(half)
        outputs.start(1)

    back_group(2, own_grad, 0, late_start)
    serve(len(micro))
    back_group(3, own_grad, span, lambda: output_step(1))
    if half > 2:
        output_step(2)

    def prepare(group, step):
        crossing[(group, step)].wait_recv()
        slot = places.index(step)
        lanes = slice(group * span, (group + 1) * span)
        for start in range(0, rows, 48):
            place = slice(start, start + 48)
            crossed[slot, place, lanes] = crossed[slot, place, lanes] + own_grad[slot, place, lanes]

    attend = [
        RingScatter(
            places,
            lambda slot, number=number: crossed.at[slot, :, lanes_of(number, span)],
            ring_got.at[:, :, :, lanes_of(number, span)],
            ring_send.at[number],
            ring_receive.at[number],
        )
        for number in range(2)
    ]

    def attend_start(group):
        prepare(group, half)
        attend[group].start(1)

    def attend_step(group, hop):
        prepare(group, half - hop)
        prepare(group, hop - half)
        attend[group].step(hop)

    attend_start(0)
    whole = weights.shape[2]
    fetch["weights"].wait()

    def terms_of(block):
        return dot(back[block, :], weights[...].reshape(features, whole), ((1,), (1,)))

    def theirs_tile(number, carry):
        place = (1 - places.side) * half_rows + number * big
        value = terms_of(pl.ds(pl.multiple_of(place, big), big))
        terms[pl.ds(pl.multiple_of(number * big, big), big), :] = value.astype(bf16)
        return carry

    lax.fori_loop(0, half_rows // big, theirs_tile, 0)
    terms_swap = remote(terms, got_terms, across.at[2], across.at[3], places.core())
    terms_swap.start()
    attend_step(0, 1)
    for hop in range(3, half):
        output_step(hop)
    terms_swap.wait()
    for number in range(half_rows // big):
        for copy in token_rows:
            copy.wait()
        here = slice(number * big, (number + 1) * big)
        place = places.side * half_rows + number * big
        value = terms_of(pl.ds(pl.multiple_of(place, big), big)) + got_terms[here, :].astype(f32)
        values = tokens[...].astype(f32)
        inverse = lax.rsqrt(jnp.mean(values * values, axis=1, keepdims=True) + norm_eps)
        scaled = value * gain_rows[0:1, :]
        inner = jnp.mean(scaled * values, axis=1, keepdims=True)
        result = hidden_grad[...] + inverse * scaled - values * (inverse * inverse * inverse) * inner
        tokens_grad[here, :] = result.astype(bf16)
        if number < half_rows // big - 1:
            token_rows = row_loads(tokens_hbm, hidden_hbm, number + 1)
            for copy in token_rows:
                copy.start()
        if number == 0 and half > 2:
            attend_step(0, 2)
    attend_start(1)
    for hop in range(3, half):
        attend_step(0, hop)
    prepare(0, 0)

    prepare_output(0)
    outputs.wait(half)

    for start in range(0, rows, 48):
        place = slice(start, start + 48)
        late = outputs.rings[1].total(place)
        output_own[place, :ring_width] = outputs.rings[0].total(place)
        output_own[place, ring_width:] = late[:, : columns - ring_width]
        output_across[0, place, :] = late[:, columns - ring_width :].astype(bf16)
    output_swap = remote(output_across.at[0], output_across.at[1], across.at[4], across.at[5], places.chip())
    output_swap.start()
    attend_step(1, 1)
    ups.wait(half)
    for name in ("gate_sum", "gate_part", "up_part"):
        fetch[name].wait()

    def up_tile(number, carry):
        place = pl.ds(pl.multiple_of(number * 16, 16), 16)
        early = gate_sum[place, :]
        gate_out[place, :lane_half] = early
        gain = jnp.sum(early * gate_part[place, :lane_half].astype(f32), axis=1, keepdims=True)
        late = (
            (gate_out, gate_part, lane_half, 0), (up_sum, up_part, 0, 1), (up_sum, up_part, lane_half, 2),
        )
        for target, weight, lane, part in late:
            lanes = slice(lane, lane + lane_half)
            value = ups.rings[part].total(place)
            target[place, lanes] = value
            gain += jnp.sum(value * weight[place, lanes].astype(f32), axis=1, keepdims=True)
        lane = lax.broadcasted_iota(jnp.int32, (16, LANES), 1)
        gain_parts[0, place, :] = jnp.where(lane == 1, gain, 0.0)
        return carry

    lax.fori_loop(0, rows // 16, up_tile, 0)

    out_swap.wait()
    for number in range(half_rows // big):
        here = slice(number * big, (number + 1) * big)
        source = first_out if number < half_rows // big // 2 else second_out
        share = pltpu.make_async_copy(source.at[pl.ds(number * big % out_rows, big)], tokens, load_sem.at[4])
        near = pltpu.make_async_copy(near_hbm.at[pl.ds(number * big, big)], hidden_grad, load_sem.at[5])
        share.start()
        near.start()
        share.wait()
        near.wait()
        layer_out[here, :] = (hidden_grad[...] + tokens[...].astype(f32)).astype(bf16)
    if half > 2:
        attend_step(1, 2)

    def attend_total(part):
        attend[part].wait(half)
        for start in range(0, rows, 48):
            place = slice(start, start + 48)
            value = attend[part].total(place)
            query_sum[place, part * 2 * HEAD : (part + 1) * 2 * HEAD] = value[:, : 2 * HEAD]
            key_sum[place, part * HEAD : (part + 1) * HEAD] = value[:, 2 * HEAD : 3 * HEAD]
            value_sum[place, part * HEAD : (part + 1) * HEAD] = value[:, 3 * HEAD :]
            weight = attend_shard[place, part * span : (part + 1) * span].astype(f32)
            gain = jnp.sum(value * weight, axis=1, keepdims=True)
            lane = lax.broadcasted_iota(jnp.int32, (48, LANES), 1)
            gain_parts[0, place, :] += jnp.where(lane == 0, gain, 0.0)

    attend_total(0)
    for hop in range(3, half):
        attend_step(1, hop)
    prepare(1, 0)
    output_swap.wait()
    output_sum[:, :kept] = output_own[:, :kept] + output_across[1].astype(f32)
    output_sum[:, kept:] = output_own[:, kept:]
    attend_total(1)
    gain_copies = []
    for number, device in enumerate((places.core(), places.chip(), diagonal)):
        copy = remote(
            gain_parts.at[0], gain_parts.at[1 + number], gain_send.at[number], gain_receive.at[number], device
        )
        copy.start()
        gain_copies.append(copy)
    for copy in list(crossing.values()) + list(out_crossing.values()):
        copy.wait_send()
    ups.finish()
    outputs.finish()
    for ring in attend:
        ring.finish()
    for copy in gain_copies:
        copy.wait()
    gain_sum[...] = (gain_parts[0] + gain_parts[1]) + (gain_parts[2] + gain_parts[3])


def finish(
    size, tokens, hidden_grad, branch, normed, weights, output_spread, qkv, att, logs, gain_rows, up_grad, up_shard,
    gate_sum, gate_shard, attend_shard, far_out, near_out, first_out,
):
    half_rows, features = tokens.shape
    rows, width = attend_shard.shape
    columns = output_spread.shape[1] // 2 // LANES * HEAD
    units = up_shard.shape[1]
    vmem = pl.BlockSpec(memory_space=pltpu.VMEM)
    anywhere = pl.BlockSpec(memory_space=pl.ANY)
    dma = pltpu.SemaphoreType.DMA
    half = size // 2
    bf16, f32 = jnp.bfloat16, jnp.float32
    cos, sin = rope_tables()
    shape = jax.ShapeDtypeStruct
    buffer = pltpu.VMEM
    return pl.pallas_call(
        functools.partial(finish_kernel, size),
        in_specs=[anywhere] * 15 + [vmem] * 7,
        out_specs=[vmem] * 9 + [anywhere],
        out_shape=[
            shape((half_rows, features), bf16),
            shape((rows, width // 2), f32),
            shape((rows, width // 4), f32),
            shape((rows, width // 4), f32),
            shape((rows, columns), f32),
            shape((rows, units), f32),
            shape((rows, units), f32),
            shape((rows, LANES), f32),
            shape((half_rows, features), bf16),
            shape((half_rows // 2, features), bf16),
        ],
        scratch_shapes=[
            buffer((LENGTH, features), bf16),
            buffer((LENGTH, 2 * LANES), bf16),
            buffer((LENGTH, 2 * width), bf16),
            buffer((LENGTH, 2 * LANES), f32),
            buffer((LENGTH, LANES), f32),
            buffer((LENGTH, LANES), f32),
            buffer((size, rows, width), bf16),
            buffer((size, rows, width), bf16),
            buffer((size, rows, width), bf16),
            buffer((2, half, rows, width), bf16),
            buffer((size, rows, 2 * columns), bf16),
            buffer((2, half, rows, columns + LANES), bf16),
            buffer((size, rows, columns - LANES), bf16),
            buffer(up_grad.shape, bf16),
            buffer((2, half, rows, up_grad.shape[1]), bf16),
            buffer((half_rows, features), bf16),
            buffer((half_rows, features), bf16),
            buffer((rows, columns), f32),
            buffer((2, rows, LANES), bf16),
            buffer((4, rows, LANES), f32),
            buffer(gate_sum.shape, f32),
            buffer((rows, units), bf16),
            buffer((rows, units), bf16),
            buffer((LENGTH, features), bf16),
            buffer(weights.shape, bf16),
            buffer(output_spread.shape, bf16),
            buffer((2, LENGTH, 4 * LANES), bf16),
            buffer(att.shape, bf16),
            buffer((256, features), bf16),
            buffer((256, features), f32),
            dma((16,)),
            dma((2, 2, half)), dma((2, 2, half)),
            dma((2, 2, half)), dma((2, 2, half)),
            dma((3, 2, half)), dma((3, 2, half)),
            dma((3, size)), dma((3, size)),
            dma((6,)),
            dma((3,)), dma((3,)),
        ],
        compiler_params=pltpu.CompilerParams(collective_id=2, has_side_effects=True, vmem_limit_bytes=63 * 2**20),
        cost_estimate=pl.CostEstimate(flops=3 * 10**10, bytes_accessed=300 * 2**20, transcendentals=0),
        name="finish",
    )(
        tokens, hidden_grad, branch, normed, weights, output_spread, qkv, att, up_grad, up_shard, gate_sum, gate_shard,
        far_out, near_out, first_out, logs, gain_rows, attend_shard, jnp.asarray(cos), jnp.asarray(sin),
        jnp.asarray(spread(4, (1, 1, 1, 0)), bf16), jnp.asarray(spread(4, (0,) * 4), bf16),
    )


def local(
    dp_size,
    tokens,
    first_gain,
    query_weight,
    key_weight,
    value_weight,
    output_weight,
    second_gain,
    gate_weight,
    up_weight,
    down_weight,
    cotangent,
):
    f32 = jnp.float32
    (
        normed, weights, output_spread, qkv, attended, hidden_state, two_slots, cot_slots, feed, down, inner, factors,
        logs, gain_rows, attend_shard,
    ) = begin(
        dp_size, tokens, cotangent, first_gain, second_gain, query_weight, key_weight, value_weight, output_weight.T,
        gate_weight, up_weight, down_weight.T,
    )
    late_grad, gate_sum, down_sum, hidden_grad, branch, far_out, near_out, first_out = middle(
        dp_size, two_slots, cot_slots, feed, down, inner, factors, hidden_state, gain_rows
    )
    tokens_grad, query_sum, key_sum, value_sum, output_sum, up_sum, gate_sum, gain_sums, layer_out, _ = finish(
        dp_size, tokens, hidden_grad, branch, normed, weights, output_spread, qkv, attended, logs, gain_rows,
        late_grad, up_weight, gate_sum, gate_weight, attend_shard, far_out, near_out, first_out,
    )
    return (
        layer_out,
        tokens_grad,
        gain_sums[:, 0] / first_gain.astype(f32),
        query_sum,
        key_sum,
        value_sum,
        output_sum.T,
        gain_sums[:, 1] / second_gain.astype(f32),
        gate_sum,
        up_sum,
        down_sum.T,
    )


def solution(mesh):
    in_specs = (
        P(("dp", "tensor"), None),
        P("dp"),
        P("dp", "tensor"),
        P("dp", "tensor"),
        P("dp", "tensor"),
        P("tensor", "dp"),
        P("dp"),
        P("dp", "tensor"),
        P("dp", "tensor"),
        P("tensor", "dp"),
        P(("dp", "tensor"), None),
    )
    out_specs = (
        P(("dp", "tensor"), None),
        P(("dp", "tensor"), None),
        P("dp"),
        P("dp", "tensor"),
        P("dp", "tensor"),
        P("dp", "tensor"),
        P("tensor", "dp"),
        P("dp"),
        P("dp", "tensor"),
        P("dp", "tensor"),
        P("tensor", "dp"),
    )
    body = functools.partial(local, mesh.shape["dp"])
    return jax.shard_map(body, mesh=mesh, in_specs=in_specs, out_specs=out_specs, check_vma=False)
```
